32 devices in a mesh: clip: 16 (over z, x, core), seq: 2 (over y).
Axes of the slice: x: 2, y: 2, z: 4, core: 2. Of those that a mesh axis runs over, the one named last changes fastest.
Arguments:
- inputs: bfloat16 [32, 3136, 768], P('clip', 'seq'), may hold values from -6 to 6
- frame_tokens: int32 [32], P('clip'), may hold values from 98 to 196, as said below
- clip_frames: int32 [32], P('clip'), may hold values from 8 to 16, as said below
- norm1_gain: float32 [768], replicated, may hold values from 0.1 to 1.9
- norm1_bias: float32 [768], replicated, may hold values from -3 to 3
- qkv_weight: bfloat16 [768, 2304], replicated, may hold values from -0.3125 to 0.3125
- query_bias: float32 [768], replicated, may hold values from -3 to 3
- value_bias: float32 [768], replicated, may hold values from -3 to 3
- out_weight: bfloat16 [768, 768], replicated, may hold values from -0.875 to 0.875
- out_bias: float32 [768], replicated, may hold values from -3 to 3
- norm2_gain: float32 [768], replicated, may hold values from 0.1 to 1.9
- norm2_bias: float32 [768], replicated, may hold values from -3 to 3
- fc1_weight: bfloat16 [768, 3072], replicated, may hold values from -0.21875 to 0.21875
- fc1_bias: float32 [3072], replicated, may hold values from -3 to 3
- fc2_weight: bfloat16 [3072, 768], replicated, may hold values from -0.15625 to 0.15625
- fc2_bias: float32 [768], replicated, may hold values from -3 to 3
- learn_gain: float32 [768], replicated, may hold values from 0.1 to 1.9
- learn_bias: float32 [768], replicated, may hold values from -3 to 3
- map1_weight: bfloat16 [768, 64], replicated, may hold values from -0.21875 to 0.21875
- map1_bias: float32 [64], replicated, may hold values from -3 to 3
- map2_weight: bfloat16 [64, 8], replicated, may hold values from -1.5 to 1.5
- map2_bias: float32 [8], replicated, may hold values from -4 to 4
- cot_pooled: bfloat16 [32, 16, 8, 768], P('clip', 'seq'), may hold values from -6 to 6
Outputs:
- pooled: bfloat16 [32, 16, 8, 768], P('clip', 'seq')
- penalty: float32 [], replicated
- input_grad: float32 [32, 3136, 768], P('clip', 'seq')
- norm1_gain_grad: float32 [768], replicated
- norm1_bias_grad: float32 [768], replicated
- qkv_weight_grad: float32 [768, 2304], P('clip', 'seq')
- query_bias_grad: float32 [768], replicated
- value_bias_grad: float32 [768], replicated
- out_weight_grad: float32 [768, 768], P('clip', 'seq')
- out_bias_grad: float32 [768], replicated
- norm2_gain_grad: float32 [768], replicated
- norm2_bias_grad: float32 [768], replicated
- fc1_weight_grad: float32 [768, 3072], P('clip', 'seq')
- fc1_bias_grad: float32 [3072], replicated
- fc2_weight_grad: float32 [3072, 768], P('clip', 'seq')
- fc2_bias_grad: float32 [768], replicated
- learn_gain_grad: float32 [768], replicated
- learn_bias_grad: float32 [768], replicated
- map1_weight_grad: float32 [768, 64], replicated
- map1_bias_grad: float32 [64], replicated
- map2_weight_grad: float32 [64, 8], replicated
- map2_bias_grad: float32 [8], replicated
The draws below stay inside these ranges and needn't reach their ends.
Inputs may be any that keep to these rules, and one draw needn't show every extreme that they name: `frame_tokens`: every 2 clips that one index of clip holds contain one whose frames hold 196 tokens. `clip_frames`: every 2 clips that one index of clip holds contain one of 16 frames.
All inputs are finite; a program needn't handle non-finite values.
Results may differ from the reference program's by a relative error of at most 0.028.
Values may be sent and summed in bfloat16 or wider, within the bound.
No kernel may reach another device: no remote copies, remote signals or barrier semaphores. Data moves between devices by JAX's collectives and lax.ppermute only.
A program may use at most 384 MiB of HBM per device.

```python
import jax
import jax.numpy as jnp
from jax import lax

D = 768
HEADS = 12
HEAD = 64
FF = 3072
MAPH = 64
NTOK = 8
PATCH = 196
CLIP_DEV = 2
FRAMES = 16
CLIPS = 32


def group_full(key, lowest, highest_value):
    first, second = jax.random.split(key)
    counts = jax.random.randint(first, (CLIPS,), lowest, highest_value + 1)
    groups = CLIPS // CLIP_DEV
    picked = jax.random.randint(second, (groups,), 0, CLIP_DEV)
    within = jnp.arange(CLIPS, dtype=jnp.int32).reshape(groups, CLIP_DEV) % CLIP_DEV
    chosen = (within == picked[:, None]).reshape(CLIPS)
    return jnp.where(chosen, highest_value, counts).astype(jnp.int32)


def draw_frame_tokens(key, part):
    key = jax.random.fold_in(key, 11)
    return group_full(key, PATCH // 2, PATCH)


def draw_clip_frames(key, part):
    key = jax.random.fold_in(key, 23)
    return group_full(key, FRAMES // 2, FRAMES)


def block_scale(own_key, shape, cuts, low, top_value):
    def one(dim, parts):
        heights = jax.random.uniform(jax.random.fold_in(jax.random.fold_in(own_key, 6), dim), (parts,), jnp.float32, low / len(cuts), top_value / len(cuts))
        return jnp.repeat(jnp.exp(heights), shape[dim] // parts).reshape((-1,) + (1,) * (len(shape) - dim - 1))

    level = one(*cuts[0])
    for cut in cuts[1:]:
        level = level * one(*cut)
    return level


def noise(stream_key, extent, width, reach, cuts=(), kind=jnp.bfloat16):
    level = block_scale(stream_key, extent, cuts, -0.22, 0.18) if cuts else 1.0
    drawn = jax.random.normal(stream_key, extent, jnp.float32) * width * level
    return jnp.minimum(jnp.maximum(drawn, -reach), reach).astype(kind)


def setup_inputs(seed: int = 0) -> dict:
    splits = jax.random.split(jax.random.key(seed), 24)
    inputs = noise(splits[0], (CLIPS, FRAMES * PATCH, D), 1.0, 6.0, ((0, 16), (1, 2)))
    frame_tokens = draw_frame_tokens(jax.random.fold_in(splits[23], 71), 0)
    clip_frames = draw_clip_frames(jax.random.fold_in(splits[23], 71), 0)
    norm1_gain = jnp.clip(1.0 + 0.18 * jax.random.normal(splits[3], (D,), jnp.float32), 0.1, 1.9)
    norm1_bias = noise(splits[4], (D,), 0.5, 3.0, (), jnp.float32)
    qkv_weight = noise(splits[5], (D, 3 * D), (D // 2) ** -0.5, 0.3125)
    query_bias = noise(splits[6], (D,), 0.5, 3.0, (), jnp.float32)
    value_bias = noise(splits[7], (D,), 0.5, 3.0, (), jnp.float32)
    out_weight = noise(splits[8], (D, D), (D // 16) ** -0.5, 0.875)
    out_bias = noise(splits[9], (D,), 0.5, 3.0, (), jnp.float32)
    norm2_gain = jnp.clip(1.0 + 0.18 * jax.random.normal(splits[10], (D,), jnp.float32), 0.1, 1.9)
    norm2_bias = noise(splits[11], (D,), 0.5, 3.0, (), jnp.float32)
    fc1_weight = noise(splits[12], (D, FF), D ** -0.5, 0.21875)
    fc1_bias = noise(splits[13], (FF,), 0.5, 3.0, (), jnp.float32)
    fc2_weight = noise(splits[14], (FF, D), (FF // 2) ** -0.5, 0.15625)
    fc2_bias = noise(splits[15], (D,), 0.5, 3.0, (), jnp.float32)
    learn_gain = jnp.clip(1.0 + 0.18 * jax.random.normal(splits[16], (D,), jnp.float32), 0.1, 1.9)
    learn_bias = noise(splits[17], (D,), 0.5, 3.0, (), jnp.float32)
    map1_weight = noise(splits[18], (D, MAPH), D ** -0.5, 0.21875)
    map1_bias = noise(splits[19], (MAPH,), 0.5, 3.0, (), jnp.float32)
    map2_weight = noise(splits[20], (MAPH, NTOK), (MAPH // 4) ** -0.5, 1.5)
    map2_bias = noise(splits[21], (NTOK,), 1.0, 4.0, (), jnp.float32)
    cot_pooled = noise(splits[22], (CLIPS, FRAMES, NTOK, D), 1.0, 6.0, ((0, 16), (1, 2)))
    return {"inputs": inputs, "frame_tokens": frame_tokens, "clip_frames": clip_frames, "norm1_gain": norm1_gain, "norm1_bias": norm1_bias, "qkv_weight": qkv_weight, "query_bias": query_bias, "value_bias": value_bias, "out_weight": out_weight, "out_bias": out_bias, "norm2_gain": norm2_gain, "norm2_bias": norm2_bias, "fc1_weight": fc1_weight, "fc1_bias": fc1_bias, "fc2_weight": fc2_weight, "fc2_bias": fc2_bias, "learn_gain": learn_gain, "learn_bias": learn_bias, "map1_weight": map1_weight, "map1_bias": map1_bias, "map2_weight": map2_weight, "map2_bias": map2_bias, "cot_pooled": cot_pooled}


@jax.custom_vjp
def low(v):
    return lax.optimization_barrier(v.astype(jnp.bfloat16)).astype(jnp.float32)

@jax.custom_vjp
def low_back(v):
    return v

def low_keep(v):
    return (low(v), None)

def low_pass(kept, grad):
    return (grad,)

def back_keep(v):
    return (v, None)

def back_low(kept, grad):
    return (low(grad),)
low.defvjp(low_keep, low_pass)
low_back.defvjp(back_keep, back_low)
epsilon = 1e-06
masked_score = -1e+30
highest = lax.Precision.HIGHEST

def rounded_both(value):
    return low(low_back(value))

def normed(value, gain, bias):
    average = lax.optimization_barrier(jnp.mean(value, axis=-1, keepdims=True))
    centered = value - average
    variance = lax.optimization_barrier(jnp.mean(centered * centered, axis=-1, keepdims=True))
    return centered * lax.rsqrt(variance + epsilon) * gain + bias

def matmul(left, right):
    return jnp.dot(left, right, precision=highest)

def gelu_exact(value):
    return jax.nn.gelu(value, approximate=False)

def clip_forward(params, clip_rows, token_count, frame_count):
    norm1_gain, norm1_bias, qkv_weight, query_bias, value_bias, out_weight, out_bias, norm2_gain, norm2_bias, fc1_weight, fc1_bias, fc2_weight, fc2_bias, learn_gain, learn_bias, map1_weight, map1_bias, map2_weight, map2_bias = params
    row_ids = jnp.arange(FRAMES * PATCH, dtype=jnp.int32)
    frame_ids = row_ids // PATCH
    slot_ids = row_ids - frame_ids * PATCH
    allowed = (frame_ids < frame_count) & (slot_ids < token_count)
    valid = allowed.astype(jnp.float32)
    act1 = low(normed(clip_rows, norm1_gain, norm1_bias))
    mixed = matmul(act1, qkv_weight)
    scaling = HEAD ** (-0.5)
    queries = low(low_back(mixed[:, :D] + query_bias) * scaling)
    key_rows = rounded_both(mixed[:, D:2 * D])
    value_rows = rounded_both(mixed[:, 2 * D:] + value_bias)

    def split_heads(value):
        return value.reshape(-1, HEADS, HEAD).transpose(1, 0, 2)

    def one_head(operands):
        query_head, key_head, value_head = operands
        scores = low_back(matmul(query_head, key_head.T))
        scores = jnp.where(allowed[None, :], scores, masked_score)
        largest = lax.optimization_barrier(jnp.max(scores, axis=-1, keepdims=True))
        weights = jnp.exp(scores - largest)
        probs = low(weights / lax.optimization_barrier(jnp.sum(weights, axis=-1, keepdims=True)))
        return matmul(probs, value_head)
    per_head = lax.map(jax.checkpoint(one_head), (split_heads(queries), split_heads(key_rows), split_heads(value_rows)))
    attended = rounded_both(per_head.transpose(1, 0, 2).reshape(-1, D))
    resid1 = clip_rows + low_back(matmul(attended, out_weight) + out_bias)
    act2 = low(normed(resid1, norm2_gain, norm2_bias))
    hidden = low(gelu_exact(low_back(matmul(act2, fc1_weight) + fc1_bias)))
    resid2 = resid1 + low_back(matmul(hidden, fc2_weight) + fc2_bias)
    act3 = low(normed(resid2, learn_gain, learn_bias))
    map_hidden = low(gelu_exact(low_back(matmul(act3, map1_weight) + map1_bias)))
    gates = jax.nn.sigmoid(low_back(matmul(map_hidden, map2_weight) + map2_bias)) * valid[:, None]
    inverse = lax.rsqrt(token_count.astype(jnp.float32))
    pooled = inverse * jnp.einsum('fpk,fpd->fkd', low(gates).reshape(FRAMES, PATCH, NTOK), low(resid2).reshape(FRAMES, PATCH, D), precision=highest)
    gate_sum = lax.optimization_barrier(jnp.sum(gates, axis=-1))
    gate_square = lax.optimization_barrier(jnp.sum(gates * gates, axis=-1))
    intersection = jnp.sum(gate_sum * gate_sum - gate_square) / (NTOK * (NTOK - 1)) / token_count.astype(jnp.float32)
    return (pooled, intersection)

def reference(inputs, frame_tokens, clip_frames, norm1_gain, norm1_bias, qkv_weight, query_bias, value_bias, out_weight, out_bias, norm2_gain, norm2_bias, fc1_weight, fc1_bias, fc2_weight, fc2_bias, learn_gain, learn_bias, map1_weight, map1_bias, map2_weight, map2_bias, cot_pooled):
    params = tuple((item.astype(jnp.float32) for item in (norm1_gain, norm1_bias, qkv_weight, query_bias, value_bias, out_weight, out_bias, norm2_gain, norm2_bias, fc1_weight, fc1_bias, fc2_weight, fc2_bias, learn_gain, learn_bias, map1_weight, map1_bias, map2_weight, map2_bias)))
    slots_all = jnp.asarray(CLIPS * FRAMES, jnp.float32)
    state = inputs.astype(jnp.float32)

    def forward(clip_states, weights):

        def per_clip(operands):
            clip_rows, token_count, frame_count = operands
            return jax.checkpoint(clip_forward)(weights, clip_rows, token_count, frame_count)
        pooled, intersection = lax.map(per_clip, (clip_states, frame_tokens, clip_frames))
        return (pooled, jnp.sum(intersection) / slots_all)
    (pooled, penalty), pullback = jax.vjp(forward, state, params)
    input_grad, grads = pullback((cot_pooled.astype(jnp.float32), jnp.ones((), jnp.float32)))
    return (pooled.astype(jnp.bfloat16), penalty, input_grad, grads[0], grads[1], grads[2], grads[3], grads[4], grads[5], grads[6], grads[7], grads[8], grads[9], grads[10], grads[11], grads[12], grads[13], grads[14], grads[15], grads[16], grads[17], grads[18])
```

```python
import jax
import jax.numpy as jnp
from jax import lax
from jax.experimental import pallas as pl
from jax.experimental.pallas import tpu as pltpu
from jax.sharding import PartitionSpec as P

HEADS = 12
HEAD = 64
NTOK = 8
PATCH = 196
TILE = 256
LOG2E = 1.4426950408889634
LN2 = 0.6931471805599453
VMEM = 60 * 1024 * 1024

epsilon = 1e-06
masked_score = -1e30
bf16 = jnp.bfloat16
f32 = jnp.float32

NN = (((1,), (0,)), ((), ()))
NT = (((1,), (1,)), ((), ()))
TN = (((0,), (0,)), ((), ()))


def dot(left, right, dims=NN):
    return lax.dot_general(left, right, dims, preferred_element_type=f32)


def split3(value):
    hi = value.astype(bf16).astype(f32)
    mid = (value - hi).astype(bf16).astype(f32)
    return hi, mid, value - hi - mid


def attend_kernel(q, k, v, kaug, att, aq, qp, vt, acc):
    rows = q.shape[0]
    keys = k.shape[0]
    chunks = keys // TILE
    qt = q[...].T
    zero = jnp.zeros((HEAD, rows), bf16)
    ids = lax.broadcasted_iota(jnp.int32, (128, rows), 0)
    for j in range(2):
        part = qt[j * HEAD : (j + 1) * HEAD]
        qp[j, 0:HEAD] = part if j == 0 else zero
        qp[j, HEAD:128] = zero if j == 0 else part
        qp[j, 128:256] = jnp.where(ids == 3, 1.0, 0.0).astype(bf16)
    vt[...] = v[...].T
    ones = jnp.ones((16, TILE), bf16)

    def left(base):
        return jnp.concatenate([k[pl.ds(base, TILE), :], kaug[pl.ds(base, TILE), :]], axis=1)

    def values(j, base):
        return jnp.concatenate([vt[j * HEAD : (j + 1) * HEAD, pl.ds(base, TILE)], ones], axis=0)

    def fold(t, first):
        base = t * TILE if first else pl.multiple_of(t * TILE, TILE)
        for j in range(2):
            p = jnp.exp2(dot(left(base), qp[j])).astype(bf16)
            part = dot(values(j, base), p)
            if first:
                acc[j] = part
            else:
                acc[j] += part

    fold(0, True)

    @pl.loop(1, chunks)
    def _(t):
        fold(t, False)

    for j in range(2):
        total = acc[j, HEAD : HEAD + 1]
        fine = (total > 2.0**-60) & (total < 2.0**60)
        bad = jnp.max(jnp.where(fine, 0.0, 1.0)) > 0.5
        acc[j, HEAD + 8 : HEAD + 9] = jnp.zeros((1, rows), f32)

        @pl.when(bad)
        def _():
            def largest(t, best):
                s = dot(left(pl.multiple_of(t * TILE, TILE)), qp[j])
                return jnp.maximum(best, jnp.max(s, axis=0, keepdims=True))

            best = lax.fori_loop(0, chunks, largest, jnp.full((1, rows), -1e38, f32))
            acc[j] = jnp.zeros((HEAD + 16, rows), f32)

            @pl.loop(0, chunks)
            def _(t):
                base = pl.multiple_of(t * TILE, TILE)
                p = jnp.exp2(dot(left(base), qp[j]) - best).astype(bf16)
                acc[j] += dot(values(j, base), p)

            acc[j, HEAD + 8 : HEAD + 9] = best

    ids = lax.broadcasted_iota(jnp.int32, (HEAD, rows), 0)
    outs = []
    augs = []
    for j in range(2):
        total = acc[j, HEAD : HEAD + 1]
        outs.append(acc[j, 0:HEAD] * (1.0 / total))
        lse = jnp.log2(total) + acc[j, HEAD + 8 : HEAD + 9]
        hi, mid, low = split3(-lse)
        aug = jnp.where(ids == 0, hi, jnp.where(ids == 1, mid, jnp.where(ids == 2, low, 0.0)))
        augs.append(jnp.where(ids == 3, 1.0, aug))
    att[...] = jnp.concatenate(outs, axis=0).T.astype(bf16)
    aq[...] = jnp.concatenate(augs, axis=0).T.astype(bf16)


def attend(mixed, keys_values, kaug):
    rows = mixed.shape[0]
    keys = keys_values.shape[0]
    pairs = HEADS // 2
    first = keys_values.shape[1] // 128 - 2 * pairs
    return pl.pallas_call(
        attend_kernel,
        grid=(pairs,),
        in_specs=[
            pl.BlockSpec((rows, 128), lambda h: (0, h)),
            pl.BlockSpec((keys, 128), lambda h: (0, first + h)),
            pl.BlockSpec((keys, 128), lambda h: (0, first + pairs + h)),
            pl.BlockSpec((keys, 128), lambda h: (0, 0)),
        ],
        out_specs=[
            pl.BlockSpec((rows, 128), lambda h: (0, h)),
            pl.BlockSpec((rows, 128), lambda h: (0, h)),
        ],
        out_shape=[
            jax.ShapeDtypeStruct((rows, HEADS * HEAD), bf16),
            jax.ShapeDtypeStruct((rows, HEADS * HEAD), bf16),
        ],
        scratch_shapes=[
            pltpu.VMEM((2, 256, rows), bf16),
            pltpu.VMEM((128, keys), bf16),
            pltpu.VMEM((2, HEAD + 16, rows), f32),
        ],
        compiler_params=pltpu.CompilerParams(vmem_limit_bytes=VMEM),
        cost_estimate=pl.CostEstimate(
            flops=4 * HEADS * rows * keys * 256, transcendentals=HEADS * rows * keys, bytes_accessed=rows * 768 * 10
        ),
        name="attend",
    )(mixed, keys_values, keys_values, kaug)


def attend_back_kernel(q, do, att, aq, k, v, kaug_t, dq, dk, dv, kp, vp, dkt, dvt):
    step = pl.program_id(1)
    rows = q.shape[0]
    keys = k.shape[0]
    tiles = keys // TILE
    pad = HEAD - 16

    @pl.when(step == 0)
    def _():
        for source, held in ((k, kp), (v, vp)):
            flat = source[...].T
            zero = jnp.zeros((HEAD, keys), bf16)
            rest = jnp.zeros((pad, keys), bf16)
            for j in range(2):
                part = flat[j * HEAD : (j + 1) * HEAD]
                held[j, 0:HEAD] = part if j == 0 else zero
                held[j, HEAD:128] = zero if j == 0 else part
                aug = jnp.concatenate([kaug_t[...], rest], axis=0)
                held[j, 128 : 128 + HEAD] = aug if j == 0 else zero
                held[j, 128 + HEAD : 256] = zero if j == 0 else aug
        dkt[...] = jnp.zeros_like(dkt)
        dvt[...] = jnp.zeros_like(dvt)

    lane = lax.broadcasted_iota(jnp.int32, (rows, 128), 1)
    product = do[...].astype(f32) * att[...].astype(f32)
    inner0 = jnp.sum(jnp.where(lane < HEAD, product, 0.0), axis=1, keepdims=True)
    inner1 = jnp.sum(jnp.where(lane < HEAD, 0.0, product), axis=1, keepdims=True)
    hi, mid, low = split3(-jnp.where(lane < HEAD, inner0, inner1))
    within = lane % HEAD
    ado = jnp.where(within == 0, hi, jnp.where(within == 1, mid, jnp.where(within == 2, low, 0.0))).astype(bf16)
    qa = jnp.concatenate([q[...], aq[...]], axis=1)
    da = jnp.concatenate([do[...], ado], axis=1)
    qt = q[...].T
    dot_ = do[...].T
    units = [(j, t) for j in range(2) for t in range(tiles)]
    totals = [None, None]

    def scores(j, t):
        cols = slice(t * TILE, (t + 1) * TILE)
        return dot(qa, kp[j, :, cols]), dot(da, vp[j, :, cols])

    def weigh(s, dp):
        p = jnp.exp2(s)
        return p.astype(bf16), (p * dp).astype(bf16)

    def collect(j, t, p, ds):
        cols = slice(t * TILE, (t + 1) * TILE)
        part = slice(j * HEAD, (j + 1) * HEAD)
        dvt[part, cols] += dot(dot_[part], p)
        dkt[part, cols] += dot(qt[part], ds)
        more = dot(ds, k[cols, :])
        totals[j] = more if totals[j] is None else totals[j] + more

    raw = {}
    ready = {}
    count = len(units)
    for i in range(count + 2):
        if i < count:
            raw[i] = scores(*units[i])
        if 0 <= i - 1 < count:
            ready[i - 1] = weigh(*raw.pop(i - 1))
        if 0 <= i - 2 < count:
            collect(*units[i - 2], *ready.pop(i - 2))
    dq[...] = (jnp.where(lane < HEAD, totals[0], totals[1]) * HEAD ** (-0.5)).astype(bf16)

    @pl.when(step == pl.num_programs(1) - 1)
    def _():
        dk[...] = (dkt[...] * LN2).T.astype(bf16)
        dv[...] = dvt[...].T.astype(bf16)


def attend_back(mixed, keys_values, grad_att, att, aq, kaug_t):
    rows = mixed.shape[0]
    keys = keys_values.shape[0]
    pairs = HEADS // 2
    first = keys_values.shape[1] // 128 - 2 * pairs
    here = pl.BlockSpec((TILE, 128), lambda h, r: (r, h))
    whole = pl.BlockSpec((keys, 128), lambda h, r: (0, h))
    return pl.pallas_call(
        attend_back_kernel,
        grid=(pairs, rows // TILE),
        in_specs=[
            here,
            here,
            here,
            here,
            pl.BlockSpec((keys, 128), lambda h, r: (0, first + h)),
            pl.BlockSpec((keys, 128), lambda h, r: (0, first + pairs + h)),
            pl.BlockSpec((16, keys), lambda h, r: (0, 0)),
        ],
        out_specs=[here, whole, whole],
        out_shape=[
            jax.ShapeDtypeStruct((rows, HEADS * HEAD), bf16),
            jax.ShapeDtypeStruct((keys, HEADS * HEAD), bf16),
            jax.ShapeDtypeStruct((keys, HEADS * HEAD), bf16),
        ],
        scratch_shapes=[
            pltpu.VMEM((2, 256, keys), bf16),
            pltpu.VMEM((2, 256, keys), bf16),
            pltpu.VMEM((128, keys), f32),
            pltpu.VMEM((128, keys), f32),
        ],
        compiler_params=pltpu.CompilerParams(vmem_limit_bytes=VMEM),
        cost_estimate=pl.CostEstimate(
            flops=10 * HEADS * rows * keys * 200, transcendentals=HEADS * rows * keys, bytes_accessed=rows * 768 * 20
        ),
        name="attend_back",
    )(mixed, grad_att, att, aq, keys_values, keys_values, kaug_t)


def normed(value, gain, bias):
    average = jnp.mean(value, axis=-1, keepdims=True)
    centered = value - average
    variance = jnp.mean(centered * centered, axis=-1, keepdims=True)
    return centered * lax.rsqrt(variance + epsilon) * gain + bias


def norm_back(value, gain, bias, grad):
    result, pullback = jax.vjp(normed, value, gain, bias)
    return pullback(grad)


def gelu_exact(value):
    return jax.nn.gelu(value, approximate=False)


def gelu_back(value, grad):
    result, pullback = jax.vjp(gelu_exact, value)
    return pullback(grad)[0]


def column_sums(grad):
    return jnp.sum(grad.astype(f32), axis=0)


def shards(
    inputs,
    frame_tokens,
    clip_frames,
    norm1_gain,
    norm1_bias,
    qkv_weight,
    query_bias,
    value_bias,
    out_weight,
    out_bias,
    norm2_gain,
    norm2_bias,
    fc1_weight,
    fc1_bias,
    fc2_weight,
    fc2_bias,
    learn_gain,
    learn_bias,
    map1_weight,
    map1_bias,
    map2_weight,
    map2_bias,
    cot_pooled,
):
    clip_count, piece, width = inputs.shape
    seq_size = lax.axis_size("seq")
    position = lax.axis_index("seq")
    clip_size = lax.axis_size("clip")
    frames_here = piece // PATCH
    scaling = HEAD ** (-0.5)
    slots_all = float(clip_count * clip_size * seq_size * frames_here)
    group = seq_size // clip_count
    mine = position // group
    seat = position % group

    def route(turn):
        return [
            (s, ((s % clip_count + turn) % clip_count) * group + s // clip_count) for s in range(seq_size)
        ]

    def send(value, turn, back=False):
        pairs = route(turn)
        if back:
            pairs = [(b, a) for a, b in pairs]
        if all(a == b for a, b in pairs):
            return value
        return lax.ppermute(value, "seq", pairs)

    def scatter(whole):
        return [
            send(lax.dynamic_index_in_dim(whole, (position + turn) % clip_count, 0, False), turn)
            for turn in range(clip_count)
        ]

    def gather_back(pieces):
        home = [send(part, turn, True) for turn, part in enumerate(pieces)]
        stacked = jnp.stack(home)
        order = (jnp.arange(clip_count) - position) % clip_count
        return stacked[order]

    tokens = lax.dynamic_index_in_dim(frame_tokens, mine, 0, False)
    frames = lax.dynamic_index_in_dim(clip_frames, mine, 0, False)
    rows = clip_count * piece
    padded = -(-rows // TILE) * TILE
    gap = padded - rows

    x_low = jnp.concatenate(scatter(inputs) + [jnp.zeros((gap, width), bf16)], axis=0)
    cot = jnp.concatenate(scatter(cot_pooled), axis=0).reshape(clip_count * frames_here * NTOK, width)

    def placed(ids, at_seat):
        turn = ids // piece
        source = clip_count * at_seat + (mine - turn) % clip_count
        local = ids - turn * piece
        frame = local // PATCH
        slot = local - frame * PATCH
        inside = (source * frames_here + frame < frames) & (slot < tokens) & (ids < rows)
        return inside, jnp.where(ids < rows, turn * frames_here + frame, -1)

    row_ids = jnp.arange(padded, dtype=jnp.int32)
    inside, frame_ids = placed(row_ids, seat)
    valid = inside.astype(f32)[:, None]
    key_ids = jnp.arange(group * padded, dtype=jnp.int32)
    key_inside, _ = placed(key_ids % padded, key_ids // padded)
    lane16 = jnp.arange(HEAD)
    key_mask = jnp.where(key_inside, 0.0, masked_score)
    kaug = jnp.where(lane16[None, :] < 3, 1.0, jnp.where(lane16[None, :] == 3, key_mask[:, None], 0.0)).astype(bf16)
    kaug = jnp.concatenate([kaug, jnp.zeros_like(kaug)], axis=1)
    sub16 = jnp.arange(16)[:, None]
    kaug_t = jnp.where(sub16 < 3, 1.0, jnp.where(sub16 == 3, key_mask[None, :], 0.0)).astype(bf16)

    state = x_low.astype(f32)
    act1 = normed(state, norm1_gain, norm1_bias).astype(bf16)
    zeros = jnp.zeros((width,), f32)
    ones = jnp.ones((width,), f32)
    col_scale = jnp.concatenate([ones * (scaling * LOG2E), ones, ones])
    col_bias = jnp.concatenate([query_bias * (scaling * LOG2E), zeros, value_bias])
    mixed = (dot(act1, qkv_weight) * col_scale + col_bias).astype(bf16)
    if group == 1:
        keys_values = mixed
    else:
        both = lax.all_gather(mixed[:, width:], "seq", axis=0, tiled=True)
        keys_values = lax.dynamic_slice_in_dim(both, mine * (group * padded), group * padded, 0)
    att, aq = attend(mixed, keys_values, kaug)

    resid1 = state + dot(att, out_weight) + out_bias
    act2 = normed(resid1, norm2_gain, norm2_bias).astype(bf16)
    hidden_pre = dot(act2, fc1_weight) + fc1_bias
    hidden = gelu_exact(hidden_pre).astype(bf16)
    resid2 = resid1 + dot(hidden, fc2_weight) + fc2_bias
    act3 = normed(resid2, learn_gain, learn_bias).astype(bf16)
    map_pre = dot(act3, map1_weight) + map1_bias
    map_hidden = gelu_exact(map_pre).astype(bf16)
    logits = dot(map_hidden, map2_weight) + map2_bias
    sigmoid_raw = jax.nn.sigmoid(logits)
    gates = sigmoid_raw * valid
    inverse = lax.rsqrt(tokens.astype(f32))
    slots = clip_count * frames_here * NTOK
    spread = (frame_ids[:, None] == jnp.arange(slots, dtype=jnp.int32)[None, :] // NTOK).astype(f32)
    gates_low = gates.astype(bf16)
    gates_wide = (jnp.tile(gates_low.astype(f32), (1, slots // NTOK)) * spread).astype(bf16)
    output_low = resid2.astype(bf16)
    pooled = (dot(gates_wide, output_low, TN) * inverse).astype(bf16)
    pooled = pooled.reshape(clip_count, frames_here, NTOK, width)
    pooled = gather_back([pooled[t] for t in range(clip_count)])
    gate_sum = jnp.sum(gates, axis=-1, keepdims=True)
    gate_square = jnp.sum(gates * gates, axis=-1)
    pair_count = NTOK * (NTOK - 1)
    intersection = jnp.sum(gate_sum[:, 0] * gate_sum[:, 0] - gate_square) * inverse * inverse / pair_count
    grad_out = dot(gates_wide, cot) * inverse
    grad_wide = dot(output_low, cot, NT) * spread
    grad_gate = jnp.sum(grad_wide.reshape(padded, slots // NTOK, NTOK), axis=1) * inverse
    penalty_factor = 2.0 / pair_count * (inverse * inverse) / slots_all
    grad_gate = (grad_gate + penalty_factor * (gate_sum - gates)) * valid
    grad_logit = (grad_gate * sigmoid_raw * (1.0 - sigmoid_raw)).astype(bf16)
    map2_grad = dot(map_hidden, grad_logit, TN)
    map2_bias_grad = column_sums(grad_logit)
    grad_mpre = gelu_back(map_pre, dot(grad_logit, map2_weight, NT)).astype(bf16)
    map1_grad = dot(act3, grad_mpre, TN)
    map1_bias_grad = column_sums(grad_mpre)
    grad_res2, learn_gain_grad, learn_bias_grad = norm_back(
        resid2, learn_gain, learn_bias, dot(grad_mpre, map1_weight, NT)
    )
    grad_res2 = grad_res2 + grad_out
    branch_two = grad_res2.astype(bf16)

    def reduce_matrix(matrix):
        matrix = lax.psum_scatter(matrix.astype(bf16), "clip", scatter_dimension=0, tiled=True)
        return lax.psum_scatter(matrix, "seq", scatter_dimension=1, tiled=True).astype(f32)

    fc2_grad = reduce_matrix(dot(hidden, branch_two, TN))
    fc2_bias_grad = column_sums(branch_two)
    grad_pre = gelu_back(hidden_pre, dot(branch_two, fc2_weight, NT)).astype(bf16)
    fc1_grad = reduce_matrix(dot(act2, grad_pre, TN))
    fc1_bias_grad = column_sums(grad_pre)
    grad_res1, norm2_gain_grad, norm2_bias_grad = norm_back(
        resid1, norm2_gain, norm2_bias, dot(grad_pre, fc1_weight, NT)
    )
    grad_res1 = grad_res1 + grad_res2
    branch_one = grad_res1.astype(bf16)
    out_grad = reduce_matrix(dot(att, branch_one, TN))
    out_bias_grad = column_sums(branch_one)
    grad_att = dot(branch_one, out_weight, NT).astype(bf16)

    def flat_sum(parts):
        sizes = [part.size for part in parts]
        flat = jnp.concatenate([part.reshape(-1) for part in parts])
        total = lax.psum(flat, ("clip", "seq"))
        outs = []
        at = 0
        for part, size in zip(parts, sizes):
            outs.append(total[at : at + size].reshape(part.shape))
            at += size
        return outs

    early = flat_sum(
        [
            out_bias_grad,
            norm2_gain_grad,
            norm2_bias_grad,
            fc1_bias_grad,
            fc2_bias_grad,
            learn_gain_grad,
            learn_bias_grad,
            map1_grad,
            map1_bias_grad,
            map2_grad,
            map2_bias_grad,
            intersection.reshape(1),
        ]
    )

    grad_q, grad_k, grad_v = attend_back(mixed, keys_values, grad_att, att, aq, kaug_t)
    if group > 1:
        both = jnp.zeros((seq_size * padded, 2 * width), bf16)
        both = lax.dynamic_update_slice_in_dim(
            both, jnp.concatenate([grad_k, grad_v], axis=1), mine * (group * padded), 0
        )
        both = lax.psum_scatter(both, "seq", scatter_dimension=0, tiled=True)
        grad_k, grad_v = both[:, :width], both[:, width:]
    grad_mixed = jnp.concatenate([grad_q, grad_k, grad_v], axis=1)
    qkv_grad = reduce_matrix(dot(act1, grad_mixed, TN))
    query_bias_grad = column_sums(grad_q)
    value_bias_grad = column_sums(grad_v)
    grad_in, norm1_gain_grad, norm1_bias_grad = norm_back(
        state, norm1_gain, norm1_bias, dot(grad_mixed, qkv_weight, NT)
    )
    input_grad = (grad_in + grad_res1)[:rows].reshape(clip_count, piece, width).astype(bf16)
    input_grad = gather_back([input_grad[t] for t in range(clip_count)]).astype(f32)
    late = flat_sum([norm1_gain_grad, norm1_bias_grad, query_bias_grad, value_bias_grad])
    penalty = early[11].reshape(()) / slots_all
    return (
        pooled,
        penalty,
        input_grad,
        late[0],
        late[1],
        qkv_grad,
        late[2],
        late[3],
        out_grad,
        early[0],
        early[1],
        early[2],
        fc1_grad,
        early[3],
        fc2_grad,
        early[4],
        early[5],
        early[6],
        early[7],
        early[8],
        early[9],
        early[10],
    )


def solution(mesh):
    row_spec = P("clip", "seq", None)
    pool_spec = P("clip", "seq", None, None)
    matrix_spec = P("clip", "seq")
    in_specs = (row_spec, P("clip"), P("clip")) + (P(),) * 19 + (pool_spec,)
    out_specs = (
        (pool_spec, P(), row_spec, P(), P(), matrix_spec, P(), P(), matrix_spec, P(), P(), P(), matrix_spec, P())
        + (matrix_spec,)
        + (P(),) * 7
    )
    return jax.shard_map(shards, mesh=mesh, in_specs=in_specs, out_specs=out_specs, check_vma=False)
```

```python
import jax
import jax.numpy as jnp
from jax import lax
from jax.experimental import pallas as pl
from jax.experimental.pallas import tpu as pltpu
from jax.sharding import PartitionSpec as P

HEADS = 12
HEAD = 64
NTOK = 8
PATCH = 196
TILE = 256
MIDDLE = 448
LOG2E = 1.4426950408889634
LN2 = 0.6931471805599453
VMEM = 60 * 1024 * 1024

epsilon = 1e-06
masked_score = -1e30
bf16 = jnp.bfloat16
f32 = jnp.float32

NN = (((1,), (0,)), ((), ()))
NT = (((1,), (1,)), ((), ()))


def dot(left, right, dims=NN):
    return lax.dot_general(left, right, dims, preferred_element_type=f32)


def split3(value):
    hi = value.astype(bf16).astype(f32)
    mid = (value - hi).astype(bf16).astype(f32)
    return hi, mid, value - hi - mid


def up(count, unit):
    return -(-count // unit) * unit


def tile_of(count, most):
    return max(size for size in range(16, most + 1, 16) if count % size == 0)


def blocks_of(count, unit):
    return [(base, min(unit, count - base)) for base in range(0, count, unit)]


def flip(value):
    return jnp.concatenate([value[base : base + size].T for base, size in blocks_of(value.shape[0], 128)], axis=1)


def spread_heads(source, held, aug):
    count = source.shape[0]
    zero = jnp.zeros((HEAD, held.shape[2]), bf16)
    for j in range(2):
        other = (1 - j) * HEAD
        held[j, other : other + HEAD] = zero
        if held.shape[2] > count:
            edge = count // 128 * 128
            held[j, j * HEAD : (j + 1) * HEAD, edge:] = jnp.zeros((HEAD, held.shape[2] - edge), bf16)
        held[j, 128:256] = aug(j)
    for base, size in blocks_of(count, 256):
        flat = flip(source[base : base + size])
        for j in range(2):
            held[j, j * HEAD : (j + 1) * HEAD, base : base + size] = flat[j * HEAD : (j + 1) * HEAD]


def spread_queries(q, qp):
    ids = lax.broadcasted_iota(jnp.int32, (128, qp.shape[2]), 0)
    spread_heads(q, qp, lambda j: jnp.where(ids == 3, 1.0, 0.0).astype(bf16))


def flip_into(source, target):
    for base, size in blocks_of(source.shape[0], 256):
        target[:, base : base + size] = flip(source[base : base + size])


def key_block(k, kaug, base, size):
    return jnp.concatenate([k[pl.ds(base, size), :], kaug[pl.ds(base, size), :]], axis=1)


def value_block(vt, j, base, size):
    ones = jnp.ones((16, size), bf16)
    return jnp.concatenate([vt[j * HEAD : (j + 1) * HEAD, pl.ds(base, size)], ones], axis=0)


def over_tiles(step, begin, count):
    @pl.loop(begin // TILE, count // TILE, unroll=3)
    def _(t):
        step(pl.multiple_of(t * TILE, TILE), TILE)

    if count % TILE:
        step(count // TILE * TILE, count % TILE)


def fold_tile(k, kaug, qp, vt, acc, low, fresh, base, size):
    for j in range(2):
        p = jnp.exp2(dot(key_block(k, kaug, base, size), qp[j, :, low:])).astype(bf16)
        part = dot(value_block(vt, j, base, size), p)
        if fresh:
            acc[j, :, low:] = part
        else:
            acc[j, :, low:] += part


def attend_near_kernel(q, k, v, kaug, acc, qp, vt):
    spread_queries(q, qp)
    flip_into(v, vt)
    fold_tile(k, kaug, qp, vt, acc, 0, True, 0, TILE)
    over_tiles(lambda base, size: fold_tile(k, kaug, qp, vt, acc, 0, False, base, size), TILE, k.shape[0])


def attend_near(near, mixed, kaug):
    pairs = HEADS // 2
    return pl.pallas_call(
        attend_near_kernel,
        grid=(pairs,),
        in_specs=[
            pl.BlockSpec((near, 128), lambda h: (0, h)),
            pl.BlockSpec((near, 128), lambda h: (0, pairs + h)),
            pl.BlockSpec((near, 128), lambda h: (0, 2 * pairs + h)),
            pl.BlockSpec((near, 128), lambda h: (0, 0)),
        ],
        out_specs=pl.BlockSpec((2, HEAD + 16, near), lambda h: (h, 0, 0)),
        out_shape=jax.ShapeDtypeStruct((HEADS, HEAD + 16, near), f32),
        scratch_shapes=[pltpu.VMEM((2, 256, near), bf16), pltpu.VMEM((128, near), bf16)],
        compiler_params=pltpu.CompilerParams(vmem_limit_bytes=VMEM),
        cost_estimate=pl.CostEstimate(
            flops=4 * HEADS * near * near * 256, transcendentals=HEADS * near * near, bytes_accessed=near * 768 * 10
        ),
        name="attend_near",
    )(mixed, mixed, mixed, kaug)


def attend_kernel(q, k, v, kaug, *refs):
    att, aq, qp, vt, acc = refs[-5:]
    rows = q.shape[0]
    keys = k.shape[0]
    wide = qp.shape[2]
    spread_queries(q, qp)
    flip_into(v, vt)

    def fold(low, fresh):
        return lambda base, size: fold_tile(k, kaug, qp, vt, acc, low, fresh, base, size)

    begun = 0
    if len(refs) > 5:
        begun = refs[0].shape[2]
        acc[:, :, :begun] = refs[0][...]
    fold(begun, True)(0, TILE)
    if begun:
        over_tiles(fold(begun, False), TILE, begun)
    over_tiles(fold(0, False), max(begun, TILE), keys)

    for j in range(2):
        total = acc[j, HEAD : HEAD + 1]
        fine = (total > 2.0**-60) & (total < 2.0**60)
        bad = jnp.max(jnp.where(fine, 0.0, 1.0)) > 0.5
        acc[j, HEAD + 8 : HEAD + 9] = jnp.zeros((1, wide), f32)

        @pl.when(bad)
        def _():
            acc[j, 0:1] = jnp.full((1, wide), -1e38, f32)

            def largest(base, size):
                s = dot(key_block(k, kaug, base, size), qp[j])
                acc[j, 0:1] = jnp.maximum(acc[j, 0:1], jnp.max(s, axis=0, keepdims=True))

            over_tiles(largest, 0, keys)
            best = acc[j, 0:1]
            acc[j] = jnp.zeros((HEAD + 16, wide), f32)

            def again(base, size):
                p = jnp.exp2(dot(key_block(k, kaug, base, size), qp[j]) - best).astype(bf16)
                acc[j] += dot(value_block(vt, j, base, size), p)

            over_tiles(again, 0, keys)
            acc[j, HEAD + 8 : HEAD + 9] = best

    ids = lax.broadcasted_iota(jnp.int32, (HEAD, 128), 0)
    for base, size in blocks_of(rows, 128):
        here = slice(base, base + 128)
        outs = []
        augs = []
        for j in range(2):
            total = acc[j, HEAD : HEAD + 1, here]
            outs.append(acc[j, 0:HEAD, here] * (1.0 / total))
            lse = jnp.log2(total) + acc[j, HEAD + 8 : HEAD + 9, here]
            hi, mid, low = split3(-lse)
            aug = jnp.where(ids == 0, hi, jnp.where(ids == 1, mid, jnp.where(ids == 2, low, 0.0)))
            augs.append(jnp.where(ids == 3, 1.0, aug))
        att[base : base + size, :] = jnp.concatenate(outs, axis=0).T[:size].astype(bf16)
        aq[base : base + size, :] = jnp.concatenate(augs, axis=0).T[:size].astype(bf16)


def attend(mixed, keys_values, kaug, *begun):
    rows = mixed.shape[0]
    keys = keys_values.shape[0]
    pairs = HEADS // 2
    wide = up(rows, 128)
    first = keys_values.shape[1] // 128 - 2 * pairs
    return pl.pallas_call(
        attend_kernel,
        grid=(pairs,),
        in_specs=[
            pl.BlockSpec((rows, 128), lambda h: (0, h)),
            pl.BlockSpec((keys, 128), lambda h: (0, first + h)),
            pl.BlockSpec((keys, 128), lambda h: (0, first + pairs + h)),
            pl.BlockSpec((keys, 128), lambda h: (0, 0)),
        ]
        + [pl.BlockSpec((2,) + one.shape[1:], lambda h: (h, 0, 0)) for one in begun],
        out_specs=[
            pl.BlockSpec((rows, 128), lambda h: (0, h)),
            pl.BlockSpec((rows, 128), lambda h: (0, h)),
        ],
        out_shape=[
            jax.ShapeDtypeStruct((rows, HEADS * HEAD), bf16),
            jax.ShapeDtypeStruct((rows, HEADS * HEAD), bf16),
        ],
        scratch_shapes=[
            pltpu.VMEM((2, 256, wide), bf16),
            pltpu.VMEM((128, up(keys, 128)), bf16),
            pltpu.VMEM((2, HEAD + 16, wide), f32),
        ],
        compiler_params=pltpu.CompilerParams(vmem_limit_bytes=VMEM),
        cost_estimate=pl.CostEstimate(
            flops=4 * HEADS * rows * keys * 256, transcendentals=HEADS * rows * keys, bytes_accessed=rows * 768 * 10
        ),
        name="attend",
    )(mixed, keys_values, keys_values, kaug, *begun)


def attend_back_kernel(q, do, att, aq, k, v, act_rows, act_keys, kaug_t, dq, dk, dv, weight_grad, kp, vp, dkt, dvt, dqs):
    step = pl.program_id(1)
    rows = q.shape[0]
    keys = k.shape[0]
    tiles = up(keys, TILE) // TILE

    @pl.when(step == 0)
    def _():
        rest = jnp.zeros((HEAD - 16, kp.shape[2]), bf16)
        zero = jnp.zeros((HEAD, kp.shape[2]), bf16)
        halves = (jnp.concatenate([kaug_t[...], rest, zero], axis=0), jnp.concatenate([zero, kaug_t[...], rest], axis=0))
        for source, held in ((k, kp), (v, vp)):
            spread_heads(source, held, lambda j: halves[j])
        dkt[...] = jnp.zeros_like(dkt)
        dvt[...] = jnp.zeros_like(dvt)

    lane = lax.broadcasted_iota(jnp.int32, (rows, 128), 1)
    product = do[...].astype(f32) * att[...].astype(f32)
    inner0 = jnp.sum(jnp.where(lane < HEAD, product, 0.0), axis=1, keepdims=True)
    inner1 = jnp.sum(jnp.where(lane < HEAD, 0.0, product), axis=1, keepdims=True)
    hi, mid, low = split3(-jnp.where(lane < HEAD, inner0, inner1))
    within = lane % HEAD
    ado = jnp.where(within == 0, hi, jnp.where(within == 1, mid, jnp.where(within == 2, low, 0.0))).astype(bf16)
    qa = jnp.concatenate([q[...], aq[...]], axis=1)
    da = jnp.concatenate([do[...], ado], axis=1)
    qt = flip(q[...])
    dot_ = flip(do[...])
    units = [(j, t) for j in range(2) for t in range(tiles)]
    totals = [None, None]

    def scores(j, t):
        cols = slice(t * TILE, (t + 1) * TILE)
        return dot(qa, kp[j, :, cols]), dot(da, vp[j, :, cols])

    def weigh(s, dp):
        p = jnp.exp2(s)
        return p.astype(bf16), (p * dp).astype(bf16)

    def collect(j, t, p, ds):
        cols = slice(t * TILE, (t + 1) * TILE)
        part = slice(j * HEAD, (j + 1) * HEAD)
        dvt[part, cols] += dot(dot_[part], p)
        dkt[part, cols] += dot(qt[part], ds)
        more = dot(ds[:, : min(TILE, keys - t * TILE)], k[t * TILE : min(keys, (t + 1) * TILE), :])
        totals[j] = more if totals[j] is None else totals[j] + more

    raw = {}
    ready = {}
    count = len(units)
    for i in range(count + 2):
        if i < count:
            raw[i] = scores(*units[i])
        if 0 <= i - 1 < count:
            ready[i - 1] = weigh(*raw.pop(i - 1))
        if 0 <= i - 2 < count:
            collect(*units[i - 2], *ready.pop(i - 2))
    grad_q = (jnp.where(lane < HEAD, totals[0], totals[1]) * HEAD ** (-0.5)).astype(bf16)
    dq[...] = grad_q
    dqs[pl.ds(pl.multiple_of(step * rows, 16), rows), :] = grad_q

    @pl.when(step == pl.num_programs(1) - 1)
    def _():
        total = jnp.zeros((128, act_rows.shape[1]), f32)
        for base, size in blocks_of(dqs.shape[0], TILE):
            total += dot(flip(dqs[base : base + size]), act_rows[base : base + size])
        weight_grad[:, 0:128] = total.T.astype(bf16)
        total = jnp.zeros((256, act_rows.shape[1]), f32)
        for base, size in blocks_of(keys, TILE):
            grad_k = (dkt[:, base : base + size] * LN2).astype(bf16)
            grad_v = dvt[:, base : base + size].astype(bf16)
            dk[base : base + size] = grad_k.T
            dv[base : base + size] = grad_v.T
            total += dot(jnp.concatenate([grad_k, grad_v], axis=0), act_keys[base : base + size])
        weight_grad[:, 128:384] = total.T.astype(bf16)


def attend_back(start, pairs, mixed, keys_values, grad_att, att, aq, act, act_keys, kaug_t):
    rows, width = act.shape
    keys = keys_values.shape[0]
    wide = up(keys, TILE)
    size = tile_of(rows, 512)
    first = keys_values.shape[1] // 128 - HEADS
    here = pl.BlockSpec((size, 128), lambda h, r: (r, start + h))
    whole = pl.BlockSpec((keys, 128), lambda h, r: (0, h))
    return pl.pallas_call(
        attend_back_kernel,
        grid=(pairs, rows // size),
        in_specs=[
            here,
            here,
            here,
            here,
            pl.BlockSpec((keys, 128), lambda h, r: (0, first + start + h)),
            pl.BlockSpec((keys, 128), lambda h, r: (0, first + HEADS // 2 + start + h)),
            pl.BlockSpec((rows, width), lambda h, r: (0, 0), pipeline_mode=pl.Buffered(1)),
            pl.BlockSpec((keys, width), lambda h, r: (0, 0), pipeline_mode=pl.Buffered(1)),
            pl.BlockSpec((16, wide), lambda h, r: (0, 0), pipeline_mode=pl.Buffered(1)),
        ],
        out_specs=[
            pl.BlockSpec((size, 128), lambda h, r: (r, h)),
            whole,
            whole,
            pl.BlockSpec((width, 384), lambda h, r: (0, h)),
        ],
        out_shape=[
            jax.ShapeDtypeStruct((rows, pairs * 128), bf16),
            jax.ShapeDtypeStruct((keys, pairs * 128), bf16),
            jax.ShapeDtypeStruct((keys, pairs * 128), bf16),
            jax.ShapeDtypeStruct((width, pairs * 384), bf16),
        ],
        scratch_shapes=[
            pltpu.VMEM((2, 256, wide), bf16),
            pltpu.VMEM((2, 256, wide), bf16),
            pltpu.VMEM((128, wide), f32),
            pltpu.VMEM((128, wide), f32),
            pltpu.VMEM((rows, 128), bf16),
        ],
        compiler_params=pltpu.CompilerParams(vmem_limit_bytes=VMEM),
        cost_estimate=pl.CostEstimate(
            flops=20 * pairs * rows * keys * 200, transcendentals=2 * pairs * rows * keys, bytes_accessed=rows * 768 * 20
        ),
        name="attend_back",
    )(mixed, grad_att, att, aq, keys_values, keys_values, act, act_keys, kaug_t)


def norm_stats(value):
    average = jnp.mean(value, axis=-1, keepdims=True)
    centered = value - average
    variance = jnp.mean(centered * centered, axis=-1, keepdims=True)
    scale = lax.rsqrt(variance + epsilon)
    return centered * scale, scale


def norm_back(unit, scale, gain, grad):
    inner = grad * gain
    along = jnp.mean(inner * unit, axis=-1, keepdims=True)
    return scale * (inner - jnp.mean(inner, axis=-1, keepdims=True) - unit * along)


def gelu_pair(value):
    size = jnp.abs(value)
    bell = jnp.exp2(value * value * (-0.5 * LOG2E))
    base = 1.0 + 0.231641888 * size
    t = pl.reciprocal(base, approx=True)
    t = t * (2.0 - base * t)
    fit = t * (0.127414796 + t * (-0.142248368 + t * (0.7107068705 + t * (-0.7265760135 + t * 0.5307027145))))
    tail = fit * bell
    share = jnp.where(value >= 0.0, 1.0 - tail, tail)
    return value * share, share + value * (bell * 0.3989422804014327)


def column_sums(grad):
    return jnp.sum(grad, axis=0, keepdims=True)


def project_kernel(x, gain, bias, weight, col_scale, col_bias, *refs):
    mixed, act_out, x_out = refs[-3:]
    x_out[...] = x[...]
    unit, _ = norm_stats(x[...].astype(f32))
    act = (unit * gain[...] + bias[...]).astype(bf16)
    act_out[...] = act
    mixed[...] = (dot(act, weight[...]) * col_scale[...] + col_bias[...]).astype(bf16)


def fixed(array):
    return pl.BlockSpec(array.shape, lambda i: (0,) * array.ndim, pipeline_mode=pl.Buffered(1))


def project(start, total, x, others, held=()):
    count, width = x.shape
    cols = others[2].shape[1]
    sizes = (cols, width, width)
    tile = tile_of(count, 256)
    return pl.pallas_call(
        project_kernel,
        grid=(count // tile,),
        in_specs=[pl.BlockSpec((tile, width), lambda i: (i, 0))]
        + [fixed(o) for o in others]
        + [pl.BlockSpec(memory_space=pl.ANY) for _ in held],
        out_specs=[pl.BlockSpec((tile, size), lambda i: (start // tile + i, 0)) for size in sizes],
        out_shape=[jax.ShapeDtypeStruct((total, size), bf16) for size in sizes],
        input_output_aliases={6 + i: i for i in range(len(held))},
        compiler_params=pltpu.CompilerParams(vmem_limit_bytes=VMEM),
        name="project",
    )(x, *others, *held)


def middle_kernel(
    x, att, aux, bias_o, gain2, bias2, bias_1, bias_2, gain3, bias3, wo, w1, w2, m1, m2, cot,
    grad_att, grad_low, weight_grads, sums, sums_wide, small, map1g, map2g, pooled,
    hidden, slope, acc1, acc2, acco, stage, sem,
):
    step = pl.program_id(0)
    rows, width = x.shape
    wide = w1.shape[1]
    part = wide // 4

    @pl.when(step == 0)
    def _():
        for ref in (sums, sums_wide, small, map1g, map2g, pooled, acc1, acc2, acco):
            ref[...] = jnp.zeros_like(ref)

    att_low = att[...]
    resid1 = x[...].astype(f32) + dot(att_low, wo[...]) + bias_o[...]
    unit2, scale2 = norm_stats(resid1)
    act2 = (unit2 * gain2[...] + bias2[...]).astype(bf16)
    total = None
    for c in range(4):
        cols = slice(c * part, (c + 1) * part)
        value, rate = gelu_pair(dot(act2, w1[:, cols]) + bias_1[:, cols])
        value = value.astype(bf16)
        hidden[:, cols] = value
        slope[:, cols] = rate.astype(bf16)
        more = dot(value, w2[cols, :])
        total = more if total is None else total + more
    resid2 = resid1 + total + bias_2[...]
    unit3, scale3 = norm_stats(resid2)
    act3 = (unit3 * gain3[...] + bias3[...]).astype(bf16)
    map_hidden, map_slope = gelu_pair(dot(act3, m1[...]) + aux[4:5])
    map_hidden = map_hidden.astype(bf16)
    logits = dot(map_hidden, m2[...]) + aux[3:4]
    lanes = logits.shape[1]
    lane = lax.broadcasted_iota(jnp.int32, (rows, lanes), 1)
    row = lax.broadcasted_iota(jnp.int32, (rows, lanes), 0) + step * rows
    slot = row - (lane >> 3) * PATCH
    mask = (slot >= 0) & (slot.astype(f32) < aux[0:1])
    inverse = aux[1:2]
    raw = 1.0 / (1.0 + jnp.exp2(logits * (-LOG2E)))
    gates = jnp.where(mask, raw, 0.0)
    gates_low = gates.astype(bf16)
    output_low = resid2.astype(bf16)
    pooled[...] += dot(gates_low.T, output_low)
    gate_sum = jnp.sum(gates, axis=1, keepdims=True)
    inverse_row = inverse[:, 0:1]
    small[2:3] += column_sums(gates * (gate_sum - gates))

    grad_out = dot(gates_low, cot[...]) * inverse_row
    grad_gate = dot(output_low, cot[...], NT) * inverse + aux[2:3] * (gate_sum - gates)
    grad_logit = jnp.where(mask, grad_gate * raw * (1.0 - raw), 0.0)
    small[1:2] += column_sums(grad_logit)
    grad_logit = grad_logit.astype(bf16)
    map2g[...] += dot(map_hidden.T, grad_logit)
    grad_mpre = dot(grad_logit, m2[...], NT) * map_slope
    small[0:1] += column_sums(grad_mpre)
    grad_mpre = grad_mpre.astype(bf16)
    map1g[...] += dot(grad_mpre.T, act3)
    grad_act = dot(grad_mpre, m1[...], NT)
    sums[4:5] += column_sums(grad_act * unit3)
    sums[5:6] += column_sums(grad_act)
    grad_res2 = norm_back(unit3, scale3, gain3[...], grad_act) + grad_out

    sums[3:4] += column_sums(grad_res2)
    g2 = grad_res2.astype(bf16)
    g2_t = g2.T
    act2_t = act2.T
    grad_act = None
    for c in range(4):
        cols = slice(c * part, (c + 1) * part)
        grad_pre = dot(g2, w2[cols, :], NT) * slope[:, cols].astype(f32)
        sums_wide[0:1, cols] += column_sums(grad_pre)
        grad_pre = grad_pre.astype(bf16)
        acc2[:, cols] += dot(g2_t, hidden[:, cols])
        acc1[:, cols] += dot(act2_t, grad_pre)
        more = dot(grad_pre, w1[:, cols], NT)
        grad_act = more if grad_act is None else grad_act + more
    sums[1:2] += column_sums(grad_act * unit2)
    sums[2:3] += column_sums(grad_act)
    grad_res1 = norm_back(unit2, scale2, gain2[...], grad_act) + grad_res2

    sums[0:1] += column_sums(grad_res1)
    g1 = grad_res1.astype(bf16)
    grad_low[...] = g1
    acco[...] += dot(att_low.T, g1)
    grad_att[...] = dot(g1, wo[...], NT).astype(bf16)

    @pl.when(step == pl.num_programs(0) - 1)
    def _():
        share = stage.shape[1]
        groups = stage.shape[0]

        def drain(value, *targets):
            stage[...] = value.astype(bf16).reshape(stage.shape)
            copies = [pltpu.make_async_copy(stage.at[lo:hi], target, sem) for lo, hi, target in targets]
            for copy in copies:
                copy.start()
            for copy in copies:
                copy.wait()

        for c in range(4):
            cols = slice(c * part, (c + 1) * part)
            value1 = acc1[:, cols]
            value2 = acc2[:, cols].T
            if groups == 1:
                drain(value1, (0, 1, weight_grads.at[c : c + 1]))
                drain(value2, (0, 1, weight_grads.at[4 + c : 5 + c]))
            else:
                drain(value1, (0, groups, weight_grads.at[:, c]))
                drain(value2, *[(4 * i, 4 * i + 4, weight_grads.at[c * groups // 4 + i, 4:8]) for i in range(groups // 4)])
        if groups == 1:
            drain(acco[...], (0, 1, weight_grads.at[8:9]))
        else:
            drain(acco[...], (0, groups, weight_grads.at[:, 8]))


def middle(groups, x, att, *others):
    rows, width = x.shape
    wide = others[8 + 1].shape[1]
    share = width // groups
    if share % 16 == 0 and groups % 4 == 0:
        stage, blocks = (groups, share, width), (groups, 9, share, width)
    else:
        stage, blocks = (1, width, width), (9, width, width)
    lanes = others[0].shape[1]
    size = tile_of(rows, MIDDLE)
    tile = pl.BlockSpec((size, width), lambda i: (i, 0))
    anywhere = pl.BlockSpec(memory_space=pl.ANY)
    summed = [
        jax.ShapeDtypeStruct((8, width), f32),
        jax.ShapeDtypeStruct((8, wide), f32),
        jax.ShapeDtypeStruct((8, lanes), f32),
        jax.ShapeDtypeStruct((lanes, width), f32),
        jax.ShapeDtypeStruct((lanes, lanes), f32),
        jax.ShapeDtypeStruct((lanes, width), f32),
    ]
    return pl.pallas_call(
        middle_kernel,
        grid=(rows // size,),
        in_specs=[tile, tile] + [fixed(o) for o in others],
        out_specs=[tile, tile, anywhere] + [pl.BlockSpec(s.shape, lambda i: (0, 0)) for s in summed],
        out_shape=[
            jax.ShapeDtypeStruct((rows, width), bf16),
            jax.ShapeDtypeStruct((rows, width), bf16),
            jax.ShapeDtypeStruct(blocks, bf16),
        ]
        + summed,
        scratch_shapes=[
            pltpu.VMEM((size, wide), bf16),
            pltpu.VMEM((size, wide), bf16),
            pltpu.VMEM((width, wide), f32),
            pltpu.VMEM((width, wide), f32),
            pltpu.VMEM((width, width), f32),
            pltpu.VMEM(stage, bf16),
            pltpu.SemaphoreType.DMA,
        ],
        compiler_params=pltpu.CompilerParams(vmem_limit_bytes=VMEM),
        cost_estimate=pl.CostEstimate(
            flops=2 * rows * width * (6 * wide + 3 * width), transcendentals=rows * wide, bytes_accessed=rows * width * 12
        ),
        name="middle",
    )(x, att, *others)


def finish_kernel(place, x, g1, gain, bias, weight, *refs):
    grads, (grad_in, sums) = refs[:-2], refs[-2:]
    parts = len(grads) // 3
    width = x.shape[1]

    @pl.when(pl.program_id(0) == 0)
    def _():
        sums[...] = jnp.zeros_like(sums)

    unit, scale = norm_stats(x[...].astype(f32))
    grad_act = None
    for i in range(3):
        at = 0
        for n in range(parts):
            part = grads[3 * n + i][...]
            share = part.shape[1]
            if i != 1:
                sums[2 + i // 2 : 3 + i // 2, at : at + share] += column_sums(part.astype(f32))
            more = dot(part, weight[:, i * width + at : i * width + at + share], NT)
            grad_act = more if grad_act is None else grad_act + more
            at += share
    sums[0:1] += column_sums(grad_act * unit)
    sums[1:2] += column_sums(grad_act)
    total = norm_back(unit, scale, gain[...], grad_act) + g1[...].astype(f32)
    grad_in[...] = total.astype(grad_in.dtype).reshape(grad_in.shape)


def finish(start, count, x, g1, gain, bias, weight, grads, place=None, places=0):
    width = x.shape[1]
    size = tile_of(count, 256)
    begin = start // size
    tile = pl.BlockSpec((size, width), lambda i, at: (begin + i, 0))
    thin = [pl.BlockSpec((size, grad.shape[1]), lambda i, at: (begin + i, 0)) for grad in grads]
    if place is None:
        place = jnp.int32(0)
        out = (pl.BlockSpec((size, width), lambda i, at: (i, 0)), jax.ShapeDtypeStruct((count, width), bf16))
    else:
        out = (
            pl.BlockSpec((1, size, width), lambda i, at: (at[0], i, 0)),
            jax.ShapeDtypeStruct((places, count, width), f32),
        )

    def one(array):
        return pl.BlockSpec(array.shape, lambda i, at: (0, 0), pipeline_mode=pl.Buffered(1))

    return pl.pallas_call(
        finish_kernel,
        grid_spec=pltpu.PrefetchScalarGridSpec(
            num_scalar_prefetch=1,
            grid=(count // size,),
            in_specs=[tile] * 2 + [one(o) for o in (gain, bias, weight)] + thin,
            out_specs=[out[0], pl.BlockSpec((8, width), lambda i, at: (0, 0))],
        ),
        out_shape=[out[1], jax.ShapeDtypeStruct((8, width), f32)],
        compiler_params=pltpu.CompilerParams(vmem_limit_bytes=VMEM),
        cost_estimate=pl.CostEstimate(flops=1, transcendentals=0, bytes_accessed=1),
        name="finish",
    )(place.reshape(1), x, g1, gain, bias, weight, *grads)


def shards(
    inputs,
    frame_tokens,
    clip_frames,
    norm1_gain,
    norm1_bias,
    qkv_weight,
    query_bias,
    value_bias,
    out_weight,
    out_bias,
    norm2_gain,
    norm2_bias,
    fc1_weight,
    fc1_bias,
    fc2_weight,
    fc2_bias,
    learn_gain,
    learn_bias,
    map1_weight,
    map1_bias,
    map2_weight,
    map2_bias,
    cot_pooled,
):
    clip_count, piece, width = inputs.shape
    seq_size = lax.axis_size("seq")
    position = lax.axis_index("seq")
    clip_size = lax.axis_size("clip")
    frames_here = piece // PATCH
    scaling = HEAD ** (-0.5)
    slots_all = float(clip_count * clip_size * seq_size * frames_here)
    group = seq_size // clip_count
    mine = position // group
    seat = position % group

    def route(turn):
        return [
            (s, ((s % clip_count + turn) % clip_count) * group + s // clip_count) for s in range(seq_size)
        ]

    def send(value, turn, back=False):
        pairs = route(turn)
        if back:
            pairs = [(b, a) for a, b in pairs]
        if all(a == b for a, b in pairs):
            return value
        return lax.ppermute(value, "seq", pairs)

    def scatter(whole):
        return [
            send(lax.dynamic_index_in_dim(whole, (position + turn) % clip_count, 0, False), turn)
            for turn in range(clip_count)
        ]

    def gather_back(parts, kind, whole=None):
        if whole is None:
            whole = jnp.zeros((clip_count,) + parts[0].shape, kind)
        for turn, part in enumerate(parts):
            if part is not None:
                home = send(part, turn, True).astype(kind)
                whole = lax.dynamic_update_index_in_dim(whole, home, (position + turn) % clip_count, 0)
        return whole

    tokens = lax.dynamic_index_in_dim(frame_tokens, mine, 0, False)
    frames = lax.dynamic_index_in_dim(clip_frames, mine, 0, False)
    rows = clip_count * piece
    keys = group * rows
    split = piece % 16 == 0 and group == 1
    near = piece // TILE * TILE
    x_parts = scatter(inputs)
    cot = jnp.concatenate(scatter(cot_pooled), axis=0).reshape(clip_count * frames_here * NTOK, width)

    def placed(ids, at_seat):
        turn = ids // piece
        source = clip_count * at_seat + (mine - turn) % clip_count
        local = ids - turn * piece
        frame = local // PATCH
        slot = local - frame * PATCH
        return (source * frames_here + frame < frames) & (slot < tokens)

    key_ids = jnp.arange(keys, dtype=jnp.int32)
    key_inside = placed(key_ids % rows, key_ids // rows)
    lane16 = jnp.arange(HEAD)
    key_mask = jnp.where(key_inside, 0.0, masked_score)
    kaug = jnp.where(lane16[None, :] < 3, 1.0, jnp.where(lane16[None, :] == 3, key_mask[:, None], 0.0)).astype(bf16)
    kaug = jnp.concatenate([kaug, jnp.zeros_like(kaug)], axis=1)
    sub16 = jnp.arange(16)[:, None]
    wide_mask = jnp.pad(key_mask, (0, up(keys, TILE) - keys), constant_values=masked_score)
    kaug_t = jnp.where(sub16 < 3, 1.0, jnp.where(sub16 == 3, wide_mask[None, :], 0.0)).astype(bf16)

    def line(vector):
        return vector.reshape(1, -1)

    zeros = jnp.zeros((width,), f32)
    ones = jnp.ones((width,), f32)
    col_scale = line(jnp.concatenate([ones * (scaling * LOG2E), ones, ones]))
    col_bias = line(jnp.concatenate([query_bias * (scaling * LOG2E), zeros, value_bias]))
    others = (line(norm1_gain), line(norm1_bias), qkv_weight, col_scale, col_bias)
    begun = ()
    if split:
        held = project(0, rows, x_parts[0], others)
        held, begun = lax.optimization_barrier((held, (attend_near(near, held[0], kaug),)))
        mixed, act1, x_low = project(piece, rows, jnp.concatenate(x_parts[1:], axis=0), others, held)
    else:
        mixed, act1, x_low = project(0, rows, jnp.concatenate(x_parts, axis=0), others)
    if group == 1:
        keys_values, act_keys = mixed, act1
    else:
        both = lax.all_gather(mixed[:, width:], "seq", axis=0, tiled=True)
        keys_values = lax.dynamic_slice_in_dim(both, mine * keys, keys, 0)
        act_keys = lax.all_gather(act1, "seq", axis=0, tiled=True)
        act_keys = lax.dynamic_slice_in_dim(act_keys, mine * keys, keys, 0)
    att, aq = attend(mixed, keys_values, kaug, *begun)

    slots = clip_count * frames_here * NTOK
    lanes = -(-slots // 128) * 128
    pair_count = NTOK * (NTOK - 1)
    lane_ids = jnp.arange(lanes)
    lane_turn = lane_ids // (frames_here * NTOK)
    lane_frame = lane_ids // NTOK - lane_turn * frames_here
    lane_source = clip_count * seat + (mine - lane_turn) % clip_count
    lane_open = (lane_source * frames_here + lane_frame < frames) & (lane_ids < slots)
    inverse = lax.rsqrt(tokens.astype(f32))
    factor = 2.0 / pair_count * inverse * inverse / slots_all
    map_size = map1_bias.shape[0]
    aux = jnp.stack(
        [
            jnp.where(lane_open, tokens, 0).astype(f32),
            jnp.full((lanes,), inverse),
            jnp.full((lanes,), factor),
            jnp.tile(map2_bias, lanes // NTOK),
            jnp.pad(map1_bias, (0, lanes - map_size)),
        ]
        + [jnp.zeros((lanes,), f32)] * 3
    )
    map1_wide = jnp.pad(map1_weight, ((0, 0), (0, lanes - map_size)))
    map2_wide = jnp.pad(jnp.tile(map2_weight, (1, lanes // NTOK)), ((0, lanes - map_size), (0, 0)))
    cot = jnp.pad(cot, ((0, lanes - slots), (0, 0)))
    grad_att, grad_low, weight_part, sums, sums_wide, small, map1_part, map2_part, pooled = middle(
        clip_size,
        x_low,
        att,
        aux,
        line(out_bias),
        line(norm2_gain),
        line(norm2_bias),
        line(fc1_bias),
        line(fc2_bias),
        line(learn_gain),
        line(learn_bias),
        out_weight,
        fc1_weight,
        fc2_weight,
        map1_wide,
        map2_wide,
        cot,
    )

    def over_clip(matrix):
        return lax.psum_scatter(matrix, "clip", scatter_dimension=0, tiled=True)

    def over_seq(*matrices):
        thin = width // seq_size
        blocks = [
            m.reshape(m.shape[0], seq_size, -1, thin).transpose(1, 0, 2, 3).reshape(seq_size, -1, thin)
            for m in matrices
        ]
        total = lax.psum_scatter(jnp.concatenate(blocks, axis=1), "seq", scatter_dimension=0, tiled=False)
        outs = []
        at = 0
        for m, block in zip(matrices, blocks):
            count = block.shape[1]
            outs.append(total[at : at + count].reshape(m.shape[0], -1).astype(f32))
            at += count
        return outs

    def bits(size):
        return [1 << n for n in range(size.bit_length() - 1)]

    clip_steps = [("clip", bit) for bit in bits(clip_size)]
    seq_steps = [("seq", bit) for bit in bits(seq_size)]
    early_steps = clip_steps[:1] + seq_steps + clip_steps[1:]

    def meet(value, step):
        axis, bit = step
        return lax.ppermute(value, axis, [(i, i ^ bit) for i in range(lax.axis_size(axis))])

    def part_ways(blocks, step):
        axis, bit = step
        halves = blocks.reshape((-1, 2) + blocks.shape[1:])
        side = (lax.axis_index(axis) // bit) % 2
        away = lax.dynamic_index_in_dim(halves, 1 - side, 1, False)
        return lax.dynamic_index_in_dim(halves, side, 1, False), meet(away, step)

    def add_low(kept, received):
        return (kept.astype(f32) + received.astype(f32)).astype(bf16)

    def back(start, pairs, source):
        return attend_back(
            start, pairs, source, keys_values if group > 1 else source, grad_att, att, aq, act1, act_keys, kaug_t
        )

    tie = lax.optimization_barrier
    pairs = (4, 2)
    early = jnp.concatenate(
        [
            sums.reshape(-1),
            sums_wide[0],
            small.reshape(-1) * jnp.repeat(jnp.stack([1.0, 1.0, inverse * inverse] + [1.0] * 5), lanes),
            map1_part[:map_size].reshape(-1),
            jnp.sum(map2_part[:map_size].reshape(map_size, lanes // NTOK, NTOK), axis=1).reshape(-1),
        ]
    )
    share = width // clip_size
    if weight_part.ndim == 3:
        fc1_part = weight_part[:4].reshape(4, clip_size, share, width).transpose(1, 0, 2, 3)
        fc2_part = weight_part[4:8].reshape(clip_size, 4, share, width)
        weight_part = jnp.concatenate([fc1_part, fc2_part, weight_part[8].reshape(clip_size, 1, share, width)], axis=1)
    slab = over_clip(weight_part)[0]
    near_early = meet(early, early_steps[0])
    back0 = back(0, pairs[0], mixed)
    mixed, slab, early, near_early, back0 = tie((mixed, slab, early, near_early, back0))
    early = early + near_early
    near_early = meet(early, early_steps[1])
    fc1_grad, fc2_grad, out_grad = over_seq(
        slab[:4].transpose(1, 0, 2).reshape(share, 4 * width), slab[4:8].reshape(4 * share, width), slab[8]
    )
    slab0 = over_clip(back0[3])
    back1 = back(pairs[0], pairs[1], mixed)
    fc1_grad, fc2_grad, out_grad, slab0, early, near_early, back1 = tie(
        (fc1_grad, fc2_grad, out_grad, slab0, early, near_early, back1)
    )
    early = early + near_early
    pooled = (pooled[:slots] * inverse).astype(bf16).reshape(clip_count, frames_here, NTOK, width)
    pooled = gather_back([pooled[t] for t in range(clip_count)], bf16)

    grads = [list(one[:3]) for one in (back0, back1)]
    if group > 1:
        both = jnp.zeros((seq_size * rows, 2 * width), bf16)
        both = lax.dynamic_update_slice_in_dim(
            both, jnp.concatenate([one[i] for i in (1, 2) for one in grads], axis=1), mine * keys, 0
        )
        both = lax.psum_scatter(both, "seq", scatter_dimension=0, tiled=True)
        at = 0
        for i in (1, 2):
            for n in range(2):
                grads[n][i] = both[:, at : at + pairs[n] * 128]
                at += pairs[n] * 128
    grads = [grad for one in grads for grad in one]
    rest = (grad_low, line(norm1_gain), line(norm1_bias), qkv_weight, grads)
    near_early = meet(early, early_steps[2])
    kept, received = part_ways(back1[3].reshape(clip_size, share, -1), clip_steps[0])
    if split:
        far, late = finish(piece, rows - piece, x_low, *rest)
        far = [far[t * piece : (t + 1) * piece] for t in range(clip_count - 1)]
        far, x_low, late, near_early, received = tie((far, x_low, late, near_early, received))
    early = early + near_early
    near_early = meet(early, early_steps[3])
    kept, received = part_ways(add_low(kept, received), clip_steps[1])
    if split:
        local, local_sums = finish(0, piece, x_low, *rest, place=position % clip_count, places=clip_count)
        local, local_sums, near_early, received = tie((local, local_sums, near_early, received))
        input_grad = gather_back([None] + far, f32, local)
        late = (local_sums + late)[:4]
    else:
        local, late = finish(0, rows, x_low, *rest)
        input_grad = gather_back([local[t * piece : (t + 1) * piece] for t in range(clip_count)], f32)
        late = late[:4]
    early = early + near_early
    for step in early_steps[4:]:
        early = early + meet(early, step)
    slab1 = add_low(kept, received)
    for step in clip_steps[2:]:
        slab1 = add_low(*part_ways(slab1, step))
    for step in clip_steps + seq_steps:
        late = late + meet(late, step)
    qkv = [
        part.reshape(share, count, 3, 128).transpose(0, 2, 1, 3) for part, count in zip((slab0, slab1), pairs)
    ]
    qkv = jnp.concatenate(qkv, axis=2).reshape(share, seq_size, -1).transpose(1, 0, 2)
    for step in seq_steps:
        qkv = add_low(*part_ways(qkv, step))
    qkv_grad = qkv[0].astype(f32)

    at = 0
    taken = []
    for size in (sums.size, sums_wide.shape[1], small.size, map_size * width, map_size * NTOK):
        taken.append(early[at : at + size])
        at += size
    sums, fc1_bias_grad, small, map1_grad, map2_grad = taken
    sums = sums.reshape(8, width)
    small = small.reshape(8, lanes)
    map1_grad = map1_grad.reshape(map_size, width).T
    map2_grad = map2_grad.reshape(map_size, NTOK)
    map2_bias_grad = jnp.sum(small[1].reshape(lanes // NTOK, NTOK), axis=0)
    penalty = jnp.sum(small[2]) / pair_count / slots_all
    return (
        pooled,
        penalty,
        input_grad,
        late[0],
        late[1],
        qkv_grad,
        late[2],
        late[3],
        out_grad,
        sums[0],
        sums[1],
        sums[2],
        fc1_grad,
        fc1_bias_grad,
        fc2_grad,
        sums[3],
        sums[4],
        sums[5],
        map1_grad,
        small[0, :map_size],
        map2_grad,
        map2_bias_grad,
    )


def solution(mesh):
    row_spec = P("clip", "seq", None)
    pool_spec = P("clip", "seq", None, None)
    matrix_spec = P("clip", "seq")
    in_specs = (row_spec, P("clip"), P("clip")) + (P(),) * 19 + (pool_spec,)
    out_specs = (
        (pool_spec, P(), row_spec, P(), P(), matrix_spec, P(), P(), matrix_spec, P(), P(), P(), matrix_spec, P())
        + (matrix_spec,)
        + (P(),) * 7
    )
    return jax.shard_map(shards, mesh=mesh, in_specs=in_specs, out_specs=out_specs, check_vma=False)
```

```python
import jax
import jax.numpy as jnp
from jax import lax
from jax.experimental import pallas as pl
from jax.experimental.pallas import tpu as pltpu
from jax.sharding import PartitionSpec as P

HEADS = 12
HEAD = 64
NTOK = 8
PATCH = 196
TILE = 256
AHEAD = 0
MIDDLE = 448
LOG2E = 1.4426950408889634
LN2 = 0.6931471805599453
VMEM = 60 * 1024 * 1024

epsilon = 1e-06
masked_score = -1e30
bf16 = jnp.bfloat16
f32 = jnp.float32

NN = (((1,), (0,)), ((), ()))
NT = (((1,), (1,)), ((), ()))


def dot(left, right, dims=NN):
    return lax.dot_general(left, right, dims, preferred_element_type=f32)


def split3(value):
    hi = value.astype(bf16).astype(f32)
    mid = (value - hi).astype(bf16).astype(f32)
    return hi, mid, value - hi - mid


def up(count, unit):
    return -(-count // unit) * unit


def tile_of(count, most):
    return max(size for size in range(16, most + 1, 16) if count % size == 0)


def blocks_of(count, unit):
    return [(base, min(unit, count - base)) for base in range(0, count, unit)]


def flip(value):
    return jnp.concatenate([value[base : base + size].T for base, size in blocks_of(value.shape[0], 128)], axis=1)


def spread_heads(source, held, aug):
    count = source.shape[0]
    zero = jnp.zeros((HEAD, held.shape[2]), bf16)
    for j in range(2):
        other = (1 - j) * HEAD
        held[j, other : other + HEAD] = zero
        if held.shape[2] > count:
            edge = count // 128 * 128
            held[j, j * HEAD : (j + 1) * HEAD, edge:] = jnp.zeros((HEAD, held.shape[2] - edge), bf16)
        held[j, 128:256] = aug(j)
    for base, size in blocks_of(count, 256):
        flat = flip(source[base : base + size])
        for j in range(2):
            held[j, j * HEAD : (j + 1) * HEAD, base : base + size] = flat[j * HEAD : (j + 1) * HEAD]


def spread_queries(q, qp):
    ids = lax.broadcasted_iota(jnp.int32, (128, qp.shape[2]), 0)
    spread_heads(q, qp, lambda j: jnp.where(ids == 3, 1.0, 0.0).astype(bf16))


def flip_into(source, target):
    for base, size in blocks_of(source.shape[0], 256):
        target[:, base : base + size] = flip(source[base : base + size])


def key_block(k, kaug, base, size):
    return jnp.concatenate([k[pl.ds(base, size), :], kaug[pl.ds(base, size), :]], axis=1)


def value_block(vt, j, base, size):
    ones = jnp.ones((16, size), bf16)
    return jnp.concatenate([vt[j * HEAD : (j + 1) * HEAD, pl.ds(base, size)], ones], axis=0)


def over_tiles(step, begin, count):
    @pl.loop(begin // TILE, count // TILE, unroll=3)
    def _(t):
        step(pl.multiple_of(t * TILE, TILE), TILE)

    if count % TILE:
        step(count // TILE * TILE, count % TILE)


def fold_tile(k, kaug, qp, vt, acc, low, fresh, base, size):
    for j in range(2):
        p = jnp.exp2(dot(key_block(k, kaug, base, size), qp[j, :, low:])).astype(bf16)
        part = dot(value_block(vt, j, base, size), p)
        if fresh:
            acc[j, :, low:] = part
        else:
            acc[j, :, low:] += part


def attend_near_kernel(q, k, v, kaug, acc, qp, vt):
    spread_queries(q, qp)
    flip_into(v, vt)
    fold_tile(k, kaug, qp, vt, acc, 0, True, 0, TILE)
    over_tiles(lambda base, size: fold_tile(k, kaug, qp, vt, acc, 0, False, base, size), TILE, k.shape[0])


def attend_near(near, mixed, kaug):
    pairs = HEADS // 2
    return pl.pallas_call(
        attend_near_kernel,
        grid=(pairs,),
        in_specs=[
            pl.BlockSpec((near, 128), lambda h: (0, h)),
            pl.BlockSpec((near, 128), lambda h: (0, pairs + h)),
            pl.BlockSpec((near, 128), lambda h: (0, 2 * pairs + h)),
            pl.BlockSpec((near, 128), lambda h: (0, 0)),
        ],
        out_specs=pl.BlockSpec((2, HEAD + 16, near), lambda h: (h, 0, 0)),
        out_shape=jax.ShapeDtypeStruct((HEADS, HEAD + 16, near), f32),
        scratch_shapes=[pltpu.VMEM((2, 256, near), bf16), pltpu.VMEM((128, near), bf16)],
        compiler_params=pltpu.CompilerParams(vmem_limit_bytes=VMEM),
        cost_estimate=pl.CostEstimate(
            flops=4 * HEADS * near * near * 256, transcendentals=HEADS * near * near, bytes_accessed=near * 768 * 10
        ),
        name="attend_near",
    )(mixed, mixed, mixed, kaug)


def attend_kernel(q, k, v, kaug, *refs):
    att, aq, qp, vt, acc = refs[-5:]
    rows = q.shape[0]
    keys = k.shape[0]
    wide = qp.shape[2]
    spread_queries(q, qp)
    flip_into(v, vt)

    def fold(low, fresh):
        return lambda base, size: fold_tile(k, kaug, qp, vt, acc, low, fresh, base, size)

    begun = 0
    if len(refs) > 5:
        begun = refs[0].shape[2]
        acc[:, :, :begun] = refs[0][...]
    fold(begun, True)(0, TILE)
    if begun:
        over_tiles(fold(begun, False), TILE, begun)
    over_tiles(fold(0, False), max(begun, TILE), keys)

    for j in range(2):
        total = acc[j, HEAD : HEAD + 1]
        fine = (total > 2.0**-60) & (total < 2.0**60)
        bad = jnp.max(jnp.where(fine, 0.0, 1.0)) > 0.5
        acc[j, HEAD + 8 : HEAD + 9] = jnp.zeros((1, wide), f32)

        @pl.when(bad)
        def _():
            acc[j, 0:1] = jnp.full((1, wide), -1e38, f32)

            def largest(base, size):
                s = dot(key_block(k, kaug, base, size), qp[j])
                acc[j, 0:1] = jnp.maximum(acc[j, 0:1], jnp.max(s, axis=0, keepdims=True))

            over_tiles(largest, 0, keys)
            best = acc[j, 0:1]
            acc[j] = jnp.zeros((HEAD + 16, wide), f32)

            def again(base, size):
                p = jnp.exp2(dot(key_block(k, kaug, base, size), qp[j]) - best).astype(bf16)
                acc[j] += dot(value_block(vt, j, base, size), p)

            over_tiles(again, 0, keys)
            acc[j, HEAD + 8 : HEAD + 9] = best

    ids = lax.broadcasted_iota(jnp.int32, (HEAD, 128), 0)
    for base, size in blocks_of(rows, 128):
        here = slice(base, base + 128)
        outs = []
        augs = []
        for j in range(2):
            total = acc[j, HEAD : HEAD + 1, here]
            outs.append(acc[j, 0:HEAD, here] * (1.0 / total))
            lse = jnp.log2(total) + acc[j, HEAD + 8 : HEAD + 9, here]
            hi, mid, low = split3(-lse)
            aug = jnp.where(ids == 0, hi, jnp.where(ids == 1, mid, jnp.where(ids == 2, low, 0.0)))
            augs.append(jnp.where(ids == 3, 1.0, aug))
        att[base : base + size, :] = jnp.concatenate(outs, axis=0).T[:size].astype(bf16)
        aq[base : base + size, :] = jnp.concatenate(augs, axis=0).T[:size].astype(bf16)


def attend(mixed, keys_values, kaug, *begun):
    rows = mixed.shape[0]
    keys = keys_values.shape[0]
    pairs = HEADS // 2
    wide = up(rows, 128)
    first = keys_values.shape[1] // 128 - 2 * pairs
    return pl.pallas_call(
        attend_kernel,
        grid=(pairs,),
        in_specs=[
            pl.BlockSpec((rows, 128), lambda h: (0, h)),
            pl.BlockSpec((keys, 128), lambda h: (0, first + h)),
            pl.BlockSpec((keys, 128), lambda h: (0, first + pairs + h)),
            pl.BlockSpec((keys, 128), lambda h: (0, 0)),
        ]
        + [pl.BlockSpec((2,) + one.shape[1:], lambda h: (h, 0, 0)) for one in begun],
        out_specs=[
            pl.BlockSpec((rows, 128), lambda h: (0, h)),
            pl.BlockSpec((rows, 128), lambda h: (0, h)),
        ],
        out_shape=[
            jax.ShapeDtypeStruct((rows, HEADS * HEAD), bf16),
            jax.ShapeDtypeStruct((rows, HEADS * HEAD), bf16),
        ],
        scratch_shapes=[
            pltpu.VMEM((2, 256, wide), bf16),
            pltpu.VMEM((128, up(keys, 128)), bf16),
            pltpu.VMEM((2, HEAD + 16, wide), f32),
        ],
        compiler_params=pltpu.CompilerParams(vmem_limit_bytes=VMEM),
        cost_estimate=pl.CostEstimate(
            flops=4 * HEADS * rows * keys * 256, transcendentals=HEADS * rows * keys, bytes_accessed=rows * 768 * 10
        ),
        name="attend",
    )(mixed, keys_values, keys_values, kaug, *begun)


def attend_back_kernel(q, do, att, aq, k, v, act_rows, act_keys, kaug_t, dq, dk, dv, weight_grad, kp, vp, dkt, dvt, dqs):
    step = pl.program_id(1)
    rows = q.shape[0]
    keys = k.shape[0]
    tiles = up(keys, TILE) // TILE

    @pl.when(step == 0)
    def _():
        rest = jnp.zeros((HEAD - 16, kp.shape[2]), bf16)
        zero = jnp.zeros((HEAD, kp.shape[2]), bf16)
        halves = (jnp.concatenate([kaug_t[...], rest, zero], axis=0), jnp.concatenate([zero, kaug_t[...], rest], axis=0))
        for source, held in ((k, kp), (v, vp)):
            spread_heads(source, held, lambda j: halves[j])
        dkt[...] = jnp.zeros_like(dkt)
        dvt[...] = jnp.zeros_like(dvt)

    units = [(j, t) for j in range(2) for t in range(tiles)]
    count = len(units)
    totals = [None, None]
    qa = jnp.concatenate([q[...], aq[...]], axis=1)

    def cols(t):
        return slice(t * TILE, (t + 1) * TILE)

    def scores(i):
        j, t = units[i]
        return dot(qa, kp[j, :, cols(t)])

    def weigh(s, dp):
        p = jnp.exp2(s)
        return p.astype(bf16), (p * dp).astype(bf16)

    def collect(j, t, p, ds):
        part = slice(j * HEAD, (j + 1) * HEAD)
        dvt[part, cols(t)] += dot(dot_[part], p)
        dkt[part, cols(t)] += dot(qt[part], ds)
        more = dot(ds[:, : min(TILE, keys - t * TILE)], k[t * TILE : min(keys, (t + 1) * TILE), :])
        totals[j] = more if totals[j] is None else totals[j] + more

    ahead = AHEAD
    raw = {i: scores(i) for i in range(min(ahead, count))}
    lane = lax.broadcasted_iota(jnp.int32, (rows, 128), 1)
    product = do[...].astype(f32) * att[...].astype(f32)
    inner0 = jnp.sum(jnp.where(lane < HEAD, product, 0.0), axis=1, keepdims=True)
    inner1 = jnp.sum(jnp.where(lane < HEAD, 0.0, product), axis=1, keepdims=True)
    hi, mid, low = split3(-jnp.where(lane < HEAD, inner0, inner1))
    within = lane % HEAD
    ado = jnp.where(within == 0, hi, jnp.where(within == 1, mid, jnp.where(within == 2, low, 0.0))).astype(bf16)
    da = jnp.concatenate([do[...], ado], axis=1)
    ready = {}
    for i in range(count + 2):
        if i < count:
            j, t = units[i]
            s = raw.pop(i) if i in raw else scores(i)
            raw[i] = (s, dot(da, vp[j, :, cols(t)]))
        if i == 1:
            qt = flip(q[...])
            dot_ = flip(do[...])
        if 0 <= i - 1 < count:
            ready[i - 1] = weigh(*raw.pop(i - 1))
        if 0 <= i - 2 < count:
            collect(*units[i - 2], *ready.pop(i - 2))
    grad_q = (jnp.where(lane < HEAD, totals[0], totals[1]) * HEAD ** (-0.5)).astype(bf16)
    dq[...] = grad_q
    dqs[pl.ds(pl.multiple_of(step * rows, 16), rows), :] = grad_q

    @pl.when(step == pl.num_programs(1) - 1)
    def _():
        total = jnp.zeros((128, act_rows.shape[1]), f32)
        for base, size in blocks_of(dqs.shape[0], TILE):
            total += dot(flip(dqs[base : base + size]), act_rows[base : base + size])
        weight_grad[:, 0:128] = total.T.astype(bf16)
        total = jnp.zeros((256, act_rows.shape[1]), f32)
        for base, size in blocks_of(keys, TILE):
            grad_k = (dkt[:, base : base + size] * LN2).astype(bf16)
            grad_v = dvt[:, base : base + size].astype(bf16)
            dk[base : base + size] = grad_k.T
            dv[base : base + size] = grad_v.T
            total += dot(jnp.concatenate([grad_k, grad_v], axis=0), act_keys[base : base + size])
        weight_grad[:, 128:384] = total.T.astype(bf16)


def attend_back(start, pairs, mixed, keys_values, grad_att, att, aq, act, act_keys, kaug_t):
    rows, width = act.shape
    keys = keys_values.shape[0]
    wide = up(keys, TILE)
    size = tile_of(rows, 512)
    first = keys_values.shape[1] // 128 - HEADS
    here = pl.BlockSpec((size, 128), lambda h, r: (r, start + h))
    whole = pl.BlockSpec((keys, 128), lambda h, r: (0, h))
    return pl.pallas_call(
        attend_back_kernel,
        grid=(pairs, rows // size),
        in_specs=[
            here,
            here,
            here,
            here,
            pl.BlockSpec((keys, 128), lambda h, r: (0, first + start + h)),
            pl.BlockSpec((keys, 128), lambda h, r: (0, first + HEADS // 2 + start + h)),
            pl.BlockSpec((rows, width), lambda h, r: (0, 0), pipeline_mode=pl.Buffered(1)),
            pl.BlockSpec((keys, width), lambda h, r: (0, 0), pipeline_mode=pl.Buffered(1)),
            pl.BlockSpec((16, wide), lambda h, r: (0, 0), pipeline_mode=pl.Buffered(1)),
        ],
        out_specs=[
            pl.BlockSpec((size, 128), lambda h, r: (r, h)),
            whole,
            whole,
            pl.BlockSpec((width, 384), lambda h, r: (0, h)),
        ],
        out_shape=[
            jax.ShapeDtypeStruct((rows, pairs * 128), bf16),
            jax.ShapeDtypeStruct((keys, pairs * 128), bf16),
            jax.ShapeDtypeStruct((keys, pairs * 128), bf16),
            jax.ShapeDtypeStruct((width, pairs * 384), bf16),
        ],
        scratch_shapes=[
            pltpu.VMEM((2, 256, wide), bf16),
            pltpu.VMEM((2, 256, wide), bf16),
            pltpu.VMEM((128, wide), f32),
            pltpu.VMEM((128, wide), f32),
            pltpu.VMEM((rows, 128), bf16),
        ],
        compiler_params=pltpu.CompilerParams(vmem_limit_bytes=VMEM),
        cost_estimate=pl.CostEstimate(
            flops=20 * pairs * rows * keys * 200, transcendentals=2 * pairs * rows * keys, bytes_accessed=rows * 768 * 20
        ),
        name="attend_back",
    )(mixed, grad_att, att, aq, keys_values, keys_values, act, act_keys, kaug_t)


def norm_stats(value):
    average = jnp.mean(value, axis=-1, keepdims=True)
    centered = value - average
    variance = jnp.mean(centered * centered, axis=-1, keepdims=True)
    scale = lax.rsqrt(variance + epsilon)
    return centered * scale, scale


def norm_back(unit, scale, gain, grad):
    inner = grad * gain
    along = jnp.mean(inner * unit, axis=-1, keepdims=True)
    return scale * (inner - jnp.mean(inner, axis=-1, keepdims=True) - unit * along)


def gelu_pair(value):
    size = jnp.abs(value)
    bell = jnp.exp2(value * value * (-0.5 * LOG2E))
    base = 1.0 + 0.231641888 * size
    t = pl.reciprocal(base, approx=True)
    t = t * (2.0 - base * t)
    fit = t * (0.127414796 + t * (-0.142248368 + t * (0.7107068705 + t * (-0.7265760135 + t * 0.5307027145))))
    tail = fit * bell
    share = jnp.where(value >= 0.0, 1.0 - tail, tail)
    return value * share, share + value * (bell * 0.3989422804014327)


def column_sums(grad):
    return jnp.sum(grad, axis=0, keepdims=True)


def project_kernel(place, x, vec, weight, *refs):
    mixed, act_out, x_out = refs[-3:]
    width = vec.shape[1]
    rows = x[0]
    x_out[...] = rows
    unit, _ = norm_stats(rows.astype(f32))
    act = (unit * vec[0:1] + vec[1:2]).astype(bf16)
    act_out[...] = act
    total = dot(act, weight[...])
    mixed[:, :width] = ((total[:, :width] + vec[8:9]) * (HEAD ** (-0.5) * LOG2E)).astype(bf16)
    mixed[:, width : 2 * width] = total[:, width : 2 * width].astype(bf16)
    mixed[:, 2 * width :] = (total[:, 2 * width :] + vec[9:10]).astype(bf16)


def fixed(array):
    return pl.BlockSpec(array.shape, lambda i: (0,) * array.ndim, pipeline_mode=pl.Buffered(1))


def project(start, total, x, place, vec, weight, held=()):
    _, count, width = x.shape
    cols = weight.shape[1]
    sizes = (cols, width, width)
    tile = tile_of(count, 256)

    def one(array):
        return pl.BlockSpec(array.shape, lambda i, at: (0, 0), pipeline_mode=pl.Buffered(1))

    return pl.pallas_call(
        project_kernel,
        grid_spec=pltpu.PrefetchScalarGridSpec(
            num_scalar_prefetch=1,
            grid=(count // tile,),
            in_specs=[pl.BlockSpec((1, tile, width), lambda i, at: (at[0], i, 0)), one(vec), one(weight)]
            + [pl.BlockSpec(memory_space=pl.ANY) for _ in held],
            out_specs=[pl.BlockSpec((tile, size), lambda i, at: (start // tile + i, 0)) for size in sizes],
        ),
        out_shape=[jax.ShapeDtypeStruct((total, size), bf16) for size in sizes],
        input_output_aliases={4 + i: i for i in range(len(held))},
        compiler_params=pltpu.CompilerParams(vmem_limit_bytes=VMEM),
        name="project",
    )(place.reshape(1), x, vec, weight, *held)


def middle_kernel(
    x, att, aux, vec, wo, w1, w2, m1, m2, cot, grad_att, grad_low, weight_grads, sums, pooled_out,
    hidden, slope, acc1, acc2, acco, pooled, map2g, stage, sems,
):
    step = pl.program_id(0)
    rows, width = x.shape
    wide = w1.shape[1]
    part = wide // 4
    map_size = sums.shape[0] - 32
    bias_o, gain2, bias2, bias_2, gain3, bias3 = [vec[n : n + 1] for n in range(2, 8)]

    @pl.when(step == 0)
    def _():
        for ref in (sums, pooled, map2g, acc1, acc2, acco):
            ref[...] = jnp.zeros_like(ref)

    att_low = att[...]
    resid1 = x[...].astype(f32) + dot(att_low, wo[...]) + bias_o
    unit2, scale2 = norm_stats(resid1)
    act2 = (unit2 * gain2 + bias2).astype(bf16)
    total = None
    for c in range(4):
        cols = slice(c * part, (c + 1) * part)
        value, rate = gelu_pair(dot(act2, w1[:, cols]) + vec[10 + c : 11 + c])
        value = value.astype(bf16)
        hidden[:, cols] = value
        slope[:, cols] = rate.astype(bf16)
        more = dot(value, w2[cols, :])
        total = more if total is None else total + more
    resid2 = resid1 + total + bias_2
    output_low = resid2.astype(bf16)
    grad_gate = dot(output_low, cot[...], NT)
    unit3, scale3 = norm_stats(resid2)
    act3 = (unit3 * gain3 + bias3).astype(bf16)
    map_hidden, map_slope = gelu_pair(dot(act3, m1[...]) + aux[4:5])
    map_hidden = map_hidden.astype(bf16)
    logits = dot(map_hidden, m2[...]) + aux[3:4]
    lanes = logits.shape[1]
    lane = lax.broadcasted_iota(jnp.int32, (rows, lanes), 1)
    row = lax.broadcasted_iota(jnp.int32, (rows, lanes), 0) + step * rows
    slot = row - (lane >> 3) * PATCH
    mask = (slot >= 0) & (slot.astype(f32) < aux[0:1])
    inverse = aux[1:2]
    raw = 1.0 / (1.0 + jnp.exp2(logits * (-LOG2E)))
    gates = jnp.where(mask, raw, 0.0)
    gates_low = gates.astype(bf16)
    pooled[...] += dot(gates_low.T, output_low)
    gate_sum = jnp.sum(gates, axis=1, keepdims=True)
    inverse_row = inverse[:, 0:1]
    sums[6:7, 256:384] += column_sums(gates * (gate_sum - gates)) * (inverse * inverse)

    grad_out = dot(gates_low, cot[...]) * inverse_row
    grad_gate = grad_gate * inverse + aux[2:3] * (gate_sum - gates)
    grad_logit = jnp.where(mask, grad_gate * raw * (1.0 - raw), 0.0)
    sums[6:7, 128:256] += column_sums(grad_logit)
    grad_logit = grad_logit.astype(bf16)
    map2g[...] += dot(map_hidden.T, grad_logit)
    grad_mpre = dot(grad_logit, m2[...], NT) * map_slope
    sums[6:7, 0:128] += column_sums(grad_mpre)
    grad_mpre = grad_mpre.astype(bf16)
    sums[16 : 16 + map_size] += dot(grad_mpre.T[:map_size], act3)
    grad_act = dot(grad_mpre, m1[...], NT)
    sums[4:5] += column_sums(grad_act * unit3)
    sums[5:6] += column_sums(grad_act)
    grad_res2 = norm_back(unit3, scale3, gain3, grad_act) + grad_out

    sums[3:4] += column_sums(grad_res2)
    g2 = grad_res2.astype(bf16)
    g2_t = g2.T
    act2_t = act2.T
    grad_act = None
    for c in range(4):
        cols = slice(c * part, (c + 1) * part)
        grad_pre = dot(g2, w2[cols, :], NT) * slope[:, cols].astype(f32)
        sums[8 + c : 9 + c] += column_sums(grad_pre)
        grad_pre = grad_pre.astype(bf16)
        slope[:, cols] = grad_pre
        more = dot(grad_pre, w1[:, cols], NT)
        grad_act = more if grad_act is None else grad_act + more
    for c in range(4):
        cols = slice(c * part, (c + 1) * part)
        acc1[:, cols] += dot(act2_t, slope[:, cols])
        acc2[:, cols] += dot(g2_t, hidden[:, cols])
    sums[1:2] += column_sums(grad_act * unit2)
    sums[2:3] += column_sums(grad_act)
    grad_res1 = norm_back(unit2, scale2, gain2, grad_act) + grad_res2

    sums[0:1] += column_sums(grad_res1)
    g1 = grad_res1.astype(bf16)
    grad_low[...] = g1
    acco[...] += dot(att_low.T, g1)
    grad_att[...] = dot(g1, wo[...], NT).astype(bf16)

    @pl.when(step == pl.num_programs(0) - 1)
    def _():
        groups, seqs, _, share, thin = weight_grads.shape
        pending = [[], []]
        count = 0

        def drain(value, *targets):
            nonlocal count
            slot = count % 2
            count += 1
            for copy in pending[slot]:
                copy.wait()
            stage[slot] = value.astype(bf16).reshape(stage.shape[1:])
            pending[slot] = [
                pltpu.make_async_copy(stage.at[slot, lo:hi], target, sems.at[slot, n])
                for n, (lo, hi, target) in enumerate(targets)
            ]
            for copy in pending[slot]:
                copy.start()

        for t in range(4 * seqs):
            drain(acc1[:, t * thin : (t + 1) * thin], (0, groups, weight_grads.at[:, t // 4, t % 4]))
        for c in range(4):
            cols = slice(c * part, (c + 1) * part)
            for s in range(seqs):
                value = acc2[s * thin : (s + 1) * thin, cols].T
                if groups == 1:
                    drain(value, (0, 1, weight_grads.at[:, s, 4 + c]))
                else:
                    few = groups // 4
                    drain(value, *[(4 * i, 4 * i + 4, weight_grads.at[c * few + i, s, 4:8]) for i in range(few)])
        for s in range(seqs):
            drain(acco[:, s * thin : (s + 1) * thin], (0, groups, weight_grads.at[:, s, 8]))
        pooled_out[...] = (pooled[...] * inverse_row).astype(bf16)
        for g in range(map_size // 16):
            sums[16 + map_size :, g * 128 : (g + 1) * 128] = map2g[g * 16 : (g + 1) * 16]
        for copy in pending[0] + pending[1]:
            copy.wait()


def middle(groups, seqs, map_size, x, att, *others):
    rows, width = x.shape
    wide = others[3].shape[1]
    lanes = others[0].shape[1]
    if width // groups % 16 or groups % 4 or width // seqs % 128:
        groups, seqs = 1, 1
    stage = (2, groups, width // groups, width // seqs)
    size = tile_of(rows, MIDDLE)
    tile = pl.BlockSpec((size, width), lambda i: (i, 0))
    anywhere = pl.BlockSpec(memory_space=pl.ANY)
    summed = [jax.ShapeDtypeStruct((map_size + 32, width), f32), jax.ShapeDtypeStruct((lanes, width), bf16)]
    return pl.pallas_call(
        middle_kernel,
        grid=(rows // size,),
        in_specs=[tile, tile] + [fixed(o) for o in others],
        out_specs=[tile, tile, anywhere] + [pl.BlockSpec(s.shape, lambda i: (0, 0)) for s in summed],
        out_shape=[
            jax.ShapeDtypeStruct((rows, width), bf16),
            jax.ShapeDtypeStruct((rows, width), bf16),
            jax.ShapeDtypeStruct((groups, seqs, 9, width // groups, width // seqs), bf16),
        ]
        + summed,
        scratch_shapes=[
            pltpu.VMEM((size, wide), bf16),
            pltpu.VMEM((size, wide), bf16),
            pltpu.VMEM((width, wide), f32),
            pltpu.VMEM((width, wide), f32),
            pltpu.VMEM((width, width), f32),
            pltpu.VMEM((lanes, width), f32),
            pltpu.VMEM((lanes, lanes), f32),
            pltpu.VMEM(stage, bf16),
            pltpu.SemaphoreType.DMA((2, max(1, groups // 4))),
        ],
        compiler_params=pltpu.CompilerParams(vmem_limit_bytes=VMEM),
        cost_estimate=pl.CostEstimate(
            flops=2 * rows * width * (6 * wide + 3 * width), transcendentals=rows * wide, bytes_accessed=rows * width * 12
        ),
        name="middle",
    )(x, att, *others)


def finish_kernel(place, x, g1, vec, weight, *refs):
    grads, (grad_in, sums) = refs[:-2], refs[-2:]
    parts = len(grads) // 3
    width = x.shape[1]

    @pl.when(pl.program_id(0) == 0)
    def _():
        sums[...] = jnp.zeros_like(sums)

    unit, scale = norm_stats(x[...].astype(f32))
    grad_act = None
    for i in range(3):
        at = 0
        for n in range(parts):
            part = grads[3 * n + i][...]
            share = part.shape[1]
            if i != 1:
                sums[2 + i // 2 : 3 + i // 2, at : at + share] += column_sums(part.astype(f32))
            more = dot(part, weight[:, i * width + at : i * width + at + share], NT)
            grad_act = more if grad_act is None else grad_act + more
            at += share
    sums[0:1] += column_sums(grad_act * unit)
    sums[1:2] += column_sums(grad_act)
    total = norm_back(unit, scale, vec[0:1], grad_act) + g1[...].astype(f32)
    grad_in[...] = total.astype(grad_in.dtype).reshape(grad_in.shape)


def finish(start, count, x, g1, vec, weight, grads, place=None, places=0):
    width = x.shape[1]
    size = tile_of(count, 256)
    begin = start // size
    tile = pl.BlockSpec((size, width), lambda i, at: (begin + i, 0))
    thin = [pl.BlockSpec((size, grad.shape[1]), lambda i, at: (begin + i, 0)) for grad in grads]
    if place is None:
        place = jnp.int32(0)
        out = (pl.BlockSpec((size, width), lambda i, at: (i, 0)), jax.ShapeDtypeStruct((count, width), bf16))
    else:
        out = (
            pl.BlockSpec((1, size, width), lambda i, at: (at[0], i, 0)),
            jax.ShapeDtypeStruct((places, count, width), f32),
        )

    def one(array):
        return pl.BlockSpec(array.shape, lambda i, at: (0, 0), pipeline_mode=pl.Buffered(1))

    return pl.pallas_call(
        finish_kernel,
        grid_spec=pltpu.PrefetchScalarGridSpec(
            num_scalar_prefetch=1,
            grid=(count // size,),
            in_specs=[tile] * 2 + [one(o) for o in (vec, weight)] + thin,
            out_specs=[out[0], pl.BlockSpec((8, width), lambda i, at: (0, 0))],
        ),
        out_shape=[out[1], jax.ShapeDtypeStruct((8, width), f32)],
        compiler_params=pltpu.CompilerParams(vmem_limit_bytes=VMEM),
        cost_estimate=pl.CostEstimate(
            flops=2 * count * width * weight.shape[1] * 2, transcendentals=0, bytes_accessed=count * width * 10
        ),
        name="finish",
    )(place.reshape(1), x, g1, vec, weight, *grads)


def shards(
    inputs,
    frame_tokens,
    clip_frames,
    norm1_gain,
    norm1_bias,
    qkv_weight,
    query_bias,
    value_bias,
    out_weight,
    out_bias,
    norm2_gain,
    norm2_bias,
    fc1_weight,
    fc1_bias,
    fc2_weight,
    fc2_bias,
    learn_gain,
    learn_bias,
    map1_weight,
    map1_bias,
    map2_weight,
    map2_bias,
    cot_pooled,
):
    clip_count, piece, width = inputs.shape
    seq_size = lax.axis_size("seq")
    position = lax.axis_index("seq")
    clip_size = lax.axis_size("clip")
    frames_here = piece // PATCH
    scaling = HEAD ** (-0.5)
    slots_all = float(clip_count * clip_size * seq_size * frames_here)
    group = seq_size // clip_count
    mine = position // group
    seat = position % group

    def route(turn):
        return [
            (s, ((s % clip_count + turn) % clip_count) * group + s // clip_count) for s in range(seq_size)
        ]

    def send(value, turn, back=False):
        pairs = route(turn)
        if back:
            pairs = [(b, a) for a, b in pairs]
        if all(a == b for a, b in pairs):
            return value
        return lax.ppermute(value, "seq", pairs)

    def scatter(whole, first=0):
        return [
            send(lax.dynamic_index_in_dim(whole, (position + turn) % clip_count, 0, False), turn)
            for turn in range(first, clip_count)
        ]

    def gather_back(parts, kind, whole=None):
        if whole is None:
            whole = jnp.zeros((clip_count,) + parts[0].shape, kind)
        for turn, part in enumerate(parts):
            if part is not None:
                home = send(part, turn, True).astype(kind)
                whole = lax.dynamic_update_index_in_dim(whole, home, (position + turn) % clip_count, 0)
        return whole

    tokens = lax.dynamic_index_in_dim(frame_tokens, mine, 0, False)
    frames = lax.dynamic_index_in_dim(clip_frames, mine, 0, False)
    rows = clip_count * piece
    keys = group * rows
    split = piece % 16 == 0 and group == 1 and clip_count == 2
    near = piece // TILE * TILE
    cot = jnp.concatenate(scatter(cot_pooled), axis=0).reshape(clip_count * frames_here * NTOK, width)

    def placed(ids, at_seat):
        turn = ids // piece
        source = clip_count * at_seat + (mine - turn) % clip_count
        local = ids - turn * piece
        frame = local // PATCH
        slot = local - frame * PATCH
        return (source * frames_here + frame < frames) & (slot < tokens)

    key_ids = jnp.arange(keys, dtype=jnp.int32)
    key_inside = placed(key_ids % rows, key_ids // rows)
    lane16 = jnp.arange(HEAD)
    key_mask = jnp.where(key_inside, 0.0, masked_score)
    kaug = jnp.where(lane16[None, :] < 3, 1.0, jnp.where(lane16[None, :] == 3, key_mask[:, None], 0.0)).astype(bf16)
    kaug = jnp.concatenate([kaug, jnp.zeros_like(kaug)], axis=1)
    sub16 = jnp.arange(16)[:, None]
    wide_mask = jnp.pad(key_mask, (0, up(keys, TILE) - keys), constant_values=masked_score)
    kaug_t = jnp.where(sub16 < 3, 1.0, jnp.where(sub16 == 3, wide_mask[None, :], 0.0)).astype(bf16)

    vec = jnp.concatenate(
        [
            norm1_gain,
            norm1_bias,
            out_bias,
            norm2_gain,
            norm2_bias,
            fc2_bias,
            learn_gain,
            learn_bias,
            query_bias,
            value_bias,
            fc1_bias,
        ]
    ).reshape(-1, width)
    begun = ()
    if split:
        (x_far,) = scatter(inputs, 1)
        held = project(0, rows, inputs, position % clip_count, vec, qkv_weight)
        held, begun = lax.optimization_barrier((held, (attend_near(near, held[0], kaug),)))
        mixed, act1, x_low = project(piece, rows, x_far[None], jnp.int32(0), vec, qkv_weight, held)
    else:
        x_all = jnp.concatenate(scatter(inputs), axis=0)[None]
        mixed, act1, x_low = project(0, rows, x_all, jnp.int32(0), vec, qkv_weight)
    if group == 1:
        keys_values, act_keys = mixed, act1
    else:
        both = lax.all_gather(mixed[:, width:], "seq", axis=0, tiled=True)
        keys_values = lax.dynamic_slice_in_dim(both, mine * keys, keys, 0)
        act_keys = lax.all_gather(act1, "seq", axis=0, tiled=True)
        act_keys = lax.dynamic_slice_in_dim(act_keys, mine * keys, keys, 0)
    att, aq = attend(mixed, keys_values, kaug, *begun)

    slots = clip_count * frames_here * NTOK
    lanes = -(-slots // 128) * 128
    pair_count = NTOK * (NTOK - 1)
    lane_ids = jnp.arange(lanes)
    lane_turn = lane_ids // (frames_here * NTOK)
    lane_frame = lane_ids // NTOK - lane_turn * frames_here
    lane_source = clip_count * seat + (mine - lane_turn) % clip_count
    lane_open = (lane_source * frames_here + lane_frame < frames) & (lane_ids < slots)
    inverse = lax.rsqrt(tokens.astype(f32))
    factor = 2.0 / pair_count * inverse * inverse / slots_all
    map_size = map1_bias.shape[0]
    aux = jnp.stack(
        [
            jnp.where(lane_open, tokens, 0).astype(f32),
            jnp.full((lanes,), inverse),
            jnp.full((lanes,), factor),
            jnp.tile(map2_bias, lanes // NTOK),
            jnp.pad(map1_bias, (0, lanes - map_size)),
        ]
        + [jnp.zeros((lanes,), f32)] * 3
    )
    map1_wide = jnp.pad(map1_weight, ((0, 0), (0, lanes - map_size)))
    map2_wide = jnp.pad(jnp.tile(map2_weight, (1, lanes // NTOK)), ((0, lanes - map_size), (0, 0)))
    cot = jnp.pad(cot, ((0, lanes - slots), (0, 0)))
    grad_att, grad_low, weight_part, early, pooled = middle(
        clip_size,
        seq_size,
        map_size,
        x_low,
        att,
        aux,
        vec,
        out_weight,
        fc1_weight,
        fc2_weight,
        map1_wide,
        map2_wide,
        cot,
    )

    def over_clip(matrix):
        return lax.psum_scatter(matrix, "clip", scatter_dimension=0, tiled=True)

    def bits(size):
        return [1 << n for n in range(size.bit_length() - 1)]

    clip_steps = [("clip", bit) for bit in bits(clip_size)]
    seq_steps = [("seq", bit) for bit in bits(seq_size)]
    early_steps = clip_steps[:1] + seq_steps + clip_steps[1:]

    def meet(value, step):
        axis, bit = step
        return lax.ppermute(value, axis, [(i, i ^ bit) for i in range(lax.axis_size(axis))])

    def part_ways(blocks, step):
        axis, bit = step
        halves = blocks.reshape((-1, 2) + blocks.shape[1:])
        side = (lax.axis_index(axis) // bit) % 2
        away = lax.dynamic_index_in_dim(halves, 1 - side, 1, False)
        return lax.dynamic_index_in_dim(halves, side, 1, False), meet(away, step)

    def add_low(kept, received):
        return (kept.astype(f32) + received.astype(f32)).astype(bf16)

    def back(start, pairs, source):
        return attend_back(
            start, pairs, source, keys_values if group > 1 else source, grad_att, att, aq, act1, act_keys, kaug_t
        )

    tie = lax.optimization_barrier
    pairs = (4, 2)
    share = width // clip_size
    thin = width // seq_size
    if weight_part.shape[0] == 1:
        fc1_part = weight_part[0, 0, :4].transpose(1, 0, 2).reshape(clip_size, share, seq_size, 4, thin)
        fc2_part = weight_part[0, 0, 4:8].reshape(clip_size, 4, share, seq_size, thin).transpose(0, 3, 1, 2, 4)
        out_part = weight_part[0, 0, 8].reshape(clip_size, 1, share, seq_size, thin).transpose(0, 3, 1, 2, 4)
        weight_part = jnp.concatenate([fc1_part.transpose(0, 2, 3, 1, 4), fc2_part, out_part], axis=2)
    slab = over_clip(weight_part)[0]
    near_early = meet(early, early_steps[0])
    back0 = back(0, pairs[0], mixed)
    mixed, slab, early, near_early, back0 = tie((mixed, slab, early, near_early, back0))
    early = early + near_early
    near_early = meet(early, early_steps[1])
    slab = lax.psum_scatter(slab, "seq", scatter_dimension=0, tiled=False)
    slab0 = over_clip(back0[3])
    back1 = back(pairs[0], pairs[1], mixed)
    slab, slab0, early, near_early, back1 = tie((slab, slab0, early, near_early, back1))
    early = early + near_early
    pooled = pooled[:slots].reshape(clip_count, frames_here, NTOK, width)
    pooled = gather_back([pooled[t] for t in range(clip_count)], bf16)

    grads = [list(one[:3]) for one in (back0, back1)]
    if group > 1:
        both = jnp.zeros((seq_size * rows, 2 * width), bf16)
        both = lax.dynamic_update_slice_in_dim(
            both, jnp.concatenate([one[i] for i in (1, 2) for one in grads], axis=1), mine * keys, 0
        )
        both = lax.psum_scatter(both, "seq", scatter_dimension=0, tiled=True)
        at = 0
        for i in (1, 2):
            for n in range(2):
                grads[n][i] = both[:, at : at + pairs[n] * 128]
                at += pairs[n] * 128
    grads = [grad for one in grads for grad in one]
    rest = (grad_low, vec, qkv_weight, grads)
    near_early = meet(early, early_steps[2])
    kept, received = part_ways(back1[3].reshape(clip_size, share, -1), clip_steps[0])
    if split:
        size = tile_of(piece, 256)
        lead = -(-piece // size // 2) * size
        far0, sums0 = finish(piece, lead, x_low, *rest)
        far0, sums0, x_low, near_early, received = tie((far0, sums0, x_low, near_early, received))
        home0 = send(far0, 1, True)
    early = early + near_early
    near_early = meet(early, early_steps[3])
    kept, received = part_ways(add_low(kept, received), clip_steps[1])
    if split:
        far1, sums1 = finish(piece + lead, piece - lead, x_low, *rest)
        far1, sums1, x_low, near_early, received = tie((far1, sums1, x_low, near_early, received))
        home1 = send(far1, 1, True)
    early = early + near_early
    near_early = meet(early, early_steps[4])
    kept, received = part_ways(add_low(kept, received), clip_steps[2])
    if split:
        input_grad, late = finish(0, piece, x_low, *rest, place=position % clip_count, places=clip_count)
        input_grad, late, near_early, received, home0 = tie((input_grad, late, near_early, received, home0))
        other = (position + 1) % clip_count
        input_grad = lax.dynamic_update_slice(input_grad, home0.astype(f32)[None], (other, 0, 0))
        late = late + sums0 + sums1
    else:
        local, late = finish(0, rows, x_low, *rest)
        input_grad = gather_back([local[t * piece : (t + 1) * piece] for t in range(clip_count)], f32)
    early = early + near_early
    for step in early_steps[5:]:
        early = early + meet(early, step)
    slab1 = add_low(kept, received)
    for step in clip_steps[3:]:
        slab1 = add_low(*part_ways(slab1, step))
    late = late[:4]
    for step in clip_steps:
        late = late + meet(late, step)
    late, slab1, slab, early = tie((late, slab1, slab, early))
    for step in seq_steps:
        late = late + meet(late, step)
    qkv = [
        part.reshape(share, count, 3, 128).transpose(0, 2, 1, 3) for part, count in zip((slab0, slab1), pairs)
    ]
    qkv = jnp.concatenate(qkv, axis=2).reshape(share, seq_size, -1).transpose(1, 0, 2)
    for step in seq_steps:
        qkv = add_low(*part_ways(qkv, step))
    qkv_grad = qkv[0].astype(f32)
    if split:
        input_grad = lax.dynamic_update_slice(input_grad, home1.astype(f32)[None], (other, lead, 0))
    fc1_grad = slab[:4].transpose(1, 0, 2).reshape(share, 4 * thin).astype(f32)
    fc2_grad = slab[4:8].reshape(4 * share, thin).astype(f32)
    out_grad = slab[8].astype(f32)

    small = early[6]
    map1_grad = early[16 : 16 + map_size].T
    map2_grad = early[16 + map_size :, : map_size // 16 * lanes].reshape(16, map_size // 16, lanes // NTOK, NTOK)
    map2_grad = jnp.sum(map2_grad, axis=2).transpose(1, 0, 2).reshape(map_size, NTOK)
    map2_bias_grad = jnp.sum(small[128:256].reshape(-1, NTOK), axis=0)
    penalty = jnp.sum(small[256:384]) / pair_count / slots_all
    return (
        pooled,
        penalty,
        input_grad,
        late[0],
        late[1],
        qkv_grad,
        late[2],
        late[3],
        out_grad,
        early[0],
        early[1],
        early[2],
        fc1_grad,
        early[8:12].reshape(-1),
        fc2_grad,
        early[3],
        early[4],
        early[5],
        map1_grad,
        small[:map_size],
        map2_grad,
        map2_bias_grad,
    )


def solution(mesh):
    row_spec = P("clip", "seq", None)
    pool_spec = P("clip", "seq", None, None)
    matrix_spec = P("clip", "seq")
    in_specs = (row_spec, P("clip"), P("clip")) + (P(),) * 19 + (pool_spec,)
    out_specs = (
        (pool_spec, P(), row_spec, P(), P(), matrix_spec, P(), P(), matrix_spec, P(), P(), P(), matrix_spec, P())
        + (matrix_spec,)
        + (P(),) * 7
    )
    return jax.shard_map(shards, mesh=mesh, in_specs=in_specs, out_specs=out_specs, check_vma=False)
```

```python
import jax
import jax.numpy as jnp
from jax import lax
from jax.experimental import pallas as pl
from jax.experimental.pallas import tpu as pltpu
from jax.sharding import PartitionSpec as P

HEADS = 12
HEAD = 64
NTOK = 8
PATCH = 196
TILE = 256
AHEAD = 0
MIDDLE = 448
LOG2E = 1.4426950408889634
LN2 = 0.6931471805599453
VMEM = 60 * 1024 * 1024

epsilon = 1e-06
masked_score = -1e30
bf16 = jnp.bfloat16
f32 = jnp.float32

NN = (((1,), (0,)), ((), ()))
NT = (((1,), (1,)), ((), ()))


def dot(left, right, dims=NN):
    return lax.dot_general(left, right, dims, preferred_element_type=f32)


def split3(value):
    hi = value.astype(bf16).astype(f32)
    mid = (value - hi).astype(bf16).astype(f32)
    return hi, mid, value - hi - mid


def up(count, unit):
    return -(-count // unit) * unit


def tile_of(count, most):
    return max(size for size in range(16, most + 1, 16) if count % size == 0)


def blocks_of(count, unit):
    return [(base, min(unit, count - base)) for base in range(0, count, unit)]


def flip(value):
    return jnp.concatenate([value[base : base + size].T for base, size in blocks_of(value.shape[0], 128)], axis=1)


def spread_heads(source, held, aug):
    count = source.shape[0]
    zero = jnp.zeros((HEAD, held.shape[2]), bf16)
    for j in range(2):
        other = (1 - j) * HEAD
        held[j, other : other + HEAD] = zero
        if held.shape[2] > count:
            edge = count // 128 * 128
            held[j, j * HEAD : (j + 1) * HEAD, edge:] = jnp.zeros((HEAD, held.shape[2] - edge), bf16)
        held[j, 128:256] = aug(j)
    for base, size in blocks_of(count, 256):
        flat = flip(source[base : base + size])
        for j in range(2):
            held[j, j * HEAD : (j + 1) * HEAD, base : base + size] = flat[j * HEAD : (j + 1) * HEAD]


def spread_queries(q, qp):
    ids = lax.broadcasted_iota(jnp.int32, (128, qp.shape[2]), 0)
    spread_heads(q, qp, lambda j: jnp.where(ids == 3, 1.0, 0.0).astype(bf16))


def flip_into(source, target):
    for base, size in blocks_of(source.shape[0], 256):
        target[:, base : base + size] = flip(source[base : base + size])


def key_block(k, kaug, base, size):
    return jnp.concatenate([k[pl.ds(base, size), :], kaug[pl.ds(base, size), :]], axis=1)


def value_block(vt, j, base, size):
    ones = jnp.ones((16, size), bf16)
    return jnp.concatenate([vt[j * HEAD : (j + 1) * HEAD, pl.ds(base, size)], ones], axis=0)


def over_tiles(step, begin, count):
    @pl.loop(begin // TILE, count // TILE, unroll=3)
    def _(t):
        step(pl.multiple_of(t * TILE, TILE), TILE)

    if count % TILE:
        step(count // TILE * TILE, count % TILE)


def fold_tile(k, kaug, qp, vt, acc, low, fresh, base, size):
    for j in range(2):
        p = jnp.exp2(dot(key_block(k, kaug, base, size), qp[j, :, low:])).astype(bf16)
        part = dot(value_block(vt, j, base, size), p)
        if fresh:
            acc[j, :, low:] = part
        else:
            acc[j, :, low:] += part


def attend_near_kernel(q, k, v, kaug, acc, qp, vt):
    spread_queries(q, qp)
    flip_into(v, vt)
    fold_tile(k, kaug, qp, vt, acc, 0, True, 0, TILE)
    over_tiles(lambda base, size: fold_tile(k, kaug, qp, vt, acc, 0, False, base, size), TILE, k.shape[0])


def attend_near(near, mixed, kaug):
    pairs = HEADS // 2
    return pl.pallas_call(
        attend_near_kernel,
        grid=(pairs,),
        in_specs=[
            pl.BlockSpec((near, 128), lambda h: (0, h)),
            pl.BlockSpec((near, 128), lambda h: (0, pairs + h)),
            pl.BlockSpec((near, 128), lambda h: (0, 2 * pairs + h)),
            pl.BlockSpec((near, 128), lambda h: (0, 0)),
        ],
        out_specs=pl.BlockSpec((2, HEAD + 16, near), lambda h: (h, 0, 0)),
        out_shape=jax.ShapeDtypeStruct((HEADS, HEAD + 16, near), f32),
        scratch_shapes=[pltpu.VMEM((2, 256, near), bf16), pltpu.VMEM((128, near), bf16)],
        compiler_params=pltpu.CompilerParams(vmem_limit_bytes=VMEM),
        cost_estimate=pl.CostEstimate(
            flops=4 * HEADS * near * near * 256, transcendentals=HEADS * near * near, bytes_accessed=near * 768 * 10
        ),
        name="attend_near",
    )(mixed, mixed, mixed, kaug)


def attend_kernel(q, k, v, kaug, *refs):
    att, aq, qp, vt, acc = refs[-5:]
    rows = q.shape[0]
    keys = k.shape[0]
    wide = qp.shape[2]
    spread_queries(q, qp)
    flip_into(v, vt)

    def fold(low, fresh):
        return lambda base, size: fold_tile(k, kaug, qp, vt, acc, low, fresh, base, size)

    begun = 0
    if len(refs) > 5:
        begun = refs[0].shape[2]
        acc[:, :, :begun] = refs[0][...]
    fold(begun, True)(0, TILE)
    if begun:
        over_tiles(fold(begun, False), TILE, begun)
    over_tiles(fold(0, False), max(begun, TILE), keys)

    for j in range(2):
        total = acc[j, HEAD : HEAD + 1]
        fine = (total > 2.0**-60) & (total < 2.0**60)
        bad = jnp.max(jnp.where(fine, 0.0, 1.0)) > 0.5
        acc[j, HEAD + 8 : HEAD + 9] = jnp.zeros((1, wide), f32)

        @pl.when(bad)
        def _():
            acc[j, 0:1] = jnp.full((1, wide), -1e38, f32)

            def largest(base, size):
                s = dot(key_block(k, kaug, base, size), qp[j])
                acc[j, 0:1] = jnp.maximum(acc[j, 0:1], jnp.max(s, axis=0, keepdims=True))

            over_tiles(largest, 0, keys)
            best = acc[j, 0:1]
            acc[j] = jnp.zeros((HEAD + 16, wide), f32)

            def again(base, size):
                p = jnp.exp2(dot(key_block(k, kaug, base, size), qp[j]) - best).astype(bf16)
                acc[j] += dot(value_block(vt, j, base, size), p)

            over_tiles(again, 0, keys)
            acc[j, HEAD + 8 : HEAD + 9] = best

    ids = lax.broadcasted_iota(jnp.int32, (HEAD, 128), 0)
    for base, size in blocks_of(rows, 128):
        here = slice(base, base + 128)
        outs = []
        augs = []
        for j in range(2):
            total = acc[j, HEAD : HEAD + 1, here]
            outs.append(acc[j, 0:HEAD, here] * (1.0 / total))
            lse = jnp.log2(total) + acc[j, HEAD + 8 : HEAD + 9, here]
            hi, mid, low = split3(-lse)
            aug = jnp.where(ids == 0, hi, jnp.where(ids == 1, mid, jnp.where(ids == 2, low, 0.0)))
            augs.append(jnp.where(ids == 3, 1.0, aug))
        att[base : base + size, :] = jnp.concatenate(outs, axis=0).T[:size].astype(bf16)
        aq[base : base + size, :] = jnp.concatenate(augs, axis=0).T[:size].astype(bf16)


def attend(mixed, keys_values, kaug, *begun):
    rows = mixed.shape[0]
    keys = keys_values.shape[0]
    pairs = HEADS // 2
    wide = up(rows, 128)
    first = keys_values.shape[1] // 128 - 2 * pairs
    return pl.pallas_call(
        attend_kernel,
        grid=(pairs,),
        in_specs=[
            pl.BlockSpec((rows, 128), lambda h: (0, h)),
            pl.BlockSpec((keys, 128), lambda h: (0, first + h)),
            pl.BlockSpec((keys, 128), lambda h: (0, first + pairs + h)),
            pl.BlockSpec((keys, 128), lambda h: (0, 0)),
        ]
        + [pl.BlockSpec((2,) + one.shape[1:], lambda h: (h, 0, 0)) for one in begun],
        out_specs=[
            pl.BlockSpec((rows, 128), lambda h: (0, h)),
            pl.BlockSpec((rows, 128), lambda h: (0, h)),
        ],
        out_shape=[
            jax.ShapeDtypeStruct((rows, HEADS * HEAD), bf16),
            jax.ShapeDtypeStruct((rows, HEADS * HEAD), bf16),
        ],
        scratch_shapes=[
            pltpu.VMEM((2, 256, wide), bf16),
            pltpu.VMEM((128, up(keys, 128)), bf16),
            pltpu.VMEM((2, HEAD + 16, wide), f32),
        ],
        compiler_params=pltpu.CompilerParams(vmem_limit_bytes=VMEM),
        cost_estimate=pl.CostEstimate(
            flops=4 * HEADS * rows * keys * 256, transcendentals=HEADS * rows * keys, bytes_accessed=rows * 768 * 10
        ),
        name="attend",
    )(mixed, keys_values, keys_values, kaug, *begun)


def attend_back_kernel(q, do, att, aq, k, v, act_rows, act_keys, kaug_t, dq, dk, dv, weight_grad, kp, vp, dkt, dvt, dqs):
    step = pl.program_id(1)
    rows = q.shape[0]
    keys = k.shape[0]
    tiles = up(keys, TILE) // TILE

    @pl.when(step == 0)
    def _():
        rest = jnp.zeros((HEAD - 16, kp.shape[2]), bf16)
        zero = jnp.zeros((HEAD, kp.shape[2]), bf16)
        halves = (jnp.concatenate([kaug_t[...], rest, zero], axis=0), jnp.concatenate([zero, kaug_t[...], rest], axis=0))
        for source, held in ((k, kp), (v, vp)):
            spread_heads(source, held, lambda j: halves[j])
        dkt[...] = jnp.zeros_like(dkt)
        dvt[...] = jnp.zeros_like(dvt)

    units = [(j, t) for j in range(2) for t in range(tiles)]
    count = len(units)
    totals = [None, None]
    qa = jnp.concatenate([q[...], aq[...]], axis=1)

    def cols(t):
        return slice(t * TILE, (t + 1) * TILE)

    def scores(i):
        j, t = units[i]
        return dot(qa, kp[j, :, cols(t)])

    def weigh(s, dp):
        p = jnp.exp2(s)
        return p.astype(bf16), (p * dp).astype(bf16)

    def collect(j, t, p, ds):
        part = slice(j * HEAD, (j + 1) * HEAD)
        dvt[part, cols(t)] += dot(dot_[part], p)
        dkt[part, cols(t)] += dot(qt[part], ds)
        more = dot(ds[:, : min(TILE, keys - t * TILE)], k[t * TILE : min(keys, (t + 1) * TILE), :])
        totals[j] = more if totals[j] is None else totals[j] + more

    ahead = AHEAD
    raw = {i: scores(i) for i in range(min(ahead, count))}
    lane = lax.broadcasted_iota(jnp.int32, (rows, 128), 1)
    product = do[...].astype(f32) * att[...].astype(f32)
    inner0 = jnp.sum(jnp.where(lane < HEAD, product, 0.0), axis=1, keepdims=True)
    inner1 = jnp.sum(jnp.where(lane < HEAD, 0.0, product), axis=1, keepdims=True)
    hi, mid, low = split3(-jnp.where(lane < HEAD, inner0, inner1))
    within = lane % HEAD
    ado = jnp.where(within == 0, hi, jnp.where(within == 1, mid, jnp.where(within == 2, low, 0.0))).astype(bf16)
    da = jnp.concatenate([do[...], ado], axis=1)
    ready = {}
    for i in range(count + 2):
        if i < count:
            j, t = units[i]
            s = raw.pop(i) if i in raw else scores(i)
            raw[i] = (s, dot(da, vp[j, :, cols(t)]))
        if i == 1:
            qt = flip(q[...])
            dot_ = flip(do[...])
        if 0 <= i - 1 < count:
            ready[i - 1] = weigh(*raw.pop(i - 1))
        if 0 <= i - 2 < count:
            collect(*units[i - 2], *ready.pop(i - 2))
    grad_q = (jnp.where(lane < HEAD, totals[0], totals[1]) * HEAD ** (-0.5)).astype(bf16)
    dq[...] = grad_q
    dqs[pl.ds(pl.multiple_of(step * rows, 16), rows), :] = grad_q

    @pl.when(step == pl.num_programs(1) - 1)
    def _():
        total = jnp.zeros((128, act_rows.shape[1]), f32)
        for base, size in blocks_of(dqs.shape[0], TILE):
            total += dot(flip(dqs[base : base + size]), act_rows[base : base + size])
        weight_grad[:, 0:128] = total.T.astype(bf16)
        total = jnp.zeros((256, act_rows.shape[1]), f32)
        for base, size in blocks_of(keys, TILE):
            grad_k = (dkt[:, base : base + size] * LN2).astype(bf16)
            grad_v = dvt[:, base : base + size].astype(bf16)
            dk[base : base + size] = grad_k.T
            dv[base : base + size] = grad_v.T
            total += dot(jnp.concatenate([grad_k, grad_v], axis=0), act_keys[base : base + size])
        weight_grad[:, 128:384] = total.T.astype(bf16)


def attend_back(start, pairs, mixed, keys_values, grad_att, att, aq, act, act_keys, kaug_t):
    rows, width = act.shape
    keys = keys_values.shape[0]
    wide = up(keys, TILE)
    size = tile_of(rows, 512)
    first = keys_values.shape[1] // 128 - HEADS
    here = pl.BlockSpec((size, 128), lambda h, r: (r, start + h))
    whole = pl.BlockSpec((keys, 128), lambda h, r: (0, h))
    return pl.pallas_call(
        attend_back_kernel,
        grid=(pairs, rows // size),
        in_specs=[
            here,
            here,
            here,
            here,
            pl.BlockSpec((keys, 128), lambda h, r: (0, first + start + h)),
            pl.BlockSpec((keys, 128), lambda h, r: (0, first + HEADS // 2 + start + h)),
            pl.BlockSpec((rows, width), lambda h, r: (0, 0), pipeline_mode=pl.Buffered(1)),
            pl.BlockSpec((keys, width), lambda h, r: (0, 0), pipeline_mode=pl.Buffered(1)),
            pl.BlockSpec((16, wide), lambda h, r: (0, 0), pipeline_mode=pl.Buffered(1)),
        ],
        out_specs=[
            pl.BlockSpec((size, 128), lambda h, r: (r, h)),
            whole,
            whole,
            pl.BlockSpec((width, 384), lambda h, r: (0, h)),
        ],
        out_shape=[
            jax.ShapeDtypeStruct((rows, pairs * 128), bf16),
            jax.ShapeDtypeStruct((keys, pairs * 128), bf16),
            jax.ShapeDtypeStruct((keys, pairs * 128), bf16),
            jax.ShapeDtypeStruct((width, pairs * 384), bf16),
        ],
        scratch_shapes=[
            pltpu.VMEM((2, 256, wide), bf16),
            pltpu.VMEM((2, 256, wide), bf16),
            pltpu.VMEM((128, wide), f32),
            pltpu.VMEM((128, wide), f32),
            pltpu.VMEM((rows, 128), bf16),
        ],
        compiler_params=pltpu.CompilerParams(vmem_limit_bytes=VMEM),
        cost_estimate=pl.CostEstimate(
            flops=20 * pairs * rows * keys * 200, transcendentals=2 * pairs * rows * keys, bytes_accessed=rows * 768 * 20
        ),
        name="attend_back",
    )(mixed, grad_att, att, aq, keys_values, keys_values, act, act_keys, kaug_t)


def norm_stats(value):
    average = jnp.mean(value, axis=-1, keepdims=True)
    centered = value - average
    variance = jnp.mean(centered * centered, axis=-1, keepdims=True)
    scale = lax.rsqrt(variance + epsilon)
    return centered * scale, scale


def norm_back(unit, scale, gain, grad):
    inner = grad * gain
    along = jnp.mean(inner * unit, axis=-1, keepdims=True)
    return scale * (inner - jnp.mean(inner, axis=-1, keepdims=True) - unit * along)


def gelu_pair(value):
    size = jnp.abs(value)
    bell = jnp.exp2(value * value * (-0.5 * LOG2E))
    base = 1.0 + 0.231641888 * size
    t = pl.reciprocal(base, approx=True)
    t = t * (2.0 - base * t)
    fit = t * (0.127414796 + t * (-0.142248368 + t * (0.7107068705 + t * (-0.7265760135 + t * 0.5307027145))))
    tail = fit * bell
    share = jnp.where(value >= 0.0, 1.0 - tail, tail)
    return value * share, share + value * (bell * 0.3989422804014327)


def column_sums(grad):
    return jnp.sum(grad, axis=0, keepdims=True)


def project_kernel(place, x, vec, weight, *refs):
    mixed, act_out, x_out = refs[-3:]
    width = vec.shape[1]
    rows = x[0]
    x_out[...] = rows
    unit, _ = norm_stats(rows.astype(f32))
    act = (unit * vec[0:1] + vec[1:2]).astype(bf16)
    act_out[...] = act
    total = dot(act, weight[...])
    mixed[:, :width] = ((total[:, :width] + vec[8:9]) * (HEAD ** (-0.5) * LOG2E)).astype(bf16)
    mixed[:, width : 2 * width] = total[:, width : 2 * width].astype(bf16)
    mixed[:, 2 * width :] = (total[:, 2 * width :] + vec[9:10]).astype(bf16)


def fixed(array):
    return pl.BlockSpec(array.shape, lambda i: (0,) * array.ndim, pipeline_mode=pl.Buffered(1))


def project(start, total, x, place, vec, weight, held=()):
    _, count, width = x.shape
    cols = weight.shape[1]
    sizes = (cols, width, width)
    tile = tile_of(count, 256)

    def one(array):
        return pl.BlockSpec(array.shape, lambda i, at: (0, 0), pipeline_mode=pl.Buffered(1))

    return pl.pallas_call(
        project_kernel,
        grid_spec=pltpu.PrefetchScalarGridSpec(
            num_scalar_prefetch=1,
            grid=(count // tile,),
            in_specs=[pl.BlockSpec((1, tile, width), lambda i, at: (at[0], i, 0)), one(vec), one(weight)]
            + [pl.BlockSpec(memory_space=pl.ANY) for _ in held],
            out_specs=[pl.BlockSpec((tile, size), lambda i, at: (start // tile + i, 0)) for size in sizes],
        ),
        out_shape=[jax.ShapeDtypeStruct((total, size), bf16) for size in sizes],
        input_output_aliases={4 + i: i for i in range(len(held))},
        compiler_params=pltpu.CompilerParams(vmem_limit_bytes=VMEM),
        name="project",
    )(place.reshape(1), x, vec, weight, *held)


def middle_kernel(
    x, att, aux, vec, wo, w1, w2, m1, m2, cot, grad_att, grad_low, weight_grads, sums, pooled_out,
    hidden, slope, acc1, acc2, acco, pooled, map2g, stage, sems,
):
    step = pl.program_id(0)
    rows, width = x.shape
    wide = w1.shape[1]
    part = wide // 4
    map_size = sums.shape[0] - 32
    bias_o, gain2, bias2, bias_2, gain3, bias3 = [vec[n : n + 1] for n in range(2, 8)]

    @pl.when(step == 0)
    def _():
        for ref in (sums, pooled, map2g, acc1, acc2, acco):
            ref[...] = jnp.zeros_like(ref)

    att_low = att[...]
    resid1 = x[...].astype(f32) + dot(att_low, wo[...]) + bias_o
    unit2, scale2 = norm_stats(resid1)
    act2 = (unit2 * gain2 + bias2).astype(bf16)
    total = None
    for c in range(4):
        cols = slice(c * part, (c + 1) * part)
        value, rate = gelu_pair(dot(act2, w1[:, cols]) + vec[10 + c : 11 + c])
        value = value.astype(bf16)
        hidden[:, cols] = value
        slope[:, cols] = rate.astype(bf16)
        more = dot(value, w2[cols, :])
        total = more if total is None else total + more
    resid2 = resid1 + total + bias_2
    output_low = resid2.astype(bf16)
    grad_gate = dot(output_low, cot[...], NT)
    unit3, scale3 = norm_stats(resid2)
    act3 = (unit3 * gain3 + bias3).astype(bf16)
    map_hidden, map_slope = gelu_pair(dot(act3, m1[...]) + aux[4:5])
    map_hidden = map_hidden.astype(bf16)
    logits = dot(map_hidden, m2[...]) + aux[3:4]
    lanes = logits.shape[1]
    lane = lax.broadcasted_iota(jnp.int32, (rows, lanes), 1)
    row = lax.broadcasted_iota(jnp.int32, (rows, lanes), 0) + step * rows
    slot = row - (lane >> 3) * PATCH
    mask = (slot >= 0) & (slot.astype(f32) < aux[0:1])
    inverse = aux[1:2]
    raw = 1.0 / (1.0 + jnp.exp2(logits * (-LOG2E)))
    gates = jnp.where(mask, raw, 0.0)
    gates_low = gates.astype(bf16)
    pooled[...] += dot(gates_low.T, output_low)
    gate_sum = jnp.sum(gates, axis=1, keepdims=True)
    inverse_row = inverse[:, 0:1]
    sums[6:7, 256:384] += column_sums(gates * (gate_sum - gates)) * (inverse * inverse)

    grad_out = dot(gates_low, cot[...]) * inverse_row
    grad_gate = grad_gate * inverse + aux[2:3] * (gate_sum - gates)
    grad_logit = jnp.where(mask, grad_gate * raw * (1.0 - raw), 0.0)
    sums[6:7, 128:256] += column_sums(grad_logit)
    grad_logit = grad_logit.astype(bf16)
    map2g[...] += dot(map_hidden.T, grad_logit)
    grad_mpre = dot(grad_logit, m2[...], NT) * map_slope
    sums[6:7, 0:128] += column_sums(grad_mpre)
    grad_mpre = grad_mpre.astype(bf16)
    sums[16 : 16 + map_size] += dot(grad_mpre.T[:map_size], act3)
    grad_act = dot(grad_mpre, m1[...], NT)
    sums[4:5] += column_sums(grad_act * unit3)
    sums[5:6] += column_sums(grad_act)
    grad_res2 = norm_back(unit3, scale3, gain3, grad_act) + grad_out

    sums[3:4] += column_sums(grad_res2)
    g2 = grad_res2.astype(bf16)
    g2_t = g2.T
    act2_t = act2.T
    grad_act = None
    for c in range(4):
        cols = slice(c * part, (c + 1) * part)
        grad_pre = dot(g2, w2[cols, :], NT) * slope[:, cols].astype(f32)
        sums[8 + c : 9 + c] += column_sums(grad_pre)
        grad_pre = grad_pre.astype(bf16)
        slope[:, cols] = grad_pre
        more = dot(grad_pre, w1[:, cols], NT)
        grad_act = more if grad_act is None else grad_act + more
    for c in range(4):
        cols = slice(c * part, (c + 1) * part)
        acc1[:, cols] += dot(act2_t, slope[:, cols])
        acc2[:, cols] += dot(g2_t, hidden[:, cols])
    sums[1:2] += column_sums(grad_act * unit2)
    sums[2:3] += column_sums(grad_act)
    grad_res1 = norm_back(unit2, scale2, gain2, grad_act) + grad_res2

    sums[0:1] += column_sums(grad_res1)
    g1 = grad_res1.astype(bf16)
    grad_low[...] = g1
    acco[...] += dot(att_low.T, g1)
    grad_att[...] = dot(g1, wo[...], NT).astype(bf16)

    @pl.when(step == pl.num_programs(0) - 1)
    def _():
        groups, seqs, _, share, thin = weight_grads.shape
        pending = [[], []]
        count = 0

        def drain(value, *targets):
            nonlocal count
            slot = count % 2
            count += 1
            for copy in pending[slot]:
                copy.wait()
            stage[slot] = value.astype(bf16).reshape(stage.shape[1:])
            pending[slot] = [
                pltpu.make_async_copy(stage.at[slot, lo:hi], target, sems.at[slot, n])
                for n, (lo, hi, target) in enumerate(targets)
            ]
            for copy in pending[slot]:
                copy.start()

        for t in range(4 * seqs):
            drain(acc1[:, t * thin : (t + 1) * thin], (0, groups, weight_grads.at[:, t // 4, t % 4]))
        for c in range(4):
            cols = slice(c * part, (c + 1) * part)
            for s in range(seqs):
                value = acc2[s * thin : (s + 1) * thin, cols].T
                if groups == 1:
                    drain(value, (0, 1, weight_grads.at[:, s, 4 + c]))
                else:
                    few = groups // 4
                    drain(value, *[(4 * i, 4 * i + 4, weight_grads.at[c * few + i, s, 4:8]) for i in range(few)])
        for s in range(seqs):
            drain(acco[:, s * thin : (s + 1) * thin], (0, groups, weight_grads.at[:, s, 8]))
        pooled_out[...] = (pooled[...] * inverse_row).astype(bf16)
        for g in range(map_size // 16):
            sums[16 + map_size :, g * 128 : (g + 1) * 128] = map2g[g * 16 : (g + 1) * 16]
        for copy in pending[0] + pending[1]:
            copy.wait()


def middle(groups, seqs, map_size, x, att, *others):
    rows, width = x.shape
    wide = others[3].shape[1]
    lanes = others[0].shape[1]
    if width // groups % 16 or groups % 4 or width // seqs % 128:
        groups, seqs = 1, 1
    stage = (2, groups, width // groups, width // seqs)
    size = tile_of(rows, MIDDLE)
    tile = pl.BlockSpec((size, width), lambda i: (i, 0))
    anywhere = pl.BlockSpec(memory_space=pl.ANY)
    summed = [jax.ShapeDtypeStruct((map_size + 32, width), f32), jax.ShapeDtypeStruct((lanes, width), bf16)]
    return pl.pallas_call(
        middle_kernel,
        grid=(rows // size,),
        in_specs=[tile, tile] + [fixed(o) for o in others],
        out_specs=[tile, tile, anywhere] + [pl.BlockSpec(s.shape, lambda i: (0, 0)) for s in summed],
        out_shape=[
            jax.ShapeDtypeStruct((rows, width), bf16),
            jax.ShapeDtypeStruct((rows, width), bf16),
            jax.ShapeDtypeStruct((groups, seqs, 9, width // groups, width // seqs), bf16),
        ]
        + summed,
        scratch_shapes=[
            pltpu.VMEM((size, wide), bf16),
            pltpu.VMEM((size, wide), bf16),
            pltpu.VMEM((width, wide), f32),
            pltpu.VMEM((width, wide), f32),
            pltpu.VMEM((width, width), f32),
            pltpu.VMEM((lanes, width), f32),
            pltpu.VMEM((lanes, lanes), f32),
            pltpu.VMEM(stage, bf16),
            pltpu.SemaphoreType.DMA((2, max(1, groups // 4))),
        ],
        compiler_params=pltpu.CompilerParams(vmem_limit_bytes=VMEM),
        cost_estimate=pl.CostEstimate(
            flops=2 * rows * width * (6 * wide + 3 * width), transcendentals=rows * wide, bytes_accessed=rows * width * 12
        ),
        name="middle",
    )(x, att, *others)


def finish_kernel(place, x, g1, vec, weight, *refs):
    grads, (grad_in, sums) = refs[:-2], refs[-2:]
    parts = len(grads) // 3
    width = x.shape[1]

    @pl.when(pl.program_id(0) == 0)
    def _():
        sums[...] = jnp.zeros_like(sums)

    unit, scale = norm_stats(x[...].astype(f32))
    grad_act = None
    for i in range(3):
        at = 0
        for n in range(parts):
            part = grads[3 * n + i][...]
            share = part.shape[1]
            if i != 1:
                sums[2 + i // 2 : 3 + i // 2, at : at + share] += column_sums(part.astype(f32))
            more = dot(part, weight[:, i * width + at : i * width + at + share], NT)
            grad_act = more if grad_act is None else grad_act + more
            at += share
    sums[0:1] += column_sums(grad_act * unit)
    sums[1:2] += column_sums(grad_act)
    total = norm_back(unit, scale, vec[0:1], grad_act) + g1[...].astype(f32)
    grad_in[...] = total.astype(grad_in.dtype).reshape(grad_in.shape)


def finish(start, count, x, g1, vec, weight, grads, place=None, places=0):
    width = x.shape[1]
    size = tile_of(count, 256)
    begin = start // size
    tile = pl.BlockSpec((size, width), lambda i, at: (begin + i, 0))
    thin = [pl.BlockSpec((size, grad.shape[1]), lambda i, at: (begin + i, 0)) for grad in grads]
    if place is None:
        place = jnp.int32(0)
        out = (pl.BlockSpec((size, width), lambda i, at: (i, 0)), jax.ShapeDtypeStruct((count, width), bf16))
    else:
        out = (
            pl.BlockSpec((1, size, width), lambda i, at: (at[0], i, 0)),
            jax.ShapeDtypeStruct((places, count, width), f32),
        )

    def one(array):
        return pl.BlockSpec(array.shape, lambda i, at: (0, 0), pipeline_mode=pl.Buffered(1))

    return pl.pallas_call(
        finish_kernel,
        grid_spec=pltpu.PrefetchScalarGridSpec(
            num_scalar_prefetch=1,
            grid=(count // size,),
            in_specs=[tile] * 2 + [one(o) for o in (vec, weight)] + thin,
            out_specs=[out[0], pl.BlockSpec((8, width), lambda i, at: (0, 0))],
        ),
        out_shape=[out[1], jax.ShapeDtypeStruct((8, width), f32)],
        compiler_params=pltpu.CompilerParams(vmem_limit_bytes=VMEM),
        cost_estimate=pl.CostEstimate(
            flops=2 * count * width * weight.shape[1] * 2, transcendentals=0, bytes_accessed=count * width * 10
        ),
        name="finish",
    )(place.reshape(1), x, g1, vec, weight, *grads)


def shards(
    inputs,
    frame_tokens,
    clip_frames,
    norm1_gain,
    norm1_bias,
    qkv_weight,
    query_bias,
    value_bias,
    out_weight,
    out_bias,
    norm2_gain,
    norm2_bias,
    fc1_weight,
    fc1_bias,
    fc2_weight,
    fc2_bias,
    learn_gain,
    learn_bias,
    map1_weight,
    map1_bias,
    map2_weight,
    map2_bias,
    cot_pooled,
):
    clip_count, piece, width = inputs.shape
    seq_size = lax.axis_size("seq")
    position = lax.axis_index("seq")
    clip_size = lax.axis_size("clip")
    frames_here = piece // PATCH
    scaling = HEAD ** (-0.5)
    slots_all = float(clip_count * clip_size * seq_size * frames_here)
    group = seq_size // clip_count
    mine = position // group
    seat = position % group

    def route(turn):
        return [
            (s, ((s % clip_count + turn) % clip_count) * group + s // clip_count) for s in range(seq_size)
        ]

    def send(value, turn, back=False):
        pairs = route(turn)
        if back:
            pairs = [(b, a) for a, b in pairs]
        if all(a == b for a, b in pairs):
            return value
        return lax.ppermute(value, "seq", pairs)

    def scatter(whole, first=0):
        return [
            send(lax.dynamic_index_in_dim(whole, (position + turn) % clip_count, 0, False), turn)
            for turn in range(first, clip_count)
        ]

    def gather_back(parts, kind, whole=None):
        if whole is None:
            whole = jnp.zeros((clip_count,) + parts[0].shape, kind)
        for turn, part in enumerate(parts):
            if part is not None:
                home = send(part, turn, True).astype(kind)
                whole = lax.dynamic_update_index_in_dim(whole, home, (position + turn) % clip_count, 0)
        return whole

    tokens = lax.dynamic_index_in_dim(frame_tokens, mine, 0, False)
    frames = lax.dynamic_index_in_dim(clip_frames, mine, 0, False)
    rows = clip_count * piece
    keys = group * rows
    split = piece % 16 == 0 and group == 1 and clip_count == 2
    near = piece // TILE * TILE
    cot = jnp.concatenate(scatter(cot_pooled), axis=0).reshape(clip_count * frames_here * NTOK, width)

    def placed(ids, at_seat):
        turn = ids // piece
        source = clip_count * at_seat + (mine - turn) % clip_count
        local = ids - turn * piece
        frame = local // PATCH
        slot = local - frame * PATCH
        return (source * frames_here + frame < frames) & (slot < tokens)

    key_ids = jnp.arange(keys, dtype=jnp.int32)
    key_inside = placed(key_ids % rows, key_ids // rows)
    lane16 = jnp.arange(HEAD)
    key_mask = jnp.where(key_inside, 0.0, masked_score)
    kaug = jnp.where(lane16[None, :] < 3, 1.0, jnp.where(lane16[None, :] == 3, key_mask[:, None], 0.0)).astype(bf16)
    kaug = jnp.concatenate([kaug, jnp.zeros_like(kaug)], axis=1)
    sub16 = jnp.arange(16)[:, None]
    wide_mask = jnp.pad(key_mask, (0, up(keys, TILE) - keys), constant_values=masked_score)
    kaug_t = jnp.where(sub16 < 3, 1.0, jnp.where(sub16 == 3, wide_mask[None, :], 0.0)).astype(bf16)

    vec = jnp.concatenate(
        [
            norm1_gain,
            norm1_bias,
            out_bias,
            norm2_gain,
            norm2_bias,
            fc2_bias,
            learn_gain,
            learn_bias,
            query_bias,
            value_bias,
            fc1_bias,
        ]
    ).reshape(-1, width)
    begun = ()
    if split:
        (x_far,) = scatter(inputs, 1)
        held = project(0, rows, inputs, position % clip_count, vec, qkv_weight)
        held, begun = lax.optimization_barrier((held, (attend_near(near, held[0], kaug),)))
        mixed, act1, x_low = project(piece, rows, x_far[None], jnp.int32(0), vec, qkv_weight, held)
    else:
        x_all = jnp.concatenate(scatter(inputs), axis=0)[None]
        mixed, act1, x_low = project(0, rows, x_all, jnp.int32(0), vec, qkv_weight)
    if group == 1:
        keys_values, act_keys = mixed, act1
    else:
        both = lax.all_gather(mixed[:, width:], "seq", axis=0, tiled=True)
        keys_values = lax.dynamic_slice_in_dim(both, mine * keys, keys, 0)
        act_keys = lax.all_gather(act1, "seq", axis=0, tiled=True)
        act_keys = lax.dynamic_slice_in_dim(act_keys, mine * keys, keys, 0)
    att, aq = attend(mixed, keys_values, kaug, *begun)

    slots = clip_count * frames_here * NTOK
    lanes = -(-slots // 128) * 128
    pair_count = NTOK * (NTOK - 1)
    lane_ids = jnp.arange(lanes)
    lane_turn = lane_ids // (frames_here * NTOK)
    lane_frame = lane_ids // NTOK - lane_turn * frames_here
    lane_source = clip_count * seat + (mine - lane_turn) % clip_count
    lane_open = (lane_source * frames_here + lane_frame < frames) & (lane_ids < slots)
    inverse = lax.rsqrt(tokens.astype(f32))
    factor = 2.0 / pair_count * inverse * inverse / slots_all
    map_size = map1_bias.shape[0]
    aux = jnp.stack(
        [
            jnp.where(lane_open, tokens, 0).astype(f32),
            jnp.full((lanes,), inverse),
            jnp.full((lanes,), factor),
            jnp.tile(map2_bias, lanes // NTOK),
            jnp.pad(map1_bias, (0, lanes - map_size)),
        ]
        + [jnp.zeros((lanes,), f32)] * 3
    )
    map1_wide = jnp.pad(map1_weight, ((0, 0), (0, lanes - map_size)))
    map2_wide = jnp.pad(jnp.tile(map2_weight, (1, lanes // NTOK)), ((0, lanes - map_size), (0, 0)))
    cot = jnp.pad(cot, ((0, lanes - slots), (0, 0)))
    grad_att, grad_low, weight_part, early, pooled = middle(
        clip_size,
        seq_size,
        map_size,
        x_low,
        att,
        aux,
        vec,
        out_weight,
        fc1_weight,
        fc2_weight,
        map1_wide,
        map2_wide,
        cot,
    )

    def over_clip(matrix):
        return lax.psum_scatter(matrix, "clip", scatter_dimension=0, tiled=True)

    def bits(size):
        return [1 << n for n in range(size.bit_length() - 1)]

    clip_steps = [("clip", bit) for bit in bits(clip_size)]
    seq_steps = [("seq", bit) for bit in bits(seq_size)]
    early_steps = clip_steps[:1] + seq_steps + clip_steps[1:]

    def meet(value, step):
        axis, bit = step
        return lax.ppermute(value, axis, [(i, i ^ bit) for i in range(lax.axis_size(axis))])

    def part_ways(blocks, step):
        axis, bit = step
        halves = blocks.reshape((-1, 2) + blocks.shape[1:])
        side = (lax.axis_index(axis) // bit) % 2
        away = lax.dynamic_index_in_dim(halves, 1 - side, 1, False)
        return lax.dynamic_index_in_dim(halves, side, 1, False), meet(away, step)

    def add_low(kept, received):
        return (kept.astype(f32) + received.astype(f32)).astype(bf16)

    def back(start, pairs, source):
        return attend_back(
            start, pairs, source, keys_values if group > 1 else source, grad_att, att, aq, act1, act_keys, kaug_t
        )

    tie = lax.optimization_barrier
    pairs = (4, 2)
    share = width // clip_size
    thin = width // seq_size
    if weight_part.shape[0] == 1:
        fc1_part = weight_part[0, 0, :4].transpose(1, 0, 2).reshape(clip_size, share, seq_size, 4, thin)
        fc2_part = weight_part[0, 0, 4:8].reshape(clip_size, 4, share, seq_size, thin).transpose(0, 3, 1, 2, 4)
        out_part = weight_part[0, 0, 8].reshape(clip_size, 1, share, seq_size, thin).transpose(0, 3, 1, 2, 4)
        weight_part = jnp.concatenate([fc1_part.transpose(0, 2, 3, 1, 4), fc2_part, out_part], axis=2)
    slab = over_clip(weight_part)[0]
    near_early = meet(early, early_steps[0])
    back0 = back(0, pairs[0], mixed)
    mixed, slab, early, near_early, pooled, back0 = tie((mixed, slab, early, near_early, pooled, back0))
    early = early + near_early
    near_early = meet(early, early_steps[1])
    slab = lax.psum_scatter(slab, "seq", scatter_dimension=0, tiled=False)
    slab0 = over_clip(back0[3])
    pooled = pooled[:slots].reshape(clip_count, frames_here, NTOK, width)
    pooled = [send(pooled[t], t, True) for t in range(clip_count)]
    back1 = back(pairs[0], pairs[1], mixed)
    slab, slab0, early, near_early, pooled, back1 = tie((slab, slab0, early, near_early, pooled, back1))
    early = early + near_early
    grads = [list(one[:3]) for one in (back0, back1)]
    if group > 1:
        both = jnp.zeros((seq_size * rows, 2 * width), bf16)
        both = lax.dynamic_update_slice_in_dim(
            both, jnp.concatenate([one[i] for i in (1, 2) for one in grads], axis=1), mine * keys, 0
        )
        both = lax.psum_scatter(both, "seq", scatter_dimension=0, tiled=True)
        at = 0
        for i in (1, 2):
            for n in range(2):
                grads[n][i] = both[:, at : at + pairs[n] * 128]
                at += pairs[n] * 128
    grads = [grad for one in grads for grad in one]
    rest = (grad_low, vec, qkv_weight, grads)
    near_early = meet(early, early_steps[2])
    kept, received = part_ways(back1[3].reshape(clip_size, share, -1), clip_steps[0])
    if split:
        size = tile_of(piece, 256)
        lead = 2 * size if piece > 2 * size else size
        far0, sums0 = finish(piece, lead, x_low, *rest)
        far0, sums0, x_low, near_early, received = tie((far0, sums0, x_low, near_early, received))
        home0 = send(far0, 1, True)
    early = early + near_early
    near_early = meet(early, early_steps[3])
    kept, received = part_ways(add_low(kept, received), clip_steps[1])
    if split:
        far1, sums1 = finish(piece + lead, piece - lead, x_low, *rest)
        far1, sums1, x_low, near_early, received, home0 = tie((far1, sums1, x_low, near_early, received, home0))
        home1 = send(far1, 1, True)
    early = early + near_early
    near_early = meet(early, early_steps[4])
    kept, received = part_ways(add_low(kept, received), clip_steps[2])
    if split:
        input_grad, late = finish(0, piece, x_low, *rest, place=position % clip_count, places=clip_count)
        input_grad, late, near_early, received = tie((input_grad, late, near_early, received))
        other = (position + 1) % clip_count
        input_grad = lax.dynamic_update_slice(input_grad, home0.astype(f32)[None], (other, 0, 0))
        late = late + sums0 + sums1
    else:
        local, late = finish(0, rows, x_low, *rest)
        input_grad = gather_back([local[t * piece : (t + 1) * piece] for t in range(clip_count)], f32)
    early = early + near_early
    for step in early_steps[5:]:
        early = early + meet(early, step)
    slab1 = add_low(kept, received)
    for step in clip_steps[3:]:
        slab1 = add_low(*part_ways(slab1, step))
    late = late[:4]
    for first, *second in zip(clip_steps[::2], clip_steps[1::2]):
        low, high = first[1], second[0][1]
        near_sum = late + meet(late, ("clip", low))
        late = near_sum + (meet(late, ("clip", high)) + meet(late, ("clip", low + high)))
    if len(clip_steps) % 2:
        late = late + meet(late, clip_steps[-1])
    if split:
        home1, late, slab1, slab, early, pooled = tie((home1, late, slab1, slab, early, pooled))
    for step in seq_steps:
        late = late + meet(late, step)
    qkv = [
        part.reshape(share, count, 3, 128).transpose(0, 2, 1, 3) for part, count in zip((slab0, slab1), pairs)
    ]
    qkv = jnp.concatenate(qkv, axis=2).reshape(share, seq_size, -1).transpose(1, 0, 2)
    for step in seq_steps:
        qkv = add_low(*part_ways(qkv, step))
    qkv_grad = qkv[0].astype(f32)
    if split:
        input_grad = lax.dynamic_update_slice(input_grad, home1.astype(f32)[None], (other, lead, 0))
    fc1_grad = slab[:4].transpose(1, 0, 2).reshape(share, 4 * thin).astype(f32)
    fc2_grad = slab[4:8].reshape(4 * share, thin).astype(f32)
    out_grad = slab[8].astype(f32)

    pooled = jnp.stack(pooled)[(jnp.arange(clip_count) - position) % clip_count]
    small = early[6]
    map1_grad = early[16 : 16 + map_size].T
    map2_grad = early[16 + map_size :, : map_size // 16 * lanes].reshape(16, map_size // 16, lanes // NTOK, NTOK)
    map2_grad = jnp.sum(map2_grad, axis=2).transpose(1, 0, 2).reshape(map_size, NTOK)
    map2_bias_grad = jnp.sum(small[128:256].reshape(-1, NTOK), axis=0)
    penalty = jnp.sum(small[256:384]) / pair_count / slots_all
    return (
        pooled,
        penalty,
        input_grad,
        late[0],
        late[1],
        qkv_grad,
        late[2],
        late[3],
        out_grad,
        early[0],
        early[1],
        early[2],
        fc1_grad,
        early[8:12].reshape(-1),
        fc2_grad,
        early[3],
        early[4],
        early[5],
        map1_grad,
        small[:map_size],
        map2_grad,
        map2_bias_grad,
    )


def solution(mesh):
    row_spec = P("clip", "seq", None)
    pool_spec = P("clip", "seq", None, None)
    matrix_spec = P("clip", "seq")
    in_specs = (row_spec, P("clip"), P("clip")) + (P(),) * 19 + (pool_spec,)
    out_specs = (
        (pool_spec, P(), row_spec, P(), P(), matrix_spec, P(), P(), matrix_spec, P(), P(), P(), matrix_spec, P())
        + (matrix_spec,)
        + (P(),) * 7
    )
    return jax.shard_map(shards, mesh=mesh, in_specs=in_specs, out_specs=out_specs, check_vma=False)
```

```python
import jax
import jax.numpy as jnp
from jax import lax
from jax.experimental import pallas as pl
from jax.experimental.pallas import tpu as pltpu
from jax.sharding import PartitionSpec as P

HEADS = 12
HEAD = 64
NTOK = 8
PATCH = 196
TILE = 256
AHEAD = 0
MIDDLE = 448
LOG2E = 1.4426950408889634
LN2 = 0.6931471805599453
VMEM = 60 * 1024 * 1024

epsilon = 1e-06
masked_score = -1e30
bf16 = jnp.bfloat16
f32 = jnp.float32

NN = (((1,), (0,)), ((), ()))
NT = (((1,), (1,)), ((), ()))


def dot(left, right, dims=NN):
    return lax.dot_general(left, right, dims, preferred_element_type=f32)


def split3(value):
    hi = value.astype(bf16).astype(f32)
    mid = (value - hi).astype(bf16).astype(f32)
    return hi, mid, value - hi - mid


def up(count, unit):
    return -(-count // unit) * unit


def tile_of(count, most):
    return max(size for size in range(16, most + 1, 16) if count % size == 0)


def blocks_of(count, unit):
    return [(base, min(unit, count - base)) for base in range(0, count, unit)]


def flip(value):
    return jnp.concatenate([value[base : base + size].T for base, size in blocks_of(value.shape[0], 128)], axis=1)


def spread_heads(source, held, aug):
    count = source.shape[0]
    zero = jnp.zeros((HEAD, held.shape[2]), bf16)
    for j in range(2):
        other = (1 - j) * HEAD
        held[j, other : other + HEAD] = zero
        if held.shape[2] > count:
            edge = count // 128 * 128
            held[j, j * HEAD : (j + 1) * HEAD, edge:] = jnp.zeros((HEAD, held.shape[2] - edge), bf16)
        held[j, 128:256] = aug(j)
    for base, size in blocks_of(count, 256):
        flat = flip(source[base : base + size])
        for j in range(2):
            held[j, j * HEAD : (j + 1) * HEAD, base : base + size] = flat[j * HEAD : (j + 1) * HEAD]


def spread_queries(q, qp):
    ids = lax.broadcasted_iota(jnp.int32, (128, qp.shape[2]), 0)
    spread_heads(q, qp, lambda j: jnp.where(ids == 3, 1.0, 0.0).astype(bf16))


def flip_into(source, target):
    for base, size in blocks_of(source.shape[0], 256):
        target[:, base : base + size] = flip(source[base : base + size])


def key_block(k, kaug, base, size):
    return jnp.concatenate([k[pl.ds(base, size), :], kaug[pl.ds(base, size), :]], axis=1)


def value_block(vt, j, base, size):
    ones = jnp.ones((16, size), bf16)
    return jnp.concatenate([vt[j * HEAD : (j + 1) * HEAD, pl.ds(base, size)], ones], axis=0)


def over_tiles(step, begin, count):
    @pl.loop(begin // TILE, count // TILE, unroll=3)
    def _(t):
        step(pl.multiple_of(t * TILE, TILE), TILE)

    if count % TILE:
        step(count // TILE * TILE, count % TILE)


def fold_tile(k, kaug, qp, vt, acc, low, fresh, base, size):
    for j in range(2):
        p = jnp.exp2(dot(key_block(k, kaug, base, size), qp[j, :, low:])).astype(bf16)
        part = dot(value_block(vt, j, base, size), p)
        if fresh:
            acc[j, :, low:] = part
        else:
            acc[j, :, low:] += part


def attend_near_kernel(q, k, v, kaug, acc, qp, vt):
    spread_queries(q, qp)
    flip_into(v, vt)
    fold_tile(k, kaug, qp, vt, acc, 0, True, 0, TILE)
    over_tiles(lambda base, size: fold_tile(k, kaug, qp, vt, acc, 0, False, base, size), TILE, k.shape[0])


def attend_near(near, mixed, kaug):
    pairs = HEADS // 2
    return pl.pallas_call(
        attend_near_kernel,
        grid=(pairs,),
        in_specs=[
            pl.BlockSpec((near, 128), lambda h: (0, h)),
            pl.BlockSpec((near, 128), lambda h: (0, pairs + h)),
            pl.BlockSpec((near, 128), lambda h: (0, 2 * pairs + h)),
            pl.BlockSpec((near, 128), lambda h: (0, 0)),
        ],
        out_specs=pl.BlockSpec((2, HEAD + 16, near), lambda h: (h, 0, 0)),
        out_shape=jax.ShapeDtypeStruct((HEADS, HEAD + 16, near), f32),
        scratch_shapes=[pltpu.VMEM((2, 256, near), bf16), pltpu.VMEM((128, near), bf16)],
        compiler_params=pltpu.CompilerParams(vmem_limit_bytes=VMEM),
        cost_estimate=pl.CostEstimate(
            flops=4 * HEADS * near * near * 256, transcendentals=HEADS * near * near, bytes_accessed=near * 768 * 10
        ),
        name="attend_near",
    )(mixed, mixed, mixed, kaug)


def attend_kernel(q, k, v, kaug, *refs):
    att, aq, qp, vt, acc = refs[-5:]
    rows = q.shape[0]
    keys = k.shape[0]
    wide = qp.shape[2]
    spread_queries(q, qp)
    flip_into(v, vt)

    def fold(low, fresh):
        return lambda base, size: fold_tile(k, kaug, qp, vt, acc, low, fresh, base, size)

    begun = 0
    if len(refs) > 5:
        begun = refs[0].shape[2]
        acc[:, :, :begun] = refs[0][...]
    fold(begun, True)(0, TILE)
    if begun:
        over_tiles(fold(begun, False), TILE, begun)
    over_tiles(fold(0, False), max(begun, TILE), keys)

    for j in range(2):
        total = acc[j, HEAD : HEAD + 1]
        fine = (total > 2.0**-60) & (total < 2.0**60)
        bad = jnp.max(jnp.where(fine, 0.0, 1.0)) > 0.5
        acc[j, HEAD + 8 : HEAD + 9] = jnp.zeros((1, wide), f32)

        @pl.when(bad)
        def _():
            acc[j, 0:1] = jnp.full((1, wide), -1e38, f32)

            def largest(base, size):
                s = dot(key_block(k, kaug, base, size), qp[j])
                acc[j, 0:1] = jnp.maximum(acc[j, 0:1], jnp.max(s, axis=0, keepdims=True))

            over_tiles(largest, 0, keys)
            best = acc[j, 0:1]
            acc[j] = jnp.zeros((HEAD + 16, wide), f32)

            def again(base, size):
                p = jnp.exp2(dot(key_block(k, kaug, base, size), qp[j]) - best).astype(bf16)
                acc[j] += dot(value_block(vt, j, base, size), p)

            over_tiles(again, 0, keys)
            acc[j, HEAD + 8 : HEAD + 9] = best

    ids = lax.broadcasted_iota(jnp.int32, (HEAD, 128), 0)
    for base, size in blocks_of(rows, 128):
        here = slice(base, base + 128)
        outs = []
        augs = []
        for j in range(2):
            total = acc[j, HEAD : HEAD + 1, here]
            outs.append(acc[j, 0:HEAD, here] * (1.0 / total))
            lse = jnp.log2(total) + acc[j, HEAD + 8 : HEAD + 9, here]
            hi, mid, low = split3(-lse)
            aug = jnp.where(ids == 0, hi, jnp.where(ids == 1, mid, jnp.where(ids == 2, low, 0.0)))
            augs.append(jnp.where(ids == 3, 1.0, aug))
        att[base : base + size, :] = jnp.concatenate(outs, axis=0).T[:size].astype(bf16)
        aq[base : base + size, :] = jnp.concatenate(augs, axis=0).T[:size].astype(bf16)


def attend(mixed, keys_values, kaug, *begun):
    rows = mixed.shape[0]
    keys = keys_values.shape[0]
    pairs = HEADS // 2
    wide = up(rows, 128)
    first = keys_values.shape[1] // 128 - 2 * pairs
    return pl.pallas_call(
        attend_kernel,
        grid=(pairs,),
        in_specs=[
            pl.BlockSpec((rows, 128), lambda h: (0, h)),
            pl.BlockSpec((keys, 128), lambda h: (0, first + h)),
            pl.BlockSpec((keys, 128), lambda h: (0, first + pairs + h)),
            pl.BlockSpec((keys, 128), lambda h: (0, 0)),
        ]
        + [pl.BlockSpec((2,) + one.shape[1:], lambda h: (h, 0, 0)) for one in begun],
        out_specs=[
            pl.BlockSpec((rows, 128), lambda h: (0, h)),
            pl.BlockSpec((rows, 128), lambda h: (0, h)),
        ],
        out_shape=[
            jax.ShapeDtypeStruct((rows, HEADS * HEAD), bf16),
            jax.ShapeDtypeStruct((rows, HEADS * HEAD), bf16),
        ],
        scratch_shapes=[
            pltpu.VMEM((2, 256, wide), bf16),
            pltpu.VMEM((128, up(keys, 128)), bf16),
            pltpu.VMEM((2, HEAD + 16, wide), f32),
        ],
        compiler_params=pltpu.CompilerParams(vmem_limit_bytes=VMEM),
        cost_estimate=pl.CostEstimate(
            flops=4 * HEADS * rows * keys * 256, transcendentals=HEADS * rows * keys, bytes_accessed=rows * 768 * 10
        ),
        name="attend",
    )(mixed, keys_values, keys_values, kaug, *begun)


def attend_back_kernel(q, do, att, aq, k, v, act_rows, act_keys, kaug_t, dq, dk, dv, weight_grad, kp, vp, dkt, dvt, dqs):
    step = pl.program_id(1)
    rows = q.shape[0]
    keys = k.shape[0]
    tiles = up(keys, TILE) // TILE

    @pl.when(step == 0)
    def _():
        rest = jnp.zeros((HEAD - 16, kp.shape[2]), bf16)
        zero = jnp.zeros((HEAD, kp.shape[2]), bf16)
        halves = (jnp.concatenate([kaug_t[...], rest, zero], axis=0), jnp.concatenate([zero, kaug_t[...], rest], axis=0))
        for source, held in ((k, kp), (v, vp)):
            spread_heads(source, held, lambda j: halves[j])
        dkt[...] = jnp.zeros_like(dkt)
        dvt[...] = jnp.zeros_like(dvt)

    units = [(j, t) for j in range(2) for t in range(tiles)]
    count = len(units)
    totals = [None, None]
    qa = jnp.concatenate([q[...], aq[...]], axis=1)

    def cols(t):
        return slice(t * TILE, (t + 1) * TILE)

    def scores(i):
        j, t = units[i]
        return dot(qa, kp[j, :, cols(t)])

    def weigh(s, dp):
        p = jnp.exp2(s)
        return p.astype(bf16), (p * dp).astype(bf16)

    def collect(j, t, p, ds):
        part = slice(j * HEAD, (j + 1) * HEAD)
        dvt[part, cols(t)] += dot(dot_[part], p)
        dkt[part, cols(t)] += dot(qt[part], ds)
        more = dot(ds[:, : min(TILE, keys - t * TILE)], k[t * TILE : min(keys, (t + 1) * TILE), :])
        totals[j] = more if totals[j] is None else totals[j] + more

    ahead = AHEAD
    raw = {i: scores(i) for i in range(min(ahead, count))}
    lane = lax.broadcasted_iota(jnp.int32, (rows, 128), 1)
    product = do[...].astype(f32) * att[...].astype(f32)
    inner0 = jnp.sum(jnp.where(lane < HEAD, product, 0.0), axis=1, keepdims=True)
    inner1 = jnp.sum(jnp.where(lane < HEAD, 0.0, product), axis=1, keepdims=True)
    hi, mid, low = split3(-jnp.where(lane < HEAD, inner0, inner1))
    within = lane % HEAD
    ado = jnp.where(within == 0, hi, jnp.where(within == 1, mid, jnp.where(within == 2, low, 0.0))).astype(bf16)
    da = jnp.concatenate([do[...], ado], axis=1)
    ready = {}
    for i in range(count + 2):
        if i < count:
            j, t = units[i]
            s = raw.pop(i) if i in raw else scores(i)
            raw[i] = (s, dot(da, vp[j, :, cols(t)]))
        if i == 1:
            qt = flip(q[...])
            dot_ = flip(do[...])
        if 0 <= i - 1 < count:
            ready[i - 1] = weigh(*raw.pop(i - 1))
        if 0 <= i - 2 < count:
            collect(*units[i - 2], *ready.pop(i - 2))
    grad_q = (jnp.where(lane < HEAD, totals[0], totals[1]) * HEAD ** (-0.5)).astype(bf16)
    dq[...] = grad_q
    dqs[pl.ds(pl.multiple_of(step * rows, 16), rows), :] = grad_q

    @pl.when(step == pl.num_programs(1) - 1)
    def _():
        total = jnp.zeros((128, act_rows.shape[1]), f32)
        for base, size in blocks_of(dqs.shape[0], TILE):
            total += dot(flip(dqs[base : base + size]), act_rows[base : base + size])
        weight_grad[:, 0:128] = total.T.astype(bf16)
        total = jnp.zeros((256, act_rows.shape[1]), f32)
        for base, size in blocks_of(keys, TILE):
            grad_k = (dkt[:, base : base + size] * LN2).astype(bf16)
            grad_v = dvt[:, base : base + size].astype(bf16)
            dk[base : base + size] = grad_k.T
            dv[base : base + size] = grad_v.T
            total += dot(jnp.concatenate([grad_k, grad_v], axis=0), act_keys[base : base + size])
        weight_grad[:, 128:384] = total.T.astype(bf16)


def attend_back(start, pairs, mixed, keys_values, grad_att, att, aq, act, act_keys, kaug_t):
    rows, width = act.shape
    keys = keys_values.shape[0]
    wide = up(keys, TILE)
    size = tile_of(rows, 512)
    first = keys_values.shape[1] // 128 - HEADS
    here = pl.BlockSpec((size, 128), lambda h, r: (r, start + h))
    whole = pl.BlockSpec((keys, 128), lambda h, r: (0, h))
    return pl.pallas_call(
        attend_back_kernel,
        grid=(pairs, rows // size),
        in_specs=[
            here,
            here,
            here,
            here,
            pl.BlockSpec((keys, 128), lambda h, r: (0, first + start + h)),
            pl.BlockSpec((keys, 128), lambda h, r: (0, first + HEADS // 2 + start + h)),
            pl.BlockSpec((rows, width), lambda h, r: (0, 0), pipeline_mode=pl.Buffered(1)),
            pl.BlockSpec((keys, width), lambda h, r: (0, 0), pipeline_mode=pl.Buffered(1)),
            pl.BlockSpec((16, wide), lambda h, r: (0, 0), pipeline_mode=pl.Buffered(1)),
        ],
        out_specs=[
            pl.BlockSpec((size, 128), lambda h, r: (r, h)),
            whole,
            whole,
            pl.BlockSpec((width, 384), lambda h, r: (0, h)),
        ],
        out_shape=[
            jax.ShapeDtypeStruct((rows, pairs * 128), bf16),
            jax.ShapeDtypeStruct((keys, pairs * 128), bf16),
            jax.ShapeDtypeStruct((keys, pairs * 128), bf16),
            jax.ShapeDtypeStruct((width, pairs * 384), bf16),
        ],
        scratch_shapes=[
            pltpu.VMEM((2, 256, wide), bf16),
            pltpu.VMEM((2, 256, wide), bf16),
            pltpu.VMEM((128, wide), f32),
            pltpu.VMEM((128, wide), f32),
            pltpu.VMEM((rows, 128), bf16),
        ],
        compiler_params=pltpu.CompilerParams(vmem_limit_bytes=VMEM),
        cost_estimate=pl.CostEstimate(
            flops=20 * pairs * rows * keys * 200, transcendentals=2 * pairs * rows * keys, bytes_accessed=rows * 768 * 20
        ),
        name="attend_back",
    )(mixed, grad_att, att, aq, keys_values, keys_values, act, act_keys, kaug_t)


def norm_stats(value):
    average = jnp.mean(value, axis=-1, keepdims=True)
    centered = value - average
    variance = jnp.mean(centered * centered, axis=-1, keepdims=True)
    scale = lax.rsqrt(variance + epsilon)
    return centered * scale, scale


def norm_back(unit, scale, gain, grad):
    inner = grad * gain
    along = jnp.mean(inner * unit, axis=-1, keepdims=True)
    return scale * (inner - jnp.mean(inner, axis=-1, keepdims=True) - unit * along)


def gelu_pair(value):
    size = jnp.abs(value)
    bell = jnp.exp2(value * value * (-0.5 * LOG2E))
    base = 1.0 + 0.231641888 * size
    t = pl.reciprocal(base, approx=True)
    t = t * (2.0 - base * t)
    fit = t * (0.127414796 + t * (-0.142248368 + t * (0.7107068705 + t * (-0.7265760135 + t * 0.5307027145))))
    tail = fit * bell
    share = jnp.where(value >= 0.0, 1.0 - tail, tail)
    return value * share, share + value * (bell * 0.3989422804014327)


def column_sums(grad):
    return jnp.sum(grad, axis=0, keepdims=True)


def project_kernel(place, x, vec, weight, *refs):
    mixed, act_out, x_out = refs[-3:]
    width = vec.shape[1]
    rows = x[0]
    x_out[...] = rows
    unit, _ = norm_stats(rows.astype(f32))
    act = (unit * vec[0:1] + vec[1:2]).astype(bf16)
    act_out[...] = act
    total = dot(act, weight[...])
    mixed[:, :width] = ((total[:, :width] + vec[8:9]) * (HEAD ** (-0.5) * LOG2E)).astype(bf16)
    mixed[:, width : 2 * width] = total[:, width : 2 * width].astype(bf16)
    mixed[:, 2 * width :] = (total[:, 2 * width :] + vec[9:10]).astype(bf16)


def fixed(array):
    return pl.BlockSpec(array.shape, lambda i: (0,) * array.ndim, pipeline_mode=pl.Buffered(1))


def project(start, total, x, place, vec, weight, held=()):
    _, count, width = x.shape
    cols = weight.shape[1]
    sizes = (cols, width, width)
    tile = tile_of(count, 256)

    def one(array):
        return pl.BlockSpec(array.shape, lambda i, at: (0, 0), pipeline_mode=pl.Buffered(1))

    return pl.pallas_call(
        project_kernel,
        grid_spec=pltpu.PrefetchScalarGridSpec(
            num_scalar_prefetch=1,
            grid=(count // tile,),
            in_specs=[pl.BlockSpec((1, tile, width), lambda i, at: (at[0], i, 0)), one(vec), one(weight)]
            + [pl.BlockSpec(memory_space=pl.ANY) for _ in held],
            out_specs=[pl.BlockSpec((tile, size), lambda i, at: (start // tile + i, 0)) for size in sizes],
        ),
        out_shape=[jax.ShapeDtypeStruct((total, size), bf16) for size in sizes],
        input_output_aliases={4 + i: i for i in range(len(held))},
        compiler_params=pltpu.CompilerParams(vmem_limit_bytes=VMEM),
        name="project",
    )(place.reshape(1), x, vec, weight, *held)


def middle_kernel(
    x, att, aux, vec, wo, w1, w2, m1, m2, cot, grad_att, grad_low, weight_grads, sums, pooled_out,
    hidden, slope, acc1, acc2, acco, pooled, map2g, stage, sems,
):
    step = pl.program_id(0)
    rows, width = x.shape
    wide = w1.shape[1]
    part = wide // 4
    map_size = sums.shape[0] - 32
    bias_o, gain2, bias2, bias_2, gain3, bias3 = [vec[n : n + 1] for n in range(2, 8)]

    @pl.when(step == 0)
    def _():
        for ref in (sums, pooled, map2g, acc1, acc2, acco):
            ref[...] = jnp.zeros_like(ref)

    att_low = att[...]
    resid1 = x[...].astype(f32) + dot(att_low, wo[...]) + bias_o
    unit2, scale2 = norm_stats(resid1)
    act2 = (unit2 * gain2 + bias2).astype(bf16)
    total = None
    for c in range(4):
        cols = slice(c * part, (c + 1) * part)
        value, rate = gelu_pair(dot(act2, w1[:, cols]) + vec[10 + c : 11 + c])
        value = value.astype(bf16)
        hidden[:, cols] = value
        slope[:, cols] = rate.astype(bf16)
        more = dot(value, w2[cols, :])
        total = more if total is None else total + more
    resid2 = resid1 + total + bias_2
    output_low = resid2.astype(bf16)
    grad_gate = dot(output_low, cot[...], NT)
    unit3, scale3 = norm_stats(resid2)
    act3 = (unit3 * gain3 + bias3).astype(bf16)
    map_hidden, map_slope = gelu_pair(dot(act3, m1[...]) + aux[4:5])
    map_hidden = map_hidden.astype(bf16)
    logits = dot(map_hidden, m2[...]) + aux[3:4]
    lanes = logits.shape[1]
    lane = lax.broadcasted_iota(jnp.int32, (rows, lanes), 1)
    row = lax.broadcasted_iota(jnp.int32, (rows, lanes), 0) + step * rows
    slot = row - (lane >> 3) * PATCH
    mask = (slot >= 0) & (slot.astype(f32) < aux[0:1])
    inverse = aux[1:2]
    raw = 1.0 / (1.0 + jnp.exp2(logits * (-LOG2E)))
    gates = jnp.where(mask, raw, 0.0)
    gates_low = gates.astype(bf16)
    pooled[...] += dot(gates_low.T, output_low)
    gate_sum = jnp.sum(gates, axis=1, keepdims=True)
    inverse_row = inverse[:, 0:1]
    sums[6:7, 256:384] += column_sums(gates * (gate_sum - gates)) * (inverse * inverse)

    grad_out = dot(gates_low, cot[...]) * inverse_row
    grad_gate = grad_gate * inverse + aux[2:3] * (gate_sum - gates)
    grad_logit = jnp.where(mask, grad_gate * raw * (1.0 - raw), 0.0)
    sums[6:7, 128:256] += column_sums(grad_logit)
    grad_logit = grad_logit.astype(bf16)
    map2g[...] += dot(map_hidden.T, grad_logit)
    grad_mpre = dot(grad_logit, m2[...], NT) * map_slope
    sums[6:7, 0:128] += column_sums(grad_mpre)
    grad_mpre = grad_mpre.astype(bf16)
    sums[16 : 16 + map_size] += dot(grad_mpre.T[:map_size], act3)
    grad_act = dot(grad_mpre, m1[...], NT)
    sums[4:5] += column_sums(grad_act * unit3)
    sums[5:6] += column_sums(grad_act)
    grad_res2 = norm_back(unit3, scale3, gain3, grad_act) + grad_out

    sums[3:4] += column_sums(grad_res2)
    g2 = grad_res2.astype(bf16)
    g2_t = g2.T
    act2_t = act2.T
    grad_act = None
    for c in range(4):
        cols = slice(c * part, (c + 1) * part)
        grad_pre = dot(g2, w2[cols, :], NT) * slope[:, cols].astype(f32)
        sums[8 + c : 9 + c] += column_sums(grad_pre)
        grad_pre = grad_pre.astype(bf16)
        slope[:, cols] = grad_pre
        more = dot(grad_pre, w1[:, cols], NT)
        grad_act = more if grad_act is None else grad_act + more
    for c in range(4):
        cols = slice(c * part, (c + 1) * part)
        acc1[:, cols] += dot(act2_t, slope[:, cols])
        acc2[:, cols] += dot(g2_t, hidden[:, cols])
    sums[1:2] += column_sums(grad_act * unit2)
    sums[2:3] += column_sums(grad_act)
    grad_res1 = norm_back(unit2, scale2, gain2, grad_act) + grad_res2

    sums[0:1] += column_sums(grad_res1)
    g1 = grad_res1.astype(bf16)
    grad_low[...] = g1
    acco[...] += dot(att_low.T, g1)
    grad_att[...] = dot(g1, wo[...], NT).astype(bf16)

    @pl.when(step == pl.num_programs(0) - 1)
    def _():
        groups, seqs, _, share, thin = weight_grads.shape
        pending = [[], []]
        count = 0

        def drain(value, *targets):
            nonlocal count
            slot = count % 2
            count += 1
            for copy in pending[slot]:
                copy.wait()
            stage[slot] = value.astype(bf16).reshape(stage.shape[1:])
            pending[slot] = [
                pltpu.make_async_copy(stage.at[slot, lo:hi], target, sems.at[slot, n])
                for n, (lo, hi, target) in enumerate(targets)
            ]
            for copy in pending[slot]:
                copy.start()

        for t in range(4 * seqs):
            drain(acc1[:, t * thin : (t + 1) * thin], (0, groups, weight_grads.at[:, t // 4, t % 4]))
        for c in range(4):
            cols = slice(c * part, (c + 1) * part)
            for s in range(seqs):
                value = acc2[s * thin : (s + 1) * thin, cols].T
                if groups == 1:
                    drain(value, (0, 1, weight_grads.at[:, s, 4 + c]))
                else:
                    few = groups // 4
                    drain(value, *[(4 * i, 4 * i + 4, weight_grads.at[c * few + i, s, 4:8]) for i in range(few)])
        for s in range(seqs):
            drain(acco[:, s * thin : (s + 1) * thin], (0, groups, weight_grads.at[:, s, 8]))
        pooled_out[...] = (pooled[...] * inverse_row).astype(bf16)
        for g in range(map_size // 16):
            sums[16 + map_size :, g * 128 : (g + 1) * 128] = map2g[g * 16 : (g + 1) * 16]
        for copy in pending[0] + pending[1]:
            copy.wait()


def middle(groups, seqs, map_size, x, att, *others):
    rows, width = x.shape
    wide = others[3].shape[1]
    lanes = others[0].shape[1]
    if width // groups % 16 or groups % 4 or width // seqs % 128:
        groups, seqs = 1, 1
    stage = (2, groups, width // groups, width // seqs)
    size = tile_of(rows, MIDDLE)
    tile = pl.BlockSpec((size, width), lambda i: (i, 0))
    anywhere = pl.BlockSpec(memory_space=pl.ANY)
    summed = [jax.ShapeDtypeStruct((map_size + 32, width), f32), jax.ShapeDtypeStruct((lanes, width), bf16)]
    return pl.pallas_call(
        middle_kernel,
        grid=(rows // size,),
        in_specs=[tile, tile] + [fixed(o) for o in others],
        out_specs=[tile, tile, anywhere] + [pl.BlockSpec(s.shape, lambda i: (0, 0)) for s in summed],
        out_shape=[
            jax.ShapeDtypeStruct((rows, width), bf16),
            jax.ShapeDtypeStruct((rows, width), bf16),
            jax.ShapeDtypeStruct((groups, seqs, 9, width // groups, width // seqs), bf16),
        ]
        + summed,
        scratch_shapes=[
            pltpu.VMEM((size, wide), bf16),
            pltpu.VMEM((size, wide), bf16),
            pltpu.VMEM((width, wide), f32),
            pltpu.VMEM((width, wide), f32),
            pltpu.VMEM((width, width), f32),
            pltpu.VMEM((lanes, width), f32),
            pltpu.VMEM((lanes, lanes), f32),
            pltpu.VMEM(stage, bf16),
            pltpu.SemaphoreType.DMA((2, max(1, groups // 4))),
        ],
        compiler_params=pltpu.CompilerParams(vmem_limit_bytes=VMEM),
        cost_estimate=pl.CostEstimate(
            flops=2 * rows * width * (6 * wide + 3 * width), transcendentals=rows * wide, bytes_accessed=rows * width * 12
        ),
        name="middle",
    )(x, att, *others)


def finish_kernel(place, x, g1, vec, weight, *refs):
    grads, (grad_in, sums) = refs[:-2], refs[-2:]
    parts = len(grads) // 3
    width = x.shape[1]

    @pl.when(pl.program_id(0) == 0)
    def _():
        sums[...] = jnp.zeros_like(sums)

    unit, scale = norm_stats(x[...].astype(f32))
    grad_act = None
    for i in range(3):
        at = 0
        for n in range(parts):
            part = grads[3 * n + i][...]
            share = part.shape[1]
            if i != 1:
                sums[2 + i // 2 : 3 + i // 2, at : at + share] += column_sums(part.astype(f32))
            more = dot(part, weight[:, i * width + at : i * width + at + share], NT)
            grad_act = more if grad_act is None else grad_act + more
            at += share
    sums[0:1] += column_sums(grad_act * unit)
    sums[1:2] += column_sums(grad_act)
    total = norm_back(unit, scale, vec[0:1], grad_act) + g1[...].astype(f32)
    grad_in[...] = total.astype(grad_in.dtype).reshape(grad_in.shape)


def finish(start, count, x, g1, vec, weight, grads, place=None, places=0):
    width = x.shape[1]
    size = tile_of(count, 256)
    begin = start // size
    tile = pl.BlockSpec((size, width), lambda i, at: (begin + i, 0))
    thin = [pl.BlockSpec((size, grad.shape[1]), lambda i, at: (begin + i, 0)) for grad in grads]
    if place is None:
        place = jnp.int32(0)
        out = (pl.BlockSpec((size, width), lambda i, at: (i, 0)), jax.ShapeDtypeStruct((count, width), bf16))
    else:
        out = (
            pl.BlockSpec((1, size, width), lambda i, at: (at[0], i, 0)),
            jax.ShapeDtypeStruct((places, count, width), f32),
        )

    def one(array):
        return pl.BlockSpec(array.shape, lambda i, at: (0, 0), pipeline_mode=pl.Buffered(1))

    return pl.pallas_call(
        finish_kernel,
        grid_spec=pltpu.PrefetchScalarGridSpec(
            num_scalar_prefetch=1,
            grid=(count // size,),
            in_specs=[tile] * 2 + [one(o) for o in (vec, weight)] + thin,
            out_specs=[out[0], pl.BlockSpec((8, width), lambda i, at: (0, 0))],
        ),
        out_shape=[out[1], jax.ShapeDtypeStruct((8, width), f32)],
        compiler_params=pltpu.CompilerParams(vmem_limit_bytes=VMEM),
        cost_estimate=pl.CostEstimate(
            flops=2 * count * width * weight.shape[1] * 2, transcendentals=0, bytes_accessed=count * width * 10
        ),
        name="finish",
    )(place.reshape(1), x, g1, vec, weight, *grads)


def shards(
    inputs,
    frame_tokens,
    clip_frames,
    norm1_gain,
    norm1_bias,
    qkv_weight,
    query_bias,
    value_bias,
    out_weight,
    out_bias,
    norm2_gain,
    norm2_bias,
    fc1_weight,
    fc1_bias,
    fc2_weight,
    fc2_bias,
    learn_gain,
    learn_bias,
    map1_weight,
    map1_bias,
    map2_weight,
    map2_bias,
    cot_pooled,
):
    clip_count, piece, width = inputs.shape
    seq_size = lax.axis_size("seq")
    position = lax.axis_index("seq")
    clip_size = lax.axis_size("clip")
    frames_here = piece // PATCH
    scaling = HEAD ** (-0.5)
    slots_all = float(clip_count * clip_size * seq_size * frames_here)
    group = seq_size // clip_count
    mine = position // group
    seat = position % group

    def route(turn):
        return [
            (s, ((s % clip_count + turn) % clip_count) * group + s // clip_count) for s in range(seq_size)
        ]

    def send(value, turn, back=False):
        pairs = route(turn)
        if back:
            pairs = [(b, a) for a, b in pairs]
        if all(a == b for a, b in pairs):
            return value
        return lax.ppermute(value, "seq", pairs)

    def scatter(whole, first=0):
        return [
            send(lax.dynamic_index_in_dim(whole, (position + turn) % clip_count, 0, False), turn)
            for turn in range(first, clip_count)
        ]

    def gather_back(parts, kind, whole=None):
        if whole is None:
            whole = jnp.zeros((clip_count,) + parts[0].shape, kind)
        for turn, part in enumerate(parts):
            if part is not None:
                home = send(part, turn, True).astype(kind)
                whole = lax.dynamic_update_index_in_dim(whole, home, (position + turn) % clip_count, 0)
        return whole

    tokens = lax.dynamic_index_in_dim(frame_tokens, mine, 0, False)
    frames = lax.dynamic_index_in_dim(clip_frames, mine, 0, False)
    rows = clip_count * piece
    keys = group * rows
    split = piece % 16 == 0 and group == 1 and clip_count == 2
    near = piece // TILE * TILE
    cot = jnp.concatenate(scatter(cot_pooled), axis=0).reshape(clip_count * frames_here * NTOK, width)

    def placed(ids, at_seat):
        turn = ids // piece
        source = clip_count * at_seat + (mine - turn) % clip_count
        local = ids - turn * piece
        frame = local // PATCH
        slot = local - frame * PATCH
        return (source * frames_here + frame < frames) & (slot < tokens)

    key_ids = jnp.arange(keys, dtype=jnp.int32)
    key_inside = placed(key_ids % rows, key_ids // rows)
    key_mask = jnp.where(key_inside, 0.0, masked_score)
    lane = jnp.arange(128)[None, :]
    kaug = jnp.where(lane < 3, 1.0, jnp.where(lane == 3, key_mask[:, None], 0.0)).astype(bf16)
    sub16 = jnp.arange(16)[:, None]
    wide_mask = jnp.pad(key_mask, (0, up(keys, TILE) - keys), constant_values=masked_score)
    kaug_t = jnp.where(sub16 < 3, 1.0, jnp.where(sub16 == 3, wide_mask[None, :], 0.0)).astype(bf16)
    vec = jnp.concatenate(
        [
            norm1_gain,
            norm1_bias,
            out_bias,
            norm2_gain,
            norm2_bias,
            fc2_bias,
            learn_gain,
            learn_bias,
            query_bias,
            value_bias,
            fc1_bias,
        ]
    ).reshape(-1, width)
    begun = ()
    if split:
        (x_far,) = scatter(inputs, 1)
        held = project(0, rows, inputs, position % clip_count, vec, qkv_weight)
        held, begun = lax.optimization_barrier((held, (attend_near(near, held[0], kaug),)))
        mixed, act1, x_low = project(piece, rows, x_far[None], jnp.int32(0), vec, qkv_weight, held)
    else:
        x_all = jnp.concatenate(scatter(inputs), axis=0)[None]
        mixed, act1, x_low = project(0, rows, x_all, jnp.int32(0), vec, qkv_weight)
    if group == 1:
        keys_values, act_keys = mixed, act1
    else:
        both = lax.all_gather(mixed[:, width:], "seq", axis=0, tiled=True)
        keys_values = lax.dynamic_slice_in_dim(both, mine * keys, keys, 0)
        act_keys = lax.all_gather(act1, "seq", axis=0, tiled=True)
        act_keys = lax.dynamic_slice_in_dim(act_keys, mine * keys, keys, 0)
    att, aq = attend(mixed, keys_values, kaug, *begun)

    slots = clip_count * frames_here * NTOK
    lanes = -(-slots // 128) * 128
    pair_count = NTOK * (NTOK - 1)
    lane_ids = jnp.arange(lanes)
    lane_turn = lane_ids // (frames_here * NTOK)
    lane_frame = lane_ids // NTOK - lane_turn * frames_here
    lane_source = clip_count * seat + (mine - lane_turn) % clip_count
    lane_open = (lane_source * frames_here + lane_frame < frames) & (lane_ids < slots)
    inverse = lax.rsqrt(tokens.astype(f32))
    factor = 2.0 / pair_count * inverse * inverse / slots_all
    map_size = map1_bias.shape[0]
    aux = jnp.stack(
        [
            jnp.where(lane_open, tokens, 0).astype(f32),
            jnp.full((lanes,), inverse),
            jnp.full((lanes,), factor),
            jnp.tile(map2_bias, lanes // NTOK),
            jnp.pad(map1_bias, (0, lanes - map_size)),
        ]
        + [jnp.zeros((lanes,), f32)] * 3
    )
    map1_wide = jnp.pad(map1_weight, ((0, 0), (0, lanes - map_size)))
    map2_wide = jnp.pad(jnp.tile(map2_weight, (1, lanes // NTOK)), ((0, lanes - map_size), (0, 0)))
    cot = jnp.pad(cot, ((0, lanes - slots), (0, 0)))
    grad_att, grad_low, weight_part, early, pooled = middle(
        clip_size,
        seq_size,
        map_size,
        x_low,
        att,
        aux,
        vec,
        out_weight,
        fc1_weight,
        fc2_weight,
        map1_wide,
        map2_wide,
        cot,
    )

    def over_clip(matrix):
        return lax.psum_scatter(matrix, "clip", scatter_dimension=0, tiled=True)

    def bits(size):
        return [1 << n for n in range(size.bit_length() - 1)]

    clip_steps = [("clip", bit) for bit in bits(clip_size)]
    seq_steps = [("seq", bit) for bit in bits(seq_size)]
    early_steps = clip_steps[:1] + seq_steps + clip_steps[1:]

    def meet(value, step):
        axis, bit = step
        return lax.ppermute(value, axis, [(i, i ^ bit) for i in range(lax.axis_size(axis))])

    def part_ways(blocks, step):
        axis, bit = step
        halves = blocks.reshape((-1, 2) + blocks.shape[1:])
        side = (lax.axis_index(axis) // bit) % 2
        away = lax.dynamic_index_in_dim(halves, 1 - side, 1, False)
        return lax.dynamic_index_in_dim(halves, side, 1, False), meet(away, step)

    def add_low(kept, received):
        return (kept.astype(f32) + received.astype(f32)).astype(bf16)

    def back(start, pairs, source):
        return attend_back(
            start, pairs, source, keys_values if group > 1 else source, grad_att, att, aq, act1, act_keys, kaug_t
        )

    tie = lax.optimization_barrier
    pairs = (4, 2)
    share = width // clip_size
    thin = width // seq_size
    if weight_part.shape[0] == 1:
        fc1_part = weight_part[0, 0, :4].transpose(1, 0, 2).reshape(clip_size, share, seq_size, 4, thin)
        fc2_part = weight_part[0, 0, 4:8].reshape(clip_size, 4, share, seq_size, thin).transpose(0, 3, 1, 2, 4)
        out_part = weight_part[0, 0, 8].reshape(clip_size, 1, share, seq_size, thin).transpose(0, 3, 1, 2, 4)
        weight_part = jnp.concatenate([fc1_part.transpose(0, 2, 3, 1, 4), fc2_part, out_part], axis=2)
    slab = over_clip(weight_part)[0]
    near_early = meet(early, early_steps[0])
    back0 = back(0, pairs[0], mixed)
    mixed, slab, early, near_early, pooled, back0 = tie((mixed, slab, early, near_early, pooled, back0))
    early = early + near_early
    near_early = meet(early, early_steps[1])
    slab = lax.psum_scatter(slab, "seq", scatter_dimension=0, tiled=False)
    slab0 = over_clip(back0[3])
    pooled = pooled[:slots].reshape(clip_count, frames_here, NTOK, width)
    pooled = [send(pooled[t], t, True) for t in range(clip_count)]
    back1 = back(pairs[0], pairs[1], mixed)
    slab, slab0, early, near_early, pooled, back1 = tie((slab, slab0, early, near_early, pooled, back1))
    early = early + near_early
    grads = [list(one[:3]) for one in (back0, back1)]
    if group > 1:
        both = jnp.zeros((seq_size * rows, 2 * width), bf16)
        both = lax.dynamic_update_slice_in_dim(
            both, jnp.concatenate([one[i] for i in (1, 2) for one in grads], axis=1), mine * keys, 0
        )
        both = lax.psum_scatter(both, "seq", scatter_dimension=0, tiled=True)
        at = 0
        for i in (1, 2):
            for n in range(2):
                grads[n][i] = both[:, at : at + pairs[n] * 128]
                at += pairs[n] * 128
    grads = [grad for one in grads for grad in one]
    rest = (grad_low, vec, qkv_weight, grads)
    if split:
        size = tile_of(piece, 256)
        lead = 2 * size if piece > 2 * size else size
        far0, sums0 = finish(piece, lead, x_low, *rest)
        home0 = send(far0, 1, True)
        far0, x_low = tie((far0, x_low))
        far1, sums1 = finish(piece + lead, piece - lead, x_low, *rest)
        home1 = send(far1, 1, True)
        x_low, home0, far1, early, slab1 = tie((x_low, home0, far1, early, back1[3]))
    else:
        slab1 = back1[3]
    near_early = meet(early, early_steps[2])
    kept, received = part_ways(slab1.reshape(clip_size, share, -1), clip_steps[0])
    if split:
        input_grad, late = finish(0, piece, x_low, *rest, place=position % clip_count, places=clip_count)
        input_grad, late, near_early, received, slab, slab0, pooled = tie(
            (input_grad, late, near_early, received, slab, slab0, pooled)
        )
        other = (position + 1) % clip_count
        input_grad = lax.dynamic_update_slice(input_grad, home0.astype(f32)[None], (other, 0, 0))
        late = late + sums0 + sums1
    else:
        local, late = finish(0, rows, x_low, *rest)
        input_grad = gather_back([local[t * piece : (t + 1) * piece] for t in range(clip_count)], f32)
    early = early + near_early
    for step in early_steps[3:]:
        early = early + meet(early, step)
    slab1 = add_low(kept, received)
    for step in clip_steps[1:]:
        slab1 = add_low(*part_ways(slab1, step))
    late = late[:4]
    for first, *second in zip(clip_steps[::2], clip_steps[1::2]):
        low, high = first[1], second[0][1]
        near_sum = late + meet(late, ("clip", low))
        late = near_sum + (meet(late, ("clip", high)) + meet(late, ("clip", low + high)))
    if len(clip_steps) % 2:
        late = late + meet(late, clip_steps[-1])

    fc1_grad = slab[:4].transpose(1, 0, 2).reshape(share, 4 * thin).astype(f32)
    fc2_grad = slab[4:8].reshape(4 * share, thin).astype(f32)
    out_grad = slab[8].astype(f32)
    pooled = jnp.stack(pooled)[(jnp.arange(clip_count) - position) % clip_count]
    small = early[6]
    map1_grad = early[16 : 16 + map_size].T
    map2_grad = early[16 + map_size :, : map_size // 16 * lanes].reshape(16, map_size // 16, lanes // NTOK, NTOK)
    map2_grad = jnp.sum(map2_grad, axis=2).transpose(1, 0, 2).reshape(map_size, NTOK)
    map2_bias_grad = jnp.sum(small[128:256].reshape(-1, NTOK), axis=0)
    penalty = jnp.sum(small[256:384]) / pair_count / slots_all
    done = (
        [fc1_grad, fc2_grad, out_grad, pooled, map1_grad, map2_grad, map2_bias_grad, penalty, small[:map_size]]
        + [early[n] for n in range(6)]
        + [early[8:12].reshape(-1)]
    )
    qkv = [
        part.reshape(share, count, 3, 128).transpose(0, 2, 1, 3) for part, count in zip((slab0, slab1), pairs)
    ]
    qkv = jnp.concatenate(qkv, axis=2).reshape(share, seq_size, -1).transpose(1, 0, 2)
    if split:
        home1, late, qkv, done = tie((home1, late, qkv, done))
    for step in seq_steps:
        late = late + meet(late, step)
    for step in seq_steps:
        qkv = add_low(*part_ways(qkv, step))
    qkv_grad = qkv[0].astype(f32)
    if split:
        input_grad = lax.dynamic_update_slice(input_grad, home1.astype(f32)[None], (other, lead, 0))
    fc1_grad, fc2_grad, out_grad, pooled, map1_grad, map2_grad, map2_bias_grad, penalty, map1_bias_grad = done[:9]
    early = done[9:15]
    fc1_bias_grad = done[15]
    return (
        pooled,
        penalty,
        input_grad,
        late[0],
        late[1],
        qkv_grad,
        late[2],
        late[3],
        out_grad,
        early[0],
        early[1],
        early[2],
        fc1_grad,
        fc1_bias_grad,
        fc2_grad,
        early[3],
        early[4],
        early[5],
        map1_grad,
        map1_bias_grad,
        map2_grad,
        map2_bias_grad,
    )


def solution(mesh):
    row_spec = P("clip", "seq", None)
    pool_spec = P("clip", "seq", None, None)
    matrix_spec = P("clip", "seq")
    in_specs = (row_spec, P("clip"), P("clip")) + (P(),) * 19 + (pool_spec,)
    out_specs = (
        (pool_spec, P(), row_spec, P(), P(), matrix_spec, P(), P(), matrix_spec, P(), P(), P(), matrix_spec, P())
        + (matrix_spec,)
        + (P(),) * 7
    )
    return jax.shard_map(shards, mesh=mesh, in_specs=in_specs, out_specs=out_specs, check_vma=False)
```

```python
import jax
import jax.numpy as jnp
from jax import lax
from jax.experimental import pallas as pl
from jax.experimental.pallas import tpu as pltpu
from jax.sharding import PartitionSpec as P

HEADS = 12
HEAD = 64
NTOK = 8
PATCH = 196
TILE = 256
AHEAD = 0
MIDDLE = 448
LOG2E = 1.4426950408889634
LN2 = 0.6931471805599453
VMEM = 60 * 1024 * 1024

epsilon = 1e-06
masked_score = -1e30
bf16 = jnp.bfloat16
f32 = jnp.float32

NN = (((1,), (0,)), ((), ()))
NT = (((1,), (1,)), ((), ()))


def dot(left, right, dims=NN):
    return lax.dot_general(left, right, dims, preferred_element_type=f32)


def split3(value):
    hi = value.astype(bf16).astype(f32)
    mid = (value - hi).astype(bf16).astype(f32)
    return hi, mid, value - hi - mid


def up(count, unit):
    return -(-count // unit) * unit


def tile_of(count, most):
    return max(size for size in range(16, most + 1, 16) if count % size == 0)


def blocks_of(count, unit):
    return [(base, min(unit, count - base)) for base in range(0, count, unit)]


def flip(value):
    return jnp.concatenate([value[base : base + size].T for base, size in blocks_of(value.shape[0], 128)], axis=1)


def spread_heads(source, held, aug):
    count = source.shape[0]
    zero = jnp.zeros((HEAD, held.shape[2]), bf16)
    for j in range(2):
        other = (1 - j) * HEAD
        held[j, other : other + HEAD] = zero
        if held.shape[2] > count:
            edge = count // 128 * 128
            held[j, j * HEAD : (j + 1) * HEAD, edge:] = jnp.zeros((HEAD, held.shape[2] - edge), bf16)
        held[j, 128:256] = aug(j)
    for base, size in blocks_of(count, 256):
        flat = flip(source[base : base + size])
        for j in range(2):
            held[j, j * HEAD : (j + 1) * HEAD, base : base + size] = flat[j * HEAD : (j + 1) * HEAD]


def spread_queries(q, qp):
    ids = lax.broadcasted_iota(jnp.int32, (128, qp.shape[2]), 0)
    spread_heads(q, qp, lambda j: jnp.where(ids == 3, 1.0, 0.0).astype(bf16))


def flip_into(source, target):
    for base, size in blocks_of(source.shape[0], 256):
        target[:, base : base + size] = flip(source[base : base + size])


def key_block(k, kaug, base, size):
    return jnp.concatenate([k[pl.ds(base, size), :], kaug[pl.ds(base, size), :]], axis=1)


def value_block(vt, j, base, size):
    ones = jnp.ones((16, size), bf16)
    return jnp.concatenate([vt[j * HEAD : (j + 1) * HEAD, pl.ds(base, size)], ones], axis=0)


def over_tiles(step, begin, count):
    @pl.loop(begin // TILE, count // TILE, unroll=3)
    def _(t):
        step(pl.multiple_of(t * TILE, TILE), TILE)

    if count % TILE:
        step(count // TILE * TILE, count % TILE)


def fold_tile(k, kaug, qp, vt, acc, low, fresh, base, size):
    for j in range(2):
        p = jnp.exp2(dot(key_block(k, kaug, base, size), qp[j, :, low:])).astype(bf16)
        part = dot(value_block(vt, j, base, size), p)
        if fresh:
            acc[j, :, low:] = part
        else:
            acc[j, :, low:] += part


def attend_near_kernel(q, k, v, kaug, acc, qp, vt):
    spread_queries(q, qp)
    flip_into(v, vt)
    fold_tile(k, kaug, qp, vt, acc, 0, True, 0, TILE)
    over_tiles(lambda base, size: fold_tile(k, kaug, qp, vt, acc, 0, False, base, size), TILE, k.shape[0])


def attend_near(near, mixed, kaug):
    pairs = HEADS // 2
    return pl.pallas_call(
        attend_near_kernel,
        grid=(pairs,),
        in_specs=[
            pl.BlockSpec((near, 128), lambda h: (0, h)),
            pl.BlockSpec((near, 128), lambda h: (0, pairs + h)),
            pl.BlockSpec((near, 128), lambda h: (0, 2 * pairs + h)),
            pl.BlockSpec((near, 128), lambda h: (0, 0)),
        ],
        out_specs=pl.BlockSpec((2, HEAD + 16, near), lambda h: (h, 0, 0)),
        out_shape=jax.ShapeDtypeStruct((HEADS, HEAD + 16, near), f32),
        scratch_shapes=[pltpu.VMEM((2, 256, near), bf16), pltpu.VMEM((128, near), bf16)],
        compiler_params=pltpu.CompilerParams(vmem_limit_bytes=VMEM),
        cost_estimate=pl.CostEstimate(
            flops=4 * HEADS * near * near * 256, transcendentals=HEADS * near * near, bytes_accessed=near * 768 * 10
        ),
        name="attend_near",
    )(mixed, mixed, mixed, kaug)


def attend_kernel(q, k, v, kaug, *refs):
    att, aq, qp, vt, acc = refs[-5:]
    rows = q.shape[0]
    keys = k.shape[0]
    wide = qp.shape[2]
    spread_queries(q, qp)
    flip_into(v, vt)

    def fold(low, fresh):
        return lambda base, size: fold_tile(k, kaug, qp, vt, acc, low, fresh, base, size)

    begun = 0
    if len(refs) > 5:
        begun = refs[0].shape[2]
        acc[:, :, :begun] = refs[0][...]
    fold(begun, True)(0, TILE)
    if begun:
        over_tiles(fold(begun, False), TILE, begun)
    over_tiles(fold(0, False), max(begun, TILE), keys)

    for j in range(2):
        total = acc[j, HEAD : HEAD + 1]
        fine = (total > 2.0**-60) & (total < 2.0**60)
        bad = jnp.max(jnp.where(fine, 0.0, 1.0)) > 0.5
        acc[j, HEAD + 8 : HEAD + 9] = jnp.zeros((1, wide), f32)

        @pl.when(bad)
        def _():
            acc[j, 0:1] = jnp.full((1, wide), -1e38, f32)

            def largest(base, size):
                s = dot(key_block(k, kaug, base, size), qp[j])
                acc[j, 0:1] = jnp.maximum(acc[j, 0:1], jnp.max(s, axis=0, keepdims=True))

            over_tiles(largest, 0, keys)
            best = acc[j, 0:1]
            acc[j] = jnp.zeros((HEAD + 16, wide), f32)

            def again(base, size):
                p = jnp.exp2(dot(key_block(k, kaug, base, size), qp[j]) - best).astype(bf16)
                acc[j] += dot(value_block(vt, j, base, size), p)

            over_tiles(again, 0, keys)
            acc[j, HEAD + 8 : HEAD + 9] = best

    ids = lax.broadcasted_iota(jnp.int32, (HEAD, 128), 0)
    for base, size in blocks_of(rows, 128):
        here = slice(base, base + 128)
        outs = []
        augs = []
        for j in range(2):
            total = acc[j, HEAD : HEAD + 1, here]
            outs.append(acc[j, 0:HEAD, here] * (1.0 / total))
            lse = jnp.log2(total) + acc[j, HEAD + 8 : HEAD + 9, here]
            hi, mid, low = split3(-lse)
            aug = jnp.where(ids == 0, hi, jnp.where(ids == 1, mid, jnp.where(ids == 2, low, 0.0)))
            augs.append(jnp.where(ids == 3, 1.0, aug))
        att[base : base + size, :] = jnp.concatenate(outs, axis=0).T[:size].astype(bf16)
        aq[base : base + size, :] = jnp.concatenate(augs, axis=0).T[:size].astype(bf16)


def attend(mixed, keys_values, kaug, *begun):
    rows = mixed.shape[0]
    keys = keys_values.shape[0]
    pairs = HEADS // 2
    wide = up(rows, 128)
    first = keys_values.shape[1] // 128 - 2 * pairs
    return pl.pallas_call(
        attend_kernel,
        grid=(pairs,),
        in_specs=[
            pl.BlockSpec((rows, 128), lambda h: (0, h)),
            pl.BlockSpec((keys, 128), lambda h: (0, first + h)),
            pl.BlockSpec((keys, 128), lambda h: (0, first + pairs + h)),
            pl.BlockSpec((keys, 128), lambda h: (0, 0)),
        ]
        + [pl.BlockSpec((2,) + one.shape[1:], lambda h: (h, 0, 0)) for one in begun],
        out_specs=[
            pl.BlockSpec((rows, 128), lambda h: (0, h)),
            pl.BlockSpec((rows, 128), lambda h: (0, h)),
        ],
        out_shape=[
            jax.ShapeDtypeStruct((rows, HEADS * HEAD), bf16),
            jax.ShapeDtypeStruct((rows, HEADS * HEAD), bf16),
        ],
        scratch_shapes=[
            pltpu.VMEM((2, 256, wide), bf16),
            pltpu.VMEM((128, up(keys, 128)), bf16),
            pltpu.VMEM((2, HEAD + 16, wide), f32),
        ],
        compiler_params=pltpu.CompilerParams(vmem_limit_bytes=VMEM),
        cost_estimate=pl.CostEstimate(
            flops=4 * HEADS * rows * keys * 256, transcendentals=HEADS * rows * keys, bytes_accessed=rows * 768 * 10
        ),
        name="attend",
    )(mixed, keys_values, keys_values, kaug, *begun)


def attend_back_kernel(q, do, att, aq, k, v, act_rows, act_keys, kaug_t, dq, dk, dv, weight_grad, kp, vp, dkt, dvt, dqs):
    step = pl.program_id(1)
    rows = q.shape[0]
    keys = k.shape[0]
    tiles = up(keys, TILE) // TILE

    @pl.when(step == 0)
    def _():
        rest = jnp.zeros((HEAD - 16, kp.shape[2]), bf16)
        zero = jnp.zeros((HEAD, kp.shape[2]), bf16)
        halves = (jnp.concatenate([kaug_t[...], rest, zero], axis=0), jnp.concatenate([zero, kaug_t[...], rest], axis=0))
        for source, held in ((k, kp), (v, vp)):
            spread_heads(source, held, lambda j: halves[j])
        dkt[...] = jnp.zeros_like(dkt)
        dvt[...] = jnp.zeros_like(dvt)

    units = [(j, t) for j in range(2) for t in range(tiles)]
    count = len(units)
    totals = [None, None]
    qa = jnp.concatenate([q[...], aq[...]], axis=1)

    def cols(t):
        return slice(t * TILE, (t + 1) * TILE)

    def scores(i):
        j, t = units[i]
        return dot(qa, kp[j, :, cols(t)])

    def weigh(s, dp):
        p = jnp.exp2(s)
        return p.astype(bf16), (p * dp).astype(bf16)

    def collect(j, t, p, ds):
        part = slice(j * HEAD, (j + 1) * HEAD)
        dvt[part, cols(t)] += dot(dot_[part], p)
        dkt[part, cols(t)] += dot(qt[part], ds)
        more = dot(ds[:, : min(TILE, keys - t * TILE)], k[t * TILE : min(keys, (t + 1) * TILE), :])
        totals[j] = more if totals[j] is None else totals[j] + more

    ahead = AHEAD
    raw = {i: scores(i) for i in range(min(ahead, count))}
    lane = lax.broadcasted_iota(jnp.int32, (rows, 128), 1)
    product = do[...].astype(f32) * att[...].astype(f32)
    inner0 = jnp.sum(jnp.where(lane < HEAD, product, 0.0), axis=1, keepdims=True)
    inner1 = jnp.sum(jnp.where(lane < HEAD, 0.0, product), axis=1, keepdims=True)
    hi, mid, low = split3(-jnp.where(lane < HEAD, inner0, inner1))
    within = lane % HEAD
    ado = jnp.where(within == 0, hi, jnp.where(within == 1, mid, jnp.where(within == 2, low, 0.0))).astype(bf16)
    da = jnp.concatenate([do[...], ado], axis=1)
    ready = {}
    for i in range(count + 2):
        if i < count:
            j, t = units[i]
            s = raw.pop(i) if i in raw else scores(i)
            raw[i] = (s, dot(da, vp[j, :, cols(t)]))
        if i == 1:
            qt = flip(q[...])
            dot_ = flip(do[...])
        if 0 <= i - 1 < count:
            ready[i - 1] = weigh(*raw.pop(i - 1))
        if 0 <= i - 2 < count:
            collect(*units[i - 2], *ready.pop(i - 2))
    grad_q = (jnp.where(lane < HEAD, totals[0], totals[1]) * HEAD ** (-0.5)).astype(bf16)
    dq[...] = grad_q
    dqs[pl.ds(pl.multiple_of(step * rows, 16), rows), :] = grad_q

    @pl.when(step == pl.num_programs(1) - 1)
    def _():
        total = jnp.zeros((128, act_rows.shape[1]), f32)
        for base, size in blocks_of(dqs.shape[0], TILE):
            total += dot(flip(dqs[base : base + size]), act_rows[base : base + size])
        weight_grad[:, 0:128] = total.T.astype(bf16)
        total = jnp.zeros((256, act_rows.shape[1]), f32)
        for base, size in blocks_of(keys, TILE):
            grad_k = (dkt[:, base : base + size] * LN2).astype(bf16)
            grad_v = dvt[:, base : base + size].astype(bf16)
            dk[base : base + size] = grad_k.T
            dv[base : base + size] = grad_v.T
            total += dot(jnp.concatenate([grad_k, grad_v], axis=0), act_keys[base : base + size])
        weight_grad[:, 128:384] = total.T.astype(bf16)


def attend_back(start, pairs, mixed, keys_values, grad_att, att, aq, act, act_keys, kaug_t):
    rows, width = act.shape
    keys = keys_values.shape[0]
    wide = up(keys, TILE)
    size = tile_of(rows, 512)
    first = keys_values.shape[1] // 128 - HEADS
    here = pl.BlockSpec((size, 128), lambda h, r: (r, start + h))
    whole = pl.BlockSpec((keys, 128), lambda h, r: (0, h))
    return pl.pallas_call(
        attend_back_kernel,
        grid=(pairs, rows // size),
        in_specs=[
            here,
            here,
            here,
            here,
            pl.BlockSpec((keys, 128), lambda h, r: (0, first + start + h)),
            pl.BlockSpec((keys, 128), lambda h, r: (0, first + HEADS // 2 + start + h)),
            pl.BlockSpec((rows, width), lambda h, r: (0, 0), pipeline_mode=pl.Buffered(1)),
            pl.BlockSpec((keys, width), lambda h, r: (0, 0), pipeline_mode=pl.Buffered(1)),
            pl.BlockSpec((16, wide), lambda h, r: (0, 0), pipeline_mode=pl.Buffered(1)),
        ],
        out_specs=[
            pl.BlockSpec((size, 128), lambda h, r: (r, h)),
            whole,
            whole,
            pl.BlockSpec((width, 384), lambda h, r: (0, h)),
        ],
        out_shape=[
            jax.ShapeDtypeStruct((rows, pairs * 128), bf16),
            jax.ShapeDtypeStruct((keys, pairs * 128), bf16),
            jax.ShapeDtypeStruct((keys, pairs * 128), bf16),
            jax.ShapeDtypeStruct((width, pairs * 384), bf16),
        ],
        scratch_shapes=[
            pltpu.VMEM((2, 256, wide), bf16),
            pltpu.VMEM((2, 256, wide), bf16),
            pltpu.VMEM((128, wide), f32),
            pltpu.VMEM((128, wide), f32),
            pltpu.VMEM((rows, 128), bf16),
        ],
        compiler_params=pltpu.CompilerParams(vmem_limit_bytes=VMEM),
        cost_estimate=pl.CostEstimate(
            flops=20 * pairs * rows * keys * 200, transcendentals=2 * pairs * rows * keys, bytes_accessed=rows * 768 * 20
        ),
        name="attend_back",
    )(mixed, grad_att, att, aq, keys_values, keys_values, act, act_keys, kaug_t)


def norm_stats(value):
    average = jnp.mean(value, axis=-1, keepdims=True)
    centered = value - average
    variance = jnp.mean(centered * centered, axis=-1, keepdims=True)
    scale = lax.rsqrt(variance + epsilon)
    return centered * scale, scale


def norm_back(unit, scale, gain, grad):
    inner = grad * gain
    along = jnp.mean(inner * unit, axis=-1, keepdims=True)
    return scale * (inner - jnp.mean(inner, axis=-1, keepdims=True) - unit * along)


def gelu_pair(value):
    size = jnp.abs(value)
    bell = jnp.exp2(value * value * (-0.5 * LOG2E))
    base = 1.0 + 0.231641888 * size
    t = pl.reciprocal(base, approx=True)
    t = t * (2.0 - base * t)
    fit = t * (0.127414796 + t * (-0.142248368 + t * (0.7107068705 + t * (-0.7265760135 + t * 0.5307027145))))
    tail = fit * bell
    share = jnp.where(value >= 0.0, 1.0 - tail, tail)
    return value * share, share + value * (bell * 0.3989422804014327)


def column_sums(grad):
    return jnp.sum(grad, axis=0, keepdims=True)


def project_kernel(place, x, vec, weight, *refs):
    mixed, act_out, x_out = refs[-3:]
    width = vec.shape[1]
    rows = x[0]
    x_out[...] = rows
    unit, _ = norm_stats(rows.astype(f32))
    act = (unit * vec[0:1] + vec[1:2]).astype(bf16)
    act_out[...] = act
    total = dot(act, weight[...])
    mixed[:, :width] = ((total[:, :width] + vec[8:9]) * (HEAD ** (-0.5) * LOG2E)).astype(bf16)
    mixed[:, width : 2 * width] = total[:, width : 2 * width].astype(bf16)
    mixed[:, 2 * width :] = (total[:, 2 * width :] + vec[9:10]).astype(bf16)


def fixed(array):
    return pl.BlockSpec(array.shape, lambda i: (0,) * array.ndim, pipeline_mode=pl.Buffered(1))


def project(start, total, x, place, vec, weight, held=()):
    _, count, width = x.shape
    cols = weight.shape[1]
    sizes = (cols, width, width)
    tile = tile_of(count, 256)

    def one(array):
        return pl.BlockSpec(array.shape, lambda i, at: (0, 0), pipeline_mode=pl.Buffered(1))

    return pl.pallas_call(
        project_kernel,
        grid_spec=pltpu.PrefetchScalarGridSpec(
            num_scalar_prefetch=1,
            grid=(count // tile,),
            in_specs=[pl.BlockSpec((1, tile, width), lambda i, at: (at[0], i, 0)), one(vec), one(weight)]
            + [pl.BlockSpec(memory_space=pl.ANY) for _ in held],
            out_specs=[pl.BlockSpec((tile, size), lambda i, at: (start // tile + i, 0)) for size in sizes],
        ),
        out_shape=[jax.ShapeDtypeStruct((total, size), bf16) for size in sizes],
        input_output_aliases={4 + i: i for i in range(len(held))},
        compiler_params=pltpu.CompilerParams(vmem_limit_bytes=VMEM),
        name="project",
    )(place.reshape(1), x, vec, weight, *held)


def middle_kernel(
    x, att, aux, vec, wo, w1, w2, m1, m2, cot, grad_att, grad_low, weight_grads, sums, pooled_out,
    hidden, slope, acc1, acc2, acco, pooled, map2g, stage, sems,
):
    step = pl.program_id(0)
    rows, width = x.shape
    wide = w1.shape[1]
    part = wide // 4
    map_size = sums.shape[0] - 32
    bias_o, gain2, bias2, bias_2, gain3, bias3 = [vec[n : n + 1] for n in range(2, 8)]

    @pl.when(step == 0)
    def _():
        for ref in (sums, pooled, map2g, acc1, acc2, acco):
            ref[...] = jnp.zeros_like(ref)

    att_low = att[...]
    resid1 = x[...].astype(f32) + dot(att_low, wo[...]) + bias_o
    unit2, scale2 = norm_stats(resid1)
    act2 = (unit2 * gain2 + bias2).astype(bf16)
    total = None
    for c in range(4):
        cols = slice(c * part, (c + 1) * part)
        value, rate = gelu_pair(dot(act2, w1[:, cols]) + vec[10 + c : 11 + c])
        value = value.astype(bf16)
        hidden[:, cols] = value
        slope[:, cols] = rate.astype(bf16)
        more = dot(value, w2[cols, :])
        total = more if total is None else total + more
    resid2 = resid1 + total + bias_2
    output_low = resid2.astype(bf16)
    grad_gate = dot(output_low, cot[...], NT)
    unit3, scale3 = norm_stats(resid2)
    act3 = (unit3 * gain3 + bias3).astype(bf16)
    map_hidden, map_slope = gelu_pair(dot(act3, m1[...]) + aux[4:5])
    map_hidden = map_hidden.astype(bf16)
    logits = dot(map_hidden, m2[...]) + aux[3:4]
    lanes = logits.shape[1]
    lane = lax.broadcasted_iota(jnp.int32, (rows, lanes), 1)
    row = lax.broadcasted_iota(jnp.int32, (rows, lanes), 0) + step * rows
    slot = row - (lane >> 3) * PATCH
    mask = (slot >= 0) & (slot.astype(f32) < aux[0:1])
    inverse = aux[1:2]
    raw = 1.0 / (1.0 + jnp.exp2(logits * (-LOG2E)))
    gates = jnp.where(mask, raw, 0.0)
    gates_low = gates.astype(bf16)
    pooled[...] += dot(gates_low.T, output_low)
    gate_sum = jnp.sum(gates, axis=1, keepdims=True)
    inverse_row = inverse[:, 0:1]
    sums[6:7, 256:384] += column_sums(gates * (gate_sum - gates)) * (inverse * inverse)

    grad_out = dot(gates_low, cot[...]) * inverse_row
    grad_gate = grad_gate * inverse + aux[2:3] * (gate_sum - gates)
    grad_logit = jnp.where(mask, grad_gate * raw * (1.0 - raw), 0.0)
    sums[6:7, 128:256] += column_sums(grad_logit)
    grad_logit = grad_logit.astype(bf16)
    map2g[...] += dot(map_hidden.T, grad_logit)
    grad_mpre = dot(grad_logit, m2[...], NT) * map_slope
    sums[6:7, 0:128] += column_sums(grad_mpre)
    grad_mpre = grad_mpre.astype(bf16)
    sums[16 : 16 + map_size] += dot(grad_mpre.T[:map_size], act3)
    grad_act = dot(grad_mpre, m1[...], NT)
    sums[4:5] += column_sums(grad_act * unit3)
    sums[5:6] += column_sums(grad_act)
    grad_res2 = norm_back(unit3, scale3, gain3, grad_act) + grad_out

    sums[3:4] += column_sums(grad_res2)
    g2 = grad_res2.astype(bf16)
    g2_t = g2.T
    act2_t = act2.T
    grad_act = None
    for c in range(4):
        cols = slice(c * part, (c + 1) * part)
        grad_pre = dot(g2, w2[cols, :], NT) * slope[:, cols].astype(f32)
        sums[8 + c : 9 + c] += column_sums(grad_pre)
        grad_pre = grad_pre.astype(bf16)
        slope[:, cols] = grad_pre
        more = dot(grad_pre, w1[:, cols], NT)
        grad_act = more if grad_act is None else grad_act + more
    for c in range(4):
        cols = slice(c * part, (c + 1) * part)
        acc1[:, cols] += dot(act2_t, slope[:, cols])
        acc2[:, cols] += dot(g2_t, hidden[:, cols])
    sums[1:2] += column_sums(grad_act * unit2)
    sums[2:3] += column_sums(grad_act)
    grad_res1 = norm_back(unit2, scale2, gain2, grad_act) + grad_res2

    sums[0:1] += column_sums(grad_res1)
    g1 = grad_res1.astype(bf16)
    grad_low[...] = g1
    acco[...] += dot(att_low.T, g1)
    grad_att[...] = dot(g1, wo[...], NT).astype(bf16)

    @pl.when(step == pl.num_programs(0) - 1)
    def _():
        groups, seqs, _, share, thin = weight_grads.shape
        pending = [[], []]
        count = 0

        def drain(value, *targets):
            nonlocal count
            slot = count % 2
            count += 1
            for copy in pending[slot]:
                copy.wait()
            stage[slot] = value.astype(bf16).reshape(stage.shape[1:])
            pending[slot] = [
                pltpu.make_async_copy(stage.at[slot, lo:hi], target, sems.at[slot, n])
                for n, (lo, hi, target) in enumerate(targets)
            ]
            for copy in pending[slot]:
                copy.start()

        for t in range(4 * seqs):
            drain(acc1[:, t * thin : (t + 1) * thin], (0, groups, weight_grads.at[:, t // 4, t % 4]))
        for c in range(4):
            cols = slice(c * part, (c + 1) * part)
            for s in range(seqs):
                value = acc2[s * thin : (s + 1) * thin, cols].T
                if groups == 1:
                    drain(value, (0, 1, weight_grads.at[:, s, 4 + c]))
                else:
                    few = groups // 4
                    drain(value, *[(4 * i, 4 * i + 4, weight_grads.at[c * few + i, s, 4:8]) for i in range(few)])
        for s in range(seqs):
            drain(acco[:, s * thin : (s + 1) * thin], (0, groups, weight_grads.at[:, s, 8]))
        pooled_out[...] = (pooled[...] * inverse_row).astype(bf16)
        for g in range(map_size // 16):
            sums[16 + map_size :, g * 128 : (g + 1) * 128] = map2g[g * 16 : (g + 1) * 16]
        for copy in pending[0] + pending[1]:
            copy.wait()


def middle(groups, seqs, map_size, x, att, *others):
    rows, width = x.shape
    wide = others[3].shape[1]
    lanes = others[0].shape[1]
    if width // groups % 16 or groups % 4 or width // seqs % 128:
        groups, seqs = 1, 1
    stage = (2, groups, width // groups, width // seqs)
    size = tile_of(rows, MIDDLE)
    tile = pl.BlockSpec((size, width), lambda i: (i, 0))
    anywhere = pl.BlockSpec(memory_space=pl.ANY)
    summed = [jax.ShapeDtypeStruct((map_size + 32, width), f32), jax.ShapeDtypeStruct((lanes, width), bf16)]
    return pl.pallas_call(
        middle_kernel,
        grid=(rows // size,),
        in_specs=[tile, tile] + [fixed(o) for o in others],
        out_specs=[tile, tile, anywhere] + [pl.BlockSpec(s.shape, lambda i: (0, 0)) for s in summed],
        out_shape=[
            jax.ShapeDtypeStruct((rows, width), bf16),
            jax.ShapeDtypeStruct((rows, width), bf16),
            jax.ShapeDtypeStruct((groups, seqs, 9, width // groups, width // seqs), bf16),
        ]
        + summed,
        scratch_shapes=[
            pltpu.VMEM((size, wide), bf16),
            pltpu.VMEM((size, wide), bf16),
            pltpu.VMEM((width, wide), f32),
            pltpu.VMEM((width, wide), f32),
            pltpu.VMEM((width, width), f32),
            pltpu.VMEM((lanes, width), f32),
            pltpu.VMEM((lanes, lanes), f32),
            pltpu.VMEM(stage, bf16),
            pltpu.SemaphoreType.DMA((2, max(1, groups // 4))),
        ],
        compiler_params=pltpu.CompilerParams(vmem_limit_bytes=VMEM),
        cost_estimate=pl.CostEstimate(
            flops=2 * rows * width * (6 * wide + 3 * width), transcendentals=rows * wide, bytes_accessed=rows * width * 12
        ),
        name="middle",
    )(x, att, *others)


def finish_kernel(place, x, g1, vec, weight, *refs):
    grads, (grad_in, sums) = refs[:-2], refs[-2:]
    parts = len(grads) // 3
    width = x.shape[1]

    @pl.when(pl.program_id(0) == 0)
    def _():
        sums[...] = jnp.zeros_like(sums)

    unit, scale = norm_stats(x[...].astype(f32))
    grad_act = None
    for i in range(3):
        at = 0
        for n in range(parts):
            part = grads[3 * n + i][...]
            share = part.shape[1]
            if i != 1:
                sums[2 + i // 2 : 3 + i // 2, at : at + share] += column_sums(part.astype(f32))
            more = dot(part, weight[:, i * width + at : i * width + at + share], NT)
            grad_act = more if grad_act is None else grad_act + more
            at += share
    sums[0:1] += column_sums(grad_act * unit)
    sums[1:2] += column_sums(grad_act)
    total = norm_back(unit, scale, vec[0:1], grad_act) + g1[...].astype(f32)
    grad_in[...] = total.astype(grad_in.dtype).reshape(grad_in.shape)


def finish(start, count, x, g1, vec, weight, grads, place=None, places=0):
    width = x.shape[1]
    size = tile_of(count, 256)
    begin = start // size
    tile = pl.BlockSpec((size, width), lambda i, at: (begin + i, 0))
    thin = [pl.BlockSpec((size, grad.shape[1]), lambda i, at: (begin + i, 0)) for grad in grads]
    if place is None:
        place = jnp.int32(0)
        out = (pl.BlockSpec((size, width), lambda i, at: (i, 0)), jax.ShapeDtypeStruct((count, width), bf16))
    else:
        out = (
            pl.BlockSpec((1, size, width), lambda i, at: (at[0], i, 0)),
            jax.ShapeDtypeStruct((places, count, width), f32),
        )

    def one(array):
        return pl.BlockSpec(array.shape, lambda i, at: (0, 0), pipeline_mode=pl.Buffered(1))

    return pl.pallas_call(
        finish_kernel,
        grid_spec=pltpu.PrefetchScalarGridSpec(
            num_scalar_prefetch=1,
            grid=(count // size,),
            in_specs=[tile] * 2 + [one(o) for o in (vec, weight)] + thin,
            out_specs=[out[0], pl.BlockSpec((8, width), lambda i, at: (0, 0))],
        ),
        out_shape=[out[1], jax.ShapeDtypeStruct((8, width), f32)],
        compiler_params=pltpu.CompilerParams(vmem_limit_bytes=VMEM),
        cost_estimate=pl.CostEstimate(
            flops=2 * count * width * weight.shape[1] * 2, transcendentals=0, bytes_accessed=count * width * 10
        ),
        name="finish",
    )(place.reshape(1), x, g1, vec, weight, *grads)


def shards(
    inputs,
    frame_tokens,
    clip_frames,
    norm1_gain,
    norm1_bias,
    qkv_weight,
    query_bias,
    value_bias,
    out_weight,
    out_bias,
    norm2_gain,
    norm2_bias,
    fc1_weight,
    fc1_bias,
    fc2_weight,
    fc2_bias,
    learn_gain,
    learn_bias,
    map1_weight,
    map1_bias,
    map2_weight,
    map2_bias,
    cot_pooled,
):
    clip_count, piece, width = inputs.shape
    seq_size = lax.axis_size("seq")
    position = lax.axis_index("seq")
    clip_size = lax.axis_size("clip")
    frames_here = piece // PATCH
    scaling = HEAD ** (-0.5)
    slots_all = float(clip_count * clip_size * seq_size * frames_here)
    group = seq_size // clip_count
    mine = position // group
    seat = position % group

    def route(turn):
        return [
            (s, ((s % clip_count + turn) % clip_count) * group + s // clip_count) for s in range(seq_size)
        ]

    def send(value, turn, back=False):
        pairs = route(turn)
        if back:
            pairs = [(b, a) for a, b in pairs]
        if all(a == b for a, b in pairs):
            return value
        return lax.ppermute(value, "seq", pairs)

    def scatter(whole, first=0):
        return [
            send(lax.dynamic_index_in_dim(whole, (position + turn) % clip_count, 0, False), turn)
            for turn in range(first, clip_count)
        ]

    def gather_back(parts, kind, whole=None):
        if whole is None:
            whole = jnp.zeros((clip_count,) + parts[0].shape, kind)
        for turn, part in enumerate(parts):
            if part is not None:
                home = send(part, turn, True).astype(kind)
                whole = lax.dynamic_update_index_in_dim(whole, home, (position + turn) % clip_count, 0)
        return whole

    tokens = lax.dynamic_index_in_dim(frame_tokens, mine, 0, False)
    frames = lax.dynamic_index_in_dim(clip_frames, mine, 0, False)
    rows = clip_count * piece
    keys = group * rows
    split = piece % 16 == 0 and group == 1 and clip_count == 2
    near = piece // TILE * TILE
    cot = jnp.concatenate(scatter(cot_pooled), axis=0).reshape(clip_count * frames_here * NTOK, width)

    def placed(ids, at_seat):
        turn = ids // piece
        source = clip_count * at_seat + (mine - turn) % clip_count
        local = ids - turn * piece
        frame = local // PATCH
        slot = local - frame * PATCH
        return (source * frames_here + frame < frames) & (slot < tokens)

    key_ids = jnp.arange(keys, dtype=jnp.int32)
    key_inside = placed(key_ids % rows, key_ids // rows)
    lane16 = jnp.arange(128)
    key_mask = jnp.where(key_inside, 0.0, masked_score)
    kaug = jnp.where(lane16[None, :] < 3, 1.0, jnp.where(lane16[None, :] == 3, key_mask[:, None], 0.0)).astype(bf16)
    sub16 = jnp.arange(16)[:, None]
    wide_mask = jnp.pad(key_mask, (0, up(keys, TILE) - keys), constant_values=masked_score)
    kaug_t = jnp.where(sub16 < 3, 1.0, jnp.where(sub16 == 3, wide_mask[None, :], 0.0)).astype(bf16)

    vec = jnp.concatenate(
        [
            norm1_gain,
            norm1_bias,
            out_bias,
            norm2_gain,
            norm2_bias,
            fc2_bias,
            learn_gain,
            learn_bias,
            query_bias,
            value_bias,
            fc1_bias,
        ]
    ).reshape(-1, width)
    begun = ()
    if split:
        (x_far,) = scatter(inputs, 1)
        held = project(0, rows, inputs, position % clip_count, vec, qkv_weight)
        held, begun = lax.optimization_barrier((held, (attend_near(near, held[0], kaug),)))
        mixed, act1, x_low = project(piece, rows, x_far[None], jnp.int32(0), vec, qkv_weight, held)
    else:
        x_all = jnp.concatenate(scatter(inputs), axis=0)[None]
        mixed, act1, x_low = project(0, rows, x_all, jnp.int32(0), vec, qkv_weight)
    if group == 1:
        keys_values, act_keys = mixed, act1
    else:
        both = lax.all_gather(mixed[:, width:], "seq", axis=0, tiled=True)
        keys_values = lax.dynamic_slice_in_dim(both, mine * keys, keys, 0)
        act_keys = lax.all_gather(act1, "seq", axis=0, tiled=True)
        act_keys = lax.dynamic_slice_in_dim(act_keys, mine * keys, keys, 0)
    att, aq = attend(mixed, keys_values, kaug, *begun)

    slots = clip_count * frames_here * NTOK
    lanes = -(-slots // 128) * 128
    pair_count = NTOK * (NTOK - 1)
    lane_ids = jnp.arange(lanes)
    lane_turn = lane_ids // (frames_here * NTOK)
    lane_frame = lane_ids // NTOK - lane_turn * frames_here
    lane_source = clip_count * seat + (mine - lane_turn) % clip_count
    lane_open = (lane_source * frames_here + lane_frame < frames) & (lane_ids < slots)
    inverse = lax.rsqrt(tokens.astype(f32))
    factor = 2.0 / pair_count * inverse * inverse / slots_all
    map_size = map1_bias.shape[0]
    aux = jnp.stack(
        [
            jnp.where(lane_open, tokens, 0).astype(f32),
            jnp.full((lanes,), inverse),
            jnp.full((lanes,), factor),
            jnp.tile(map2_bias, lanes // NTOK),
            jnp.pad(map1_bias, (0, lanes - map_size)),
        ]
        + [jnp.zeros((lanes,), f32)] * 3
    )
    map1_wide = jnp.pad(map1_weight, ((0, 0), (0, lanes - map_size)))
    map2_wide = jnp.pad(jnp.tile(map2_weight, (1, lanes // NTOK)), ((0, lanes - map_size), (0, 0)))
    cot = jnp.pad(cot, ((0, lanes - slots), (0, 0)))
    grad_att, grad_low, weight_part, early, pooled = middle(
        clip_size,
        seq_size,
        map_size,
        x_low,
        att,
        aux,
        vec,
        out_weight,
        fc1_weight,
        fc2_weight,
        map1_wide,
        map2_wide,
        cot,
    )

    def over_clip(matrix):
        return lax.psum_scatter(matrix, "clip", scatter_dimension=0, tiled=True)

    def bits(size):
        return [1 << n for n in range(size.bit_length() - 1)]

    clip_steps = [("clip", bit) for bit in bits(clip_size)]
    seq_steps = [("seq", bit) for bit in bits(seq_size)]
    early_steps = clip_steps[:1] + seq_steps + clip_steps[1:]

    def meet(value, step):
        axis, bit = step
        return lax.ppermute(value, axis, [(i, i ^ bit) for i in range(lax.axis_size(axis))])

    def part_ways(blocks, step):
        axis, bit = step
        halves = blocks.reshape((-1, 2) + blocks.shape[1:])
        side = (lax.axis_index(axis) // bit) % 2
        away = lax.dynamic_index_in_dim(halves, 1 - side, 1, False)
        return lax.dynamic_index_in_dim(halves, side, 1, False), meet(away, step)

    def add_low(kept, received):
        return (kept.astype(f32) + received.astype(f32)).astype(bf16)

    def back(start, pairs, source):
        return attend_back(
            start, pairs, source, keys_values if group > 1 else source, grad_att, att, aq, act1, act_keys, kaug_t
        )

    tie = lax.optimization_barrier
    pairs = (4, 2)
    share = width // clip_size
    thin = width // seq_size
    if weight_part.shape[0] == 1:
        fc1_part = weight_part[0, 0, :4].transpose(1, 0, 2).reshape(clip_size, share, seq_size, 4, thin)
        fc2_part = weight_part[0, 0, 4:8].reshape(clip_size, 4, share, seq_size, thin).transpose(0, 3, 1, 2, 4)
        out_part = weight_part[0, 0, 8].reshape(clip_size, 1, share, seq_size, thin).transpose(0, 3, 1, 2, 4)
        weight_part = jnp.concatenate([fc1_part.transpose(0, 2, 3, 1, 4), fc2_part, out_part], axis=2)
    slab = over_clip(weight_part)[0]
    near_early = meet(early, early_steps[0])
    back0 = back(0, pairs[0], mixed)
    mixed, slab, early, near_early, pooled, back0 = tie((mixed, slab, early, near_early, pooled, back0))
    early = early + near_early
    near_early = meet(early, early_steps[1])
    slab = lax.psum_scatter(slab, "seq", scatter_dimension=0, tiled=False)
    slab0 = over_clip(back0[3])
    pooled = pooled[:slots].reshape(clip_count, frames_here, NTOK, width)
    pooled = [send(pooled[t], t, True) for t in range(clip_count)]
    back1 = back(pairs[0], pairs[1], mixed)
    slab, slab0, early, near_early, pooled, back1 = tie((slab, slab0, early, near_early, pooled, back1))
    early = early + near_early
    grads = [list(one[:3]) for one in (back0, back1)]
    if group > 1:
        both = jnp.zeros((seq_size * rows, 2 * width), bf16)
        both = lax.dynamic_update_slice_in_dim(
            both, jnp.concatenate([one[i] for i in (1, 2) for one in grads], axis=1), mine * keys, 0
        )
        both = lax.psum_scatter(both, "seq", scatter_dimension=0, tiled=True)
        at = 0
        for i in (1, 2):
            for n in range(2):
                grads[n][i] = both[:, at : at + pairs[n] * 128]
                at += pairs[n] * 128
    grads = [grad for one in grads for grad in one]
    rest = (grad_low, vec, qkv_weight, grads)
    near_early = meet(early, early_steps[2])
    kept, received = part_ways(back1[3].reshape(clip_size, share, -1), clip_steps[0])
    if split:
        size = tile_of(piece, 256)
        lead = 2 * size if piece > 2 * size else size
        far0, sums0 = finish(piece, lead, x_low, *rest)
        far0, sums0, x_low, near_early, received = tie((far0, sums0, x_low, near_early, received))
        home0 = send(far0, 1, True)
    early = early + near_early
    near_early = meet(early, early_steps[3])
    kept, received = part_ways(add_low(kept, received), clip_steps[1])
    if split:
        far1, sums1 = finish(piece + lead, piece - lead, x_low, *rest)
        far1, sums1, x_low, near_early, received, home0 = tie((far1, sums1, x_low, near_early, received, home0))
        home1 = send(far1, 1, True)
    early = early + near_early
    near_early = meet(early, early_steps[4])
    kept, received = part_ways(add_low(kept, received), clip_steps[2])
    if split:
        input_grad, late = finish(0, piece, x_low, *rest, place=position % clip_count, places=clip_count)
        input_grad, late, near_early, received, slab, pooled = tie(
            (input_grad, late, near_early, received, slab, pooled)
        )
        other = (position + 1) % clip_count
        input_grad = lax.dynamic_update_slice(input_grad, home0.astype(f32)[None], (other, 0, 0))
        late = late + sums0 + sums1
    else:
        local, late = finish(0, rows, x_low, *rest)
        input_grad = gather_back([local[t * piece : (t + 1) * piece] for t in range(clip_count)], f32)
    early = early + near_early
    for step in early_steps[5:]:
        early = early + meet(early, step)
    slab1 = add_low(kept, received)
    for step in clip_steps[3:]:
        slab1 = add_low(*part_ways(slab1, step))
    late = late[:4]
    for first, *second in zip(clip_steps[::2], clip_steps[1::2]):
        low, high = first[1], second[0][1]
        near_sum = late + meet(late, ("clip", low))
        late = near_sum + (meet(late, ("clip", high)) + meet(late, ("clip", low + high)))
    if len(clip_steps) % 2:
        late = late + meet(late, clip_steps[-1])
    if split:
        home1, late, slab1, early = tie((home1, late, slab1, early))
    for step in seq_steps:
        late = late + meet(late, step)
    qkv = [
        part.reshape(share, count, 3, 128).transpose(0, 2, 1, 3) for part, count in zip((slab0, slab1), pairs)
    ]
    qkv = jnp.concatenate(qkv, axis=2).reshape(share, seq_size, -1).transpose(1, 0, 2)
    for step in seq_steps:
        qkv = add_low(*part_ways(qkv, step))
    qkv_grad = qkv[0].astype(f32)
    if split:
        input_grad = lax.dynamic_update_slice(input_grad, home1.astype(f32)[None], (other, lead, 0))
    fc1_grad = slab[:4].transpose(1, 0, 2).reshape(share, 4 * thin).astype(f32)
    fc2_grad = slab[4:8].reshape(4 * share, thin).astype(f32)
    out_grad = slab[8].astype(f32)

    pooled = jnp.stack(pooled)[(jnp.arange(clip_count) - position) % clip_count]
    small = early[6]
    map1_grad = early[16 : 16 + map_size].T
    map2_grad = early[16 + map_size :, : map_size // 16 * lanes].reshape(16, map_size // 16, lanes // NTOK, NTOK)
    map2_grad = jnp.sum(map2_grad, axis=2).transpose(1, 0, 2).reshape(map_size, NTOK)
    map2_bias_grad = jnp.sum(small[128:256].reshape(-1, NTOK), axis=0)
    penalty = jnp.sum(small[256:384]) / pair_count / slots_all
    return (
        pooled,
        penalty,
        input_grad,
        late[0],
        late[1],
        qkv_grad,
        late[2],
        late[3],
        out_grad,
        early[0],
        early[1],
        early[2],
        fc1_grad,
        early[8:12].reshape(-1),
        fc2_grad,
        early[3],
        early[4],
        early[5],
        map1_grad,
        small[:map_size],
        map2_grad,
        map2_bias_grad,
    )


def solution(mesh):
    row_spec = P("clip", "seq", None)
    pool_spec = P("clip", "seq", None, None)
    matrix_spec = P("clip", "seq")
    in_specs = (row_spec, P("clip"), P("clip")) + (P(),) * 19 + (pool_spec,)
    out_specs = (
        (pool_spec, P(), row_spec, P(), P(), matrix_spec, P(), P(), matrix_spec, P(), P(), P(), matrix_spec, P())
        + (matrix_spec,)
        + (P(),) * 7
    )
    return jax.shard_map(shards, mesh=mesh, in_specs=in_specs, out_specs=out_specs, check_vma=False)
```
